32 devices in a mesh: wide: 4 (over y, core), group: 8 (over z, x).
Axes of the slice: x: 2, y: 2, z: 4, core: 2. Of those that a mesh axis runs over, the one named last changes fastest.
Arguments:
- queries: bfloat16 [10240, 256], P(('wide', 'group')), may hold values from -32 to 32
- items: bfloat16 [10240, 256], P(('wide', 'group')), may hold values from -20 to 20
- item_owner: int32 [10240, 1], P(('wide', 'group')), may hold values from 0 to 7; in each aligned block of 320 rows (0 to 319, 320 to 639, ...) at most 80 rows name the same one
- item_offset: int32 [10240], P(('wide', 'group')), may hold values from 0 to 639
- sample_counts: int32 [10240], P(('wide', 'group')), may hold values from 1 to 4095
- table: float32 [20480, 256], P(('wide', 'group')), may hold values from -3 to 3
- accum: float32 [20480, 256], P(('wide', 'group')), may hold values from 0.001 to 0.1
Outputs:
- loss: float32 [10240], P(('wide', 'group'))
- query_grad: float32 [10240, 256], P(('wide', 'group'))
- table_new: float32 [20480, 256], P(('wide', 'group'))
- accum_new: float32 [20480, 256], P(('wide', 'group'))
The draws below stay inside these ranges and needn't reach their ends.
Inputs may be any that keep to these rules, and one draw needn't show every extreme that they name: `item_owner`: among the items of one device, at most 80 have the same owner.
All inputs are finite; a program needn't handle non-finite values.
Results may differ from the reference program's by a relative error of at most 0.005.
Values may be sent and summed in bfloat16 or wider, within the bound.
No kernel may reach another device: no remote copies, remote signals or barrier semaphores. Data moves between devices by JAX's collectives and lax.ppermute only.
A program may use at most 64 MiB of HBM per device.

```python
import math
import jax
import jax.numpy as jnp
import numpy as np
from jax import lax

D = 256
TOK_DEV = 320
ROWS_DEV = 640
CAP = 80
TOKENS = 10240
ROWS = 20480
N_WIDE = 4
N_GROUP = 8


def drawn_items(key, spread):
    blocks = TOKENS // TOK_DEV
    base = jnp.clip(jax.random.normal(key, (blocks, TOK_DEV, D), jnp.float32), -6.0, 6.0)
    second = base[:, 1]
    base = base.at[:, 1].set(second)
    factors = jnp.exp(spread * jax.random.uniform(jax.random.fold_in(key, 6), (blocks, TOK_DEV, 1), jnp.float32, -1.0, 1.0))
    factors = factors.at[:, 0:2].set(1.0)
    return jnp.clip(base * factors, -20.0, 20.0).reshape(TOKENS, D)


def draw_items(key, part):
    return drawn_items(key, 0.0).astype(jnp.bfloat16)


def draw_queries(key, part):
    key = jax.random.fold_in(key, 7)
    blocks = TOKENS // TOK_DEV
    values = jnp.clip(jax.random.normal(key, (blocks, TOK_DEV, D), jnp.float32), -6.0, 6.0)
    return jnp.clip(values, -32.0, 32.0).reshape(TOKENS, D).astype(jnp.bfloat16)


def set_ends(result, own_key, smallest, top_value):
    place = [jax.random.randint(jax.random.fold_in(own_key, axis), (), 0, length) for axis, length in enumerate(result.shape)]
    main_axis = result.shape.index(max(result.shape))
    beside = place[:main_axis] + [(place[main_axis] + 1) % result.shape[main_axis]] + place[main_axis + 1:]
    return result.at[tuple(place)].set(smallest).at[tuple(beside)].set(top_value)


def shard_levels(stream_key, shape, cuts, low, top_value):
    def one(position, parts):
        draws = jax.random.uniform(jax.random.fold_in(jax.random.fold_in(stream_key, 6), position), (parts,), jnp.float32, low / len(cuts), top_value / len(cuts))
        return jnp.repeat(jnp.exp(draws), shape[position] // parts).reshape((-1,) + (1,) * (len(shape) - position - 1))

    level = one(*cuts[0])
    for cut in cuts[1:]:
        level = level * one(*cut)
    return level


def shared_out(rng, own, number, rows, number_of, top, most, skew):
    ranking = jax.random.permutation(rng, number_of)
    heavy_load, common = portions_of(number_of, rows * top, most, skew, True), portions_of(number_of, rows * top, most, skew, False)
    places = jnp.arange(number_of)

    def named(sizes, rotation):
        used = int((sizes > 0).sum())
        fixed = max(1, used // 4)
        moved = fixed + (places - fixed + rotation * (used - fixed)) % max(1, number_of - fixed)
        return jnp.zeros((number_of,), jnp.int32).at[ranking[jnp.where(places < fixed, places, moved)]].set(jnp.asarray(sizes, jnp.int32))

    sizes = jnp.where(number % 4 == 0, named(heavy_load, number // 4), named(common, number - number // 4 - 1))
    mixed = jax.random.permutation(jax.random.fold_in(own, 3), number_of)
    donor, receiver = mixed[0:number_of // 2 * 2:2], mixed[1:number_of // 2 * 2:2]
    room = jnp.minimum(sizes[donor] - 1, most - sizes[receiver]) // 2
    room = jnp.where((donor == ranking[0]) | (receiver == ranking[0]) | (sizes[receiver] == 0), 0, jnp.maximum(room, 0))
    moved = jax.random.randint(jax.random.fold_in(own, 4), (number_of // 2,), 0, 1 << 20) % (room + 1)
    sizes = sizes.at[donor].add(-moved).at[receiver].add(moved)
    labels = jnp.searchsorted(jnp.cumsum(sizes), jnp.arange(rows * top), side="right").astype(jnp.int32)
    listing = labels.reshape(top, rows).T
    listing = listing[jax.random.permutation(jax.random.fold_in(own, 1), rows)]
    rotation = jax.random.randint(jax.random.fold_in(own, 2), (rows, 1), 0, top)
    return jnp.take_along_axis(listing, (jnp.arange(top)[None, :] + rotation) % top, axis=1)


def portions_of(number_of, total, bound, slope, full):
    loads = [(1 << 20) // math.isqrt(grade ** slope) + 1 for grade in range(1, number_of + 1)]
    largest = bound if full else min(bound, max(-(-total // number_of), total * loads[0] // sum(loads)))
    least = 1 if total - largest >= number_of - 1 else 0
    given, surplus = [largest] + [least] * (number_of - 1), total - largest - least * (number_of - 1)
    while surplus > 0:
        candidates = [i for i in range(1, number_of) if given[i] < largest] or [i for i in range(1, number_of) if given[i] < bound]
        whole, budget = sum([loads[i] for i in candidates]), surplus
        for i in candidates:
            addition = min(bound - given[i], max(1, budget * loads[i] // whole), surplus)
            given[i] = given[i] + addition
            surplus = surplus - addition
    return np.array(given)


def scatter_about(stream_key, extent, scale, bound, cuts=(), held_as=jnp.bfloat16):
    result = jax.random.normal(stream_key, extent, jnp.float32) * scale
    if len(cuts) > 0:
        result = shard_levels(stream_key, extent, cuts, -0.22, 0.18) * result
    return jnp.clip(result, min=-bound, max=bound).astype(held_as)


def setup_inputs(seed: int = 0) -> dict:
    seeds = jax.random.split(jax.random.key(seed), 8)
    queries = draw_queries(jax.random.fold_in(seeds[7], 71), 0)
    items = draw_items(jax.random.fold_in(seeds[7], 71), 0)
    item_owner_keys = jax.random.split(jax.random.fold_in(seeds[2], 1), TOKENS // TOK_DEV)
    item_owner_turns = jax.random.permutation(jax.random.fold_in(seeds[2], 3), TOKENS // TOK_DEV)
    item_owner = jax.vmap(lambda own, number: shared_out(jax.random.fold_in(seeds[2], 2), own, number, TOK_DEV, N_GROUP, 1, CAP, 2))(item_owner_keys, item_owner_turns).reshape((TOKENS, 1))
    item_offset = set_ends(jax.random.randint(seeds[3], (TOKENS,), 0, ROWS_DEV), jax.random.fold_in(seeds[3], 1), 0, ROWS_DEV - 1).astype(jnp.int32)
    sample_counts = set_ends(jax.random.randint(seeds[4], (TOKENS,), 1, 4096), jax.random.fold_in(seeds[4], 1), 1, 4095).astype(jnp.int32)
    table = scatter_about(seeds[5], (ROWS, D), 0.5, 3.0, ((0, 32),), jnp.float32)
    accum = jnp.clip(jnp.exp(math.log(0.1) - 4.6051702 * jax.random.uniform(seeds[6], (ROWS, D), jnp.float32) ** shard_levels(seeds[6], (ROWS, D), ((0, 32),), -0.2, 0.2)), 0.001, 0.1)
    return dict(queries=queries, items=items, item_owner=item_owner, item_offset=item_offset, sample_counts=sample_counts, table=table, accum=accum)


def by_group(array):
    rest = array.shape[1:]
    shaped = array.reshape((N_WIDE, N_GROUP, TOK_DEV) + rest)
    shaped = jnp.swapaxes(shaped, 0, 1)
    return shaped.reshape((N_GROUP, N_WIDE * TOK_DEV) + rest)

def from_group(array):
    rest = array.shape[2:]
    shaped = array.reshape((N_GROUP, N_WIDE, TOK_DEV) + rest)
    shaped = jnp.swapaxes(shaped, 0, 1)
    return shaped.reshape((TOKENS,) + rest)

def reference(queries, items, item_owner, item_offset, sample_counts, table, accum):
    scale = 3.0 / math.sqrt(D)
    width = N_WIDE * TOK_DEV

    def one_group(inputs):
        query_rows, item_rows, counts = inputs
        logits = jnp.dot(query_rows, item_rows.T, preferred_element_type=jnp.float32) * scale
        logits = logits - jnp.log(counts.astype(jnp.float32))[None, :]
        totals = jax.nn.logsumexp(logits, axis=1)
        index = jnp.arange(width, dtype=jnp.int32)
        hits = (index[:, None] == index[None, :]).astype(jnp.float32)
        chosen = lax.optimization_barrier(jnp.sum(logits * hits, axis=1))
        weights = (jnp.exp(logits - totals[:, None]) - hits).astype(jnp.bfloat16)
        query_part = jnp.dot(weights, item_rows, preferred_element_type=jnp.float32) * scale
        item_part = jnp.dot(weights.T, query_rows, preferred_element_type=jnp.float32) * scale
        return (totals - chosen, query_part, item_part)
    loss, query_grad, item_grad = lax.map(one_group, (by_group(queries), by_group(items), by_group(sample_counts)))
    loss = from_group(loss)
    query_grad = from_group(query_grad)
    item_grad = from_group(item_grad)
    token_index = jnp.arange(TOKENS, dtype=jnp.int32)
    rows = (token_index // (TOK_DEV * N_GROUP) * N_GROUP + item_owner[:, 0].astype(jnp.int32)) * ROWS_DEV + item_offset.astype(jnp.int32)
    grad = jnp.zeros(table.shape, jnp.float32).at[rows].add(item_grad)
    accum_new = accum + grad * grad
    table_new = table - 0.1 * grad / (jnp.sqrt(accum_new) + 1e-08)
    return (loss, query_grad, table_new, accum_new)
```

```python
import functools
import math

import jax
import jax.numpy as jnp
from jax import lax
from jax.experimental import pallas as pl
from jax.experimental.pallas import tpu as pltpu
from jax.sharding import PartitionSpec as P

D = 256
SCALE = 3.0 / math.sqrt(D)
LANES = 128
TAIL = 8
MIB = 1 << 20
NT = (((1,), (1,)), ((), ()))
TN = (((0,), (0,)), ((), ()))
F32 = jnp.float32
BF16 = jnp.bfloat16


def dot(a, b, dims=(((1,), (0,)), ((), ()))):
    return lax.dot_general(a, b, dims, preferred_element_type=F32)


def spread(column, width):
    pieces = [column] * (width // LANES)
    if width % LANES:
        pieces.append(column[:, : width % LANES])
    return jnp.concatenate(pieces, axis=1)


def code(x):
    y = x * x
    return jnp.where(x < 0, -y, y) * y


def decode(u):
    root = lax.rsqrt(lax.rsqrt(jnp.abs(u)))
    return jnp.where(u < 0, -root, root)


def route_kernel(groups, capacity, owner_ref, offset_ref, pick_ref, tail_ref):
    block = owner_ref.shape[1]
    owner = owner_ref[...]
    member = lax.broadcasted_iota(jnp.int32, (groups, block), 0) == owner
    before = lax.broadcasted_iota(jnp.int32, (block, block), 0) < lax.broadcasted_iota(
        jnp.int32, (block, block), 1
    )
    ranks = dot(member.astype(BF16), before.astype(BF16))
    rank = jnp.sum(jnp.where(member, ranks, 0.0), axis=0, keepdims=True).astype(jnp.int32)
    offset = offset_ref[...]
    high = jnp.broadcast_to((offset // LANES).astype(F32), (TAIL, block)).astype(BF16)
    low = jnp.broadcast_to((offset % LANES).astype(F32), (TAIL, block)).astype(BF16)
    slots = lax.broadcasted_iota(jnp.int32, (LANES, block), 0)
    here = slots == rank
    for g in range(groups):
        pick = (here & (owner == g)).astype(F32).astype(BF16)
        pick_ref[g] = pick[:capacity]
        tail_ref[g] = jnp.concatenate([dot(high, pick, NT), dot(low, pick, NT)], axis=1).astype(BF16)


def own_kernel(n, q_ref, *refs):
    item_refs, count_refs = refs[:n], refs[n : 2 * n]
    loss_ref, query_grad_ref, mine_ref, mate_ref, bias_ref, logits_ref = refs[2 * n :]
    block = q_ref.shape[0]
    q = q_ref[...]
    top = None
    for b in range(n):
        row = jnp.log(count_refs[b][...])
        bias = jnp.transpose(jnp.broadcast_to(row, (LANES, block)))
        bias_ref[b] = bias
        logits = dot(item_refs[b][...], q, NT) * SCALE - spread(bias, block)
        logits_ref[b] = logits
        high = jnp.max(logits, axis=0, keepdims=True)
        top = high if top is None else jnp.maximum(top, high)
    hit = lax.broadcasted_iota(jnp.int32, (block, block), 0) == lax.broadcasted_iota(
        jnp.int32, (block, block), 1
    )
    chosen = jnp.sum(jnp.where(hit, logits_ref[0], 0.0), axis=0, keepdims=True)
    total = jnp.zeros((1, block), F32)
    for b in range(n):
        e = jnp.exp(logits_ref[b] - top)
        logits_ref[b] = e
        total += jnp.sum(e, axis=0, keepdims=True)
    loss_ref[...] = top + jnp.log(total) - chosen
    inverse = 1.0 / total
    query_grad = jnp.zeros((block, D), F32)
    for b in range(n):
        weights = logits_ref[b] * inverse
        if b == 0:
            weights = jnp.where(hit, weights - 1.0, weights)
        weights = weights.astype(BF16)
        if b < 2:
            (mine_ref, mate_ref)[b][...] = dot(weights, q)
        query_grad += dot(weights, item_refs[b][...], TN)
    query_grad_ref[...] = query_grad * SCALE


def far_kernel(n, q_ref, *refs):
    item_refs = refs[:n]
    bias_ref, mine_ref, mate_ref, mine_out, mate_out, logits_ref = refs[n:]
    block = q_ref.shape[0]
    q = q_ref[...]
    top = None
    for b in range(n):
        logits = dot(item_refs[b][...], q, NT) * SCALE - spread(bias_ref[b], block)
        logits_ref[b] = logits
        high = jnp.max(logits, axis=0, keepdims=True)
        top = high if top is None else jnp.maximum(top, high)
    total = jnp.zeros((1, block), F32)
    for b in range(n):
        e = jnp.exp(logits_ref[b] - top)
        if b < 2:
            logits_ref[b] = e
        total += jnp.sum(e, axis=0, keepdims=True)
    inverse = 1.0 / total
    mate_out[...] = mate_ref[...] + dot((logits_ref[1] * inverse).astype(BF16), q)
    mine_out[...] = mine_ref[...] + dot((logits_ref[0] * inverse).astype(BF16), q)


def pack_kernel(groups, capacity, pick_ref, tail_ref, mine_ref, other_ref, out_ref):
    grad = code((mine_ref[...] + other_ref[...]) * SCALE).astype(BF16)
    for g in range(groups):
        out_ref[g, :capacity] = dot(pick_ref[g], grad).astype(BF16)
        out_ref[g, capacity:] = tail_ref[g]


def update_kernel(groups, capacity, got_ref, table_ref, accum_ref, table_out, accum_out):
    rows = table_ref.shape[0]
    first = pl.program_id(0) * rows
    index = lax.broadcasted_iota(jnp.int32, (rows, LANES), 0) + first
    index = index.astype(F32)
    grad = jnp.zeros((rows, D), F32)
    for g in range(groups):
        tail = got_ref[g, capacity : capacity + TAIL].astype(F32)[:1]
        ids = tail[:, :LANES] * LANES + tail[:, LANES:]
        put = (index == ids).astype(F32).astype(BF16)
        values = decode(got_ref[g, :capacity].astype(F32))
        high = values.astype(BF16)
        low = (values - high.astype(F32)).astype(BF16)
        both = jnp.concatenate([high, low], axis=1)
        empty = jnp.zeros((LANES - capacity, 2 * D), BF16)
        sums = dot(put, jnp.concatenate([both, empty], axis=0))
        grad += sums[:, :D] + sums[:, D:]
    accum_new = accum_ref[...] + grad * grad
    accum_out[...] = accum_new
    table_out[...] = table_ref[...] - 0.1 * grad / (jnp.sqrt(accum_new) + 1e-08)


def call(kernel, outs, *args, scratch=(), limit=16, flops=0):
    return pl.pallas_call(
        kernel,
        out_shape=[jax.ShapeDtypeStruct(s, t) for s, t in outs],
        scratch_shapes=list(scratch),
        compiler_params=pltpu.CompilerParams(vmem_limit_bytes=limit * MIB),
        cost_estimate=pl.CostEstimate(flops=flops, bytes_accessed=1 << 20, transcendentals=0),
    )(*args)


def shards(queries, items, item_owner, item_offset, sample_counts, table, accum):
    block = queries.shape[0]
    n, groups = lax.axis_size("wide"), lax.axis_size("group")
    capacity = 2 * block // groups
    slots = -(-capacity // TAIL) * TAIL

    def swap(x, k):
        return lax.ppermute(x, "wide", [(i, i ^ k) for i in range(n)])

    counts = sample_counts.astype(F32).reshape(1, block)
    far_items = [swap(items, k) for k in range(2, n, 2)]
    far_queries = [swap(queries, k) for k in range(2, n, 2)]
    mate_items = swap(items, 1)
    far_counts = [swap(counts, k) for k in range(1, n)]
    mate_far_items = [swap(x, 1) for x in far_items]
    item_blocks = [items, mate_items]
    count_blocks = [counts, far_counts[0]]
    for k in range(len(far_items)):
        item_blocks += [far_items[k], mate_far_items[k]]
        count_blocks += [far_counts[2 * k + 1], far_counts[2 * k + 2]]

    pick, tail = call(
        functools.partial(route_kernel, groups, slots),
        [((groups, slots, block), BF16), ((groups, TAIL, D), BF16)],
        item_owner.reshape(1, block),
        item_offset.reshape(1, block),
        flops=2 * groups * block * block,
    )
    part = ((block, D), F32)
    logits = pltpu.VMEM((n, block, block), F32)
    limit = 8 + 4 * n
    loss, query_grad, mine, mate, bias = call(
        functools.partial(own_kernel, n),
        [((1, block), F32), part, part, part, ((n, block, LANES), F32)],
        queries,
        *item_blocks,
        *count_blocks,
        scratch=[logits],
        limit=limit,
        flops=6 * n * block * block * D,
    )
    for far in far_queries:
        mine, mate = call(
            functools.partial(far_kernel, n),
            [part, part],
            far,
            *item_blocks,
            bias,
            mine,
            mate,
            scratch=[logits],
            limit=limit,
            flops=4 * n * block * block * D,
        )
    other = swap(mate, 1)
    (packed,) = call(
        functools.partial(pack_kernel, groups, slots),
        [((groups, slots + TAIL, D), BF16)],
        pick,
        tail,
        mine,
        other,
        flops=2 * groups * slots * block * D,
    )
    got = lax.all_to_all(packed, "group", split_axis=0, concat_axis=0, tiled=True)

    rows = table.shape[0]
    step = rows // 5
    spec = pl.BlockSpec((step, D), lambda i: (i, 0))
    table_new, accum_new = pl.pallas_call(
        functools.partial(update_kernel, groups, slots),
        out_shape=[jax.ShapeDtypeStruct(table.shape, F32)] * 2,
        grid=(rows // step,),
        in_specs=[pl.BlockSpec(got.shape, lambda i: (0, 0, 0)), spec, spec],
        out_specs=[spec, spec],
        compiler_params=pltpu.CompilerParams(vmem_limit_bytes=16 * MIB),
    )(got, table, accum)
    return (loss.reshape(block), query_grad, table_new, accum_new)


def solution(mesh):
    placed = (
        P(("wide", "group"), None),
        P(("wide", "group"), None),
        P(("wide", "group"), None),
        P(("wide", "group")),
        P(("wide", "group")),
        P(("wide", "group"), None),
        P(("wide", "group"), None),
    )
    return jax.shard_map(
        shards,
        mesh=mesh,
        in_specs=placed,
        out_specs=(
            P(("wide", "group")),
            P(("wide", "group"), None),
            P(("wide", "group"), None),
            P(("wide", "group"), None),
        ),
        check_vma=False,
    )
```

```python
import functools
import math

import jax
import jax.numpy as jnp
from jax import lax
from jax.experimental import pallas as pl
from jax.experimental.pallas import tpu as pltpu
from jax.sharding import PartitionSpec as P

D = 256
SCALE = 3.0 / math.sqrt(D)
LANES = 128
TAIL = 8
MIB = 1 << 20
NT = (((1,), (1,)), ((), ()))
TN = (((0,), (0,)), ((), ()))
F32 = jnp.float32
BF16 = jnp.bfloat16


def dot(a, b, dims=(((1,), (0,)), ((), ()))):
    return lax.dot_general(a, b, dims, preferred_element_type=F32)


def spread(column, width):
    pieces = [column] * (width // LANES)
    if width % LANES:
        pieces.append(column[:, : width % LANES])
    return jnp.concatenate(pieces, axis=1)


def code(x):
    y = x * x
    return jnp.where(x < 0, -y, y) * y


def decode(u):
    root = lax.rsqrt(lax.rsqrt(jnp.abs(u)))
    return jnp.where(u < 0, -root, root)


def diagonal(block):
    return lax.broadcasted_iota(jnp.int32, (block, block), 0) == lax.broadcasted_iota(
        jnp.int32, (block, block), 1
    )


def local_kernel(
    groups, slots, q_ref, item_ref, owner_ref, offset_ref, q_out, item_out, pick_ref, tail_ref
):
    q_out[...] = q_ref[...]
    item_out[...] = item_ref[...]
    block = owner_ref.shape[1]
    owner = owner_ref[...]
    member = lax.broadcasted_iota(jnp.int32, (groups, block), 0) == owner
    before = lax.broadcasted_iota(jnp.int32, (block, block), 0) < lax.broadcasted_iota(
        jnp.int32, (block, block), 1
    )
    ranks = dot(member.astype(BF16), before.astype(BF16))
    rank = jnp.sum(jnp.where(member, ranks, 0.0), axis=0, keepdims=True).astype(jnp.int32)
    offset = offset_ref[...]
    high = jnp.broadcast_to((offset // LANES).astype(F32), (TAIL, block)).astype(BF16)
    low = jnp.broadcast_to((offset % LANES).astype(F32), (TAIL, block)).astype(BF16)
    here = lax.broadcasted_iota(jnp.int32, (LANES, block), 0) == rank
    for g in range(groups):
        pick = (here & (owner == g)).astype(F32).astype(BF16)
        pick_ref[g * slots : (g + 1) * slots] = pick[:slots]
        tail_ref[g] = jnp.concatenate([dot(high, pick, NT), dot(low, pick, NT)], axis=1).astype(BF16)


def bias_kernel(n, *refs):
    for b in range(n):
        block = refs[b].shape[1]
        row = jnp.log(refs[b][...].astype(F32))
        refs[n][b] = jnp.transpose(jnp.broadcast_to(row, (LANES, block)))


def exponentials(n, q, item_refs, bias_ref, logits_ref):
    block = q.shape[0]
    top = None
    for b in range(n):
        logits = dot(item_refs[b][...], q, NT) * SCALE - spread(bias_ref[b], block)
        logits_ref[b] = logits
        high = jnp.max(logits, axis=0, keepdims=True)
        top = high if top is None else jnp.maximum(top, high)
    chosen = jnp.sum(jnp.where(diagonal(block), logits_ref[0], 0.0), axis=0, keepdims=True)
    total = jnp.zeros((1, block), F32)
    for b in range(n):
        e = jnp.exp(logits_ref[b] - top)
        logits_ref[b] = e
        total += jnp.sum(e, axis=0, keepdims=True)
    return top, total, chosen


def own_kernel(n, q_ref, *refs):
    item_refs = refs[:n]
    bias_ref, loss_ref, query_grad_ref, logits_ref = refs[n:]
    block = q_ref.shape[0]
    top, total, chosen = exponentials(n, q_ref[...], item_refs, bias_ref, logits_ref)
    loss_ref[...] = top + jnp.log(total) - chosen
    inverse = 1.0 / total
    query_grad = jnp.zeros((block, D), F32)
    for b in range(n):
        weights = logits_ref[b] * inverse
        if b == 0:
            weights = jnp.where(diagonal(block), weights - 1.0, weights)
        query_grad += dot(weights.astype(BF16), item_refs[b][...], TN)
    query_grad_ref[...] = query_grad * SCALE


def item_kernel(n, own, q_ref, *refs):
    item_refs = refs[:n]
    bias_ref, *before, mine_out, mate_out, logits_ref = refs[n:]
    block = q_ref.shape[0]
    q = q_ref[...]
    _, total, _ = exponentials(n, q, item_refs, bias_ref, logits_ref)
    inverse = 1.0 / total
    mate = dot((logits_ref[1] * inverse).astype(BF16), q)
    weights = logits_ref[0] * inverse
    if own:
        weights = jnp.where(diagonal(block), weights - 1.0, weights)
    mine = dot(weights.astype(BF16), q)
    if before:
        mine += before[0][...]
        mate += before[1][...]
    mine_out[...] = mine
    mate_out[...] = mate


def pack_kernel(groups, slots, pick_ref, tail_ref, mine_ref, other_ref, *out_refs):
    grad = code((mine_ref[...] + other_ref[...]) * SCALE).astype(BF16)
    picked = dot(pick_ref[...], grad).astype(BF16)
    for g in range(groups):
        out = out_refs[g] if len(out_refs) == groups else out_refs[0].at[g]
        out[:slots] = picked[g * slots : (g + 1) * slots]
        out[slots:] = tail_ref[g]


def update_kernel(groups, slots, *refs):
    got_refs = refs[:-6]
    table_ref, accum_ref, table_out, accum_out, values_ref, ids_ref = refs[-6:]
    rows = table_ref.shape[0]
    half = groups * LANES

    @pl.when(pl.program_id(0) == 0)
    def _():
        for g in range(groups):
            got = got_refs[g] if len(got_refs) == groups else got_refs[0].at[g]
            tail = got[slots : slots + TAIL].astype(F32)
            ids_ref[:, g * LANES : (g + 1) * LANES] = tail[:, :LANES] * LANES + tail[:, LANES:]
            values = decode(got[:slots].astype(F32))
            high = values.astype(BF16)
            low = (values - high.astype(F32)).astype(BF16)
            empty = jnp.zeros((LANES - slots, D), BF16)
            start = g * LANES
            values_ref[start : start + LANES] = jnp.concatenate([high, empty], axis=0)
            start += half
            values_ref[start : start + LANES] = jnp.concatenate([low, empty], axis=0)

    index = lax.broadcasted_iota(jnp.int32, (rows, half), 0) + pl.program_id(0) * rows
    put = (index.astype(F32) == ids_ref[:1]).astype(F32).astype(BF16)
    grad = dot(jnp.concatenate([put, put], axis=1), values_ref[...])
    accum_new = accum_ref[...] + grad * grad
    accum_out[...] = accum_new
    table_out[...] = table_ref[...] - 0.1 * grad / (jnp.sqrt(accum_new) + 1e-08)


def call(kernel, outs, *args, scratch=(), limit=16, flops=0):
    return pl.pallas_call(
        kernel,
        out_shape=[jax.ShapeDtypeStruct(s, t) for s, t in outs],
        scratch_shapes=list(scratch),
        compiler_params=pltpu.CompilerParams(vmem_limit_bytes=limit * MIB),
        cost_estimate=pl.CostEstimate(flops=flops, bytes_accessed=1024, transcendentals=0),
    )(*args)


def shards(queries, items, item_owner, item_offset, sample_counts, table, accum):
    block = queries.shape[0]
    n, groups = lax.axis_size("wide"), lax.axis_size("group")
    capacity = 2 * block // groups
    slots = -(-capacity // TAIL) * TAIL
    paired = groups <= 8

    def swap(x, k, axis="wide"):
        return lax.ppermute(x, axis, [(i, i ^ k) for i in range(lax.axis_size(axis))])

    far_counts = [swap(sample_counts, k) for k in range(2, n, 2)]
    far_items = [swap(items, k) for k in range(2, n, 2)]
    mate_counts = swap(sample_counts, 1)
    far_queries = [swap(queries, k) for k in range(2, n, 2)]
    mate_items = swap(items, 1)

    owner = item_owner.reshape(1, block)
    if paired:
        owner = owner ^ lax.axis_index("group")
    own_q, own_items, pick, tail = call(
        functools.partial(local_kernel, groups, slots),
        [
            ((block, D), BF16),
            ((block, D), BF16),
            ((groups * slots, block), BF16),
            ((groups, TAIL, D), BF16),
        ],
        queries,
        items,
        owner,
        item_offset.reshape(1, block),
        flops=1 << 30,
    )
    far_items, far_counts, own_items = lax.optimization_barrier((far_items, far_counts, own_items))
    item_blocks, count_blocks = [own_items, mate_items], [sample_counts, mate_counts]
    for far_item, far_count in zip(far_items, far_counts):
        item_blocks += [far_item, swap(far_item, 1)]
        count_blocks += [far_count, swap(far_count, 1)]
    (bias,) = call(
        functools.partial(bias_kernel, n),
        [((n, block, LANES), F32)],
        *[x.reshape(1, block) for x in count_blocks],
    )

    part = ((block, D), F32)
    logits = pltpu.VMEM((n, block, block), F32)
    limit = 8 + 4 * n
    mine, mate = call(
        functools.partial(item_kernel, n, True),
        [part, part],
        own_q,
        *item_blocks,
        bias,
        scratch=[logits],
        limit=limit,
    )
    for far in far_queries:
        mine, mate = call(
            functools.partial(item_kernel, n, False),
            [part, part],
            far,
            *item_blocks,
            bias,
            mine,
            mate,
            scratch=[logits],
            limit=limit,
        )
    other = swap(mate, 1)
    if paired:
        packets = [((slots + TAIL, D), BF16)] * groups
    else:
        packets = [((groups, slots + TAIL, D), BF16)]
    packed = call(
        functools.partial(pack_kernel, groups, slots), packets, pick, tail, mine, other
    )
    if paired:
        order = sorted(range(1, groups), key=lambda k: (k < groups // 2, k % 2, k))
        got = [packed[0]] + [swap(packed[k], k, "group") for k in order]
    else:
        got = [lax.all_to_all(packed[0], "group", split_axis=0, concat_axis=0, tiled=True)]
    loss, query_grad = call(
        functools.partial(own_kernel, n),
        [((1, block), F32), part],
        own_q,
        *item_blocks,
        bias,
        scratch=[logits],
        limit=limit,
        flops=6 * n * block * block * D,
    )

    rows = table.shape[0]
    step = rows // 5
    spec = pl.BlockSpec((step, D), lambda i: (i, 0))
    table_new, accum_new = pl.pallas_call(
        functools.partial(update_kernel, groups, slots),
        out_shape=[jax.ShapeDtypeStruct(table.shape, F32)] * 2,
        grid=(rows // step,),
        in_specs=[pl.BlockSpec(memory_space=pltpu.VMEM)] * len(got) + [spec, spec],
        out_specs=[spec, spec],
        scratch_shapes=[
            pltpu.VMEM((2 * groups * LANES, D), BF16),
            pltpu.VMEM((TAIL, groups * LANES), F32),
        ],
        compiler_params=pltpu.CompilerParams(vmem_limit_bytes=32 * MIB),
    )(*got, table, accum)
    return (loss.reshape(block), query_grad, table_new, accum_new)


def solution(mesh):
    placed = (
        P(("wide", "group"), None),
        P(("wide", "group"), None),
        P(("wide", "group"), None),
        P(("wide", "group")),
        P(("wide", "group")),
        P(("wide", "group"), None),
        P(("wide", "group"), None),
    )
    return jax.shard_map(
        shards,
        mesh=mesh,
        in_specs=placed,
        out_specs=(
            P(("wide", "group")),
            P(("wide", "group"), None),
            P(("wide", "group"), None),
            P(("wide", "group"), None),
        ),
        check_vma=False,
    )
```

```python
import functools
import math

import jax
import jax.numpy as jnp
from jax import lax
from jax.experimental import pallas as pl
from jax.experimental.pallas import tpu as pltpu
from jax.sharding import PartitionSpec as P

D = 256
SCALE = 3.0 / math.sqrt(D)
LANES = 128
TAIL = 8
ROW_CODES = 1 << 16
MIB = 1 << 20
NT = (((1,), (1,)), ((), ()))
TN = (((0,), (0,)), ((), ()))
F32 = jnp.float32
BF16 = jnp.bfloat16


def dot(a, b, dims=(((1,), (0,)), ((), ()))):
    return lax.dot_general(a, b, dims, preferred_element_type=F32)


def spread(column, width):
    pieces = [column] * (width // LANES)
    if width % LANES:
        pieces.append(column[:, : width % LANES])
    return jnp.concatenate(pieces, axis=1)


def code(x):
    y = x * x
    return jnp.where(x < 0, -y, y) * y


def decode(u):
    root = lax.rsqrt(lax.rsqrt(jnp.abs(u)))
    return jnp.where(u < 0, -root, root)


def diagonal(block):
    return lax.broadcasted_iota(jnp.int32, (block, block), 0) == lax.broadcasted_iota(
        jnp.int32, (block, block), 1
    )


def local_kernel(groups, slots, code_ref, pick_ref, tail_ref):
    block = code_ref.shape[1]
    owner = code_ref[...] // ROW_CODES
    offset = code_ref[...] % ROW_CODES
    member = lax.broadcasted_iota(jnp.int32, (groups, block), 0) == owner
    before = lax.broadcasted_iota(jnp.int32, (block, block), 0) < lax.broadcasted_iota(
        jnp.int32, (block, block), 1
    )
    ranks = dot(member.astype(BF16), before.astype(BF16))
    rank = jnp.sum(jnp.where(member, ranks, 0.0), axis=0, keepdims=True).astype(jnp.int32)
    high = jnp.broadcast_to((offset // LANES).astype(F32), (TAIL, block)).astype(BF16)
    low = jnp.broadcast_to((offset % LANES).astype(F32), (TAIL, block)).astype(BF16)
    here = lax.broadcasted_iota(jnp.int32, (LANES, block), 0) == rank
    for g in range(groups):
        pick = (here & (owner == g)).astype(F32).astype(BF16)
        pick_ref[g * slots : (g + 1) * slots] = pick[:slots]
        tail_ref[g] = jnp.concatenate([dot(high, pick, NT), dot(low, pick, NT)], axis=1).astype(BF16)


def bias_kernel(n, *refs):
    for b in range(n):
        block = refs[b].shape[1]
        row = jnp.log(refs[b][...].astype(F32))
        refs[n][b] = jnp.transpose(jnp.broadcast_to(row, (LANES, block)))


def item_kernel(n, m, own, *refs):
    q_refs, item_refs, bias_ref, refs = refs[:m], refs[m : m + n], refs[m + n], refs[m + n + 1 :]
    block = q_refs[0].shape[0]
    q = jnp.concatenate([ref[...] for ref in q_refs], axis=0)
    if own:
        mine_out, mate_out, loss_ref, weights_ref, logits_ref = refs
    else:
        mine_ref, mate_ref, mine_out, mate_out, logits_ref = refs
    top = None
    for b in range(n):
        logits = dot(item_refs[b][...], q, NT) * SCALE - spread(bias_ref[b], m * block)
        logits_ref[b] = logits
        high = jnp.max(logits, axis=0, keepdims=True)
        top = high if top is None else jnp.maximum(top, high)
    hit = lax.broadcasted_iota(jnp.int32, (block, m * block), 0) == lax.broadcasted_iota(
        jnp.int32, (block, m * block), 1
    )
    if own:
        chosen = jnp.sum(jnp.where(hit, logits_ref[0], 0.0), axis=0, keepdims=True)
    total = jnp.zeros((1, m * block), F32)
    for b in range(n):
        e = jnp.exp(logits_ref[b] - top)
        logits_ref[b] = e
        total += jnp.sum(e, axis=0, keepdims=True)
    inverse = 1.0 / total
    for b in range(n):
        if b > 1 and not own:
            continue
        weights = logits_ref[b] * inverse
        if b == 0 and own:
            weights = jnp.where(hit, weights - 1.0, weights)
        weights = weights.astype(BF16)
        if own:
            weights_ref[b] = weights[:, :block]
        if b < 2:
            part = dot(weights, q)
            if not own:
                part += (mine_ref, mate_ref)[b][...]
            (mine_out, mate_out)[b][...] = part
    if own:
        loss_ref[...] = (top + jnp.log(total) - chosen)[0, :block]


def query_kernel(n, weights_ref, *refs):
    item_refs, out_ref = refs[:n], refs[n]
    total = dot(weights_ref[0], item_refs[0][...], TN)
    for b in range(1, n):
        total += dot(weights_ref[b], item_refs[b][...], TN)
    out_ref[...] = total * SCALE


def pack_kernel(groups, slots, pick_ref, tail_ref, mine_ref, other_ref, *out_refs):
    grad = code((mine_ref[...] + other_ref[...]) * SCALE).astype(BF16)
    picked = dot(pick_ref[...], grad).astype(BF16)
    for g in range(groups):
        out = out_refs[g] if len(out_refs) == groups else out_refs[0].at[g]
        out[:slots] = picked[g * slots : (g + 1) * slots]
        out[slots:] = tail_ref[g]


def update_kernel(groups, slots, *refs):
    got_refs = refs[:-6]
    table_ref, accum_ref, table_out, accum_out, values_ref, ids_ref = refs[-6:]
    rows = table_ref.shape[0]
    half = groups * slots

    @pl.when(pl.program_id(0) == 0)
    def _():
        for g in range(groups):
            got = got_refs[g] if len(got_refs) == groups else got_refs[0].at[g]
            here = slice(g * slots, (g + 1) * slots)
            tail = got[slots : slots + TAIL].astype(F32)
            ids_ref[:, here] = tail[:, :slots] * LANES + tail[:, LANES : LANES + slots]
            values = decode(got[:slots].astype(F32))
            high = values.astype(BF16)
            values_ref[g * slots : (g + 1) * slots] = high
            low = (values - high.astype(F32)).astype(BF16)
            values_ref[half + g * slots : half + (g + 1) * slots] = low

    index = lax.broadcasted_iota(jnp.int32, (rows, half), 0) + pl.program_id(0) * rows
    put = (index.astype(F32) == ids_ref[:1]).astype(F32).astype(BF16)
    grad = dot(jnp.concatenate([put, put], axis=1), values_ref[...])
    accum_new = accum_ref[...] + grad * grad
    accum_out[...] = accum_new
    table_out[...] = table_ref[...] - 0.1 * grad / (jnp.sqrt(accum_new) + 1e-08)


def call(kernel, outs, *args, scratch=(), limit=16, flops=0):
    return pl.pallas_call(
        kernel,
        out_shape=[jax.ShapeDtypeStruct(s, t) for s, t in outs],
        scratch_shapes=list(scratch),
        compiler_params=pltpu.CompilerParams(vmem_limit_bytes=limit * MIB),
        cost_estimate=pl.CostEstimate(flops=flops, bytes_accessed=1024, transcendentals=0),
    )(*args)


def shards(queries, items, item_owner, item_offset, sample_counts, table, accum):
    block = queries.shape[0]
    n, groups = lax.axis_size("wide"), lax.axis_size("group")
    capacity = 2 * block // groups
    slots = -(-capacity // TAIL) * TAIL
    paired = groups <= 8

    def swap(x, k, axis="wide"):
        return lax.ppermute(x, axis, [(i, i ^ k) for i in range(lax.axis_size(axis))])

    far_counts = [swap(sample_counts, k) for k in range(2, n, 2)]
    far_items = [swap(items, k) for k in range(2, n, 2)]
    far_queries = [swap(queries, k) for k in range(2, n, 2)]

    owner = item_owner.reshape(1, block)
    if paired:
        owner = owner ^ lax.axis_index("group")
    pick, tail = call(
        functools.partial(local_kernel, groups, slots),
        [((groups * slots, block), BF16), ((groups, TAIL, D), BF16)],
        owner * ROW_CODES + item_offset.reshape(1, block),
        flops=1 << 30,
    )
    far_items, far_counts, tail = lax.optimization_barrier((far_items, far_counts, tail))
    item_blocks = [items, swap(items, 1)]
    count_blocks = [sample_counts, swap(sample_counts, 1)]
    for far_item, far_count in zip(far_items, far_counts):
        item_blocks += [far_item, swap(far_item, 1)]
        count_blocks += [far_count, swap(far_count, 1)]
    (bias,) = call(
        functools.partial(bias_kernel, n),
        [((n, block, LANES), F32)],
        *[x.reshape(1, block) for x in count_blocks],
    )

    part = ((block, D), F32)
    mine, mate, loss, weights = call(
        functools.partial(item_kernel, n, 2, True),
        [part, part, ((block,), F32), ((n, block, block), BF16)],
        queries,
        far_queries[0],
        *item_blocks,
        bias,
        scratch=[pltpu.VMEM((n, block, 2 * block), F32)],
        limit=8 + 4 * n,
    )
    for k in range(1, len(far_queries), 2):
        pair = far_queries[k : k + 2]
        mine, mate = call(
            functools.partial(item_kernel, n, len(pair), False),
            [part, part],
            *pair,
            *item_blocks,
            bias,
            mine,
            mate,
            scratch=[pltpu.VMEM((n, block, len(pair) * block), F32)],
            limit=8 + 4 * n,
        )
    other = swap(mate, 1)
    (query_grad,) = call(
        functools.partial(query_kernel, n), [part], weights, *item_blocks, flops=1 << 30
    )
    other, query_grad = lax.optimization_barrier((other, query_grad))
    if paired:
        packets = [((slots + TAIL, D), BF16)] * groups
    else:
        packets = [((groups, slots + TAIL, D), BF16)]
    packed = call(
        functools.partial(pack_kernel, groups, slots), packets, pick, tail, mine, other
    )
    if paired:
        order = sorted(range(1, groups), key=lambda k: (k < groups // 2, k % 2, k))
        got = [packed[0]] + [swap(packed[k], k, "group") for k in order]
    else:
        got = [lax.all_to_all(packed[0], "group", split_axis=0, concat_axis=0, tiled=True)]
    rows = table.shape[0]
    step = rows // 2
    spec = pl.BlockSpec((step, D), lambda i: (i, 0))
    table_new, accum_new = pl.pallas_call(
        functools.partial(update_kernel, groups, slots),
        out_shape=[jax.ShapeDtypeStruct(table.shape, F32)] * 2,
        grid=(rows // step,),
        in_specs=[pl.BlockSpec(memory_space=pltpu.VMEM)] * len(got) + [spec, spec],
        out_specs=[spec, spec],
        scratch_shapes=[
            pltpu.VMEM((2 * groups * slots, D), BF16),
            pltpu.VMEM((TAIL, groups * slots), F32),
        ],
        compiler_params=pltpu.CompilerParams(vmem_limit_bytes=32 * MIB),
    )(*got, table, accum)
    return (loss, query_grad, table_new, accum_new)


def solution(mesh):
    placed = (
        P(("wide", "group"), None),
        P(("wide", "group"), None),
        P(("wide", "group"), None),
        P(("wide", "group")),
        P(("wide", "group")),
        P(("wide", "group"), None),
        P(("wide", "group"), None),
    )
    return jax.shard_map(
        shards,
        mesh=mesh,
        in_specs=placed,
        out_specs=(
            P(("wide", "group")),
            P(("wide", "group"), None),
            P(("wide", "group"), None),
            P(("wide", "group"), None),
        ),
        check_vma=False,
    )
```

```python
import functools
import math

import jax
import jax.numpy as jnp
from jax import lax
from jax.experimental import pallas as pl
from jax.experimental.pallas import tpu as pltpu
from jax.sharding import PartitionSpec as P

D = 256
SCALE = 3.0 / math.sqrt(D)
LOG2E = math.log2(math.e)
LANES = 128
TAIL = 8
ROW_CODES = 1 << 16
MIB = 1 << 20
NT = (((1,), (1,)), ((), ()))
TN = (((0,), (0,)), ((), ()))
F32 = jnp.float32
BF16 = jnp.bfloat16


def dot(a, b, dims=(((1,), (0,)), ((), ()))):
    return lax.dot_general(a, b, dims, preferred_element_type=F32)


def spread(column, width):
    pieces = [column] * (width // LANES)
    if width % LANES:
        pieces.append(column[:, : width % LANES])
    return jnp.concatenate(pieces, axis=1)


def code(x):
    y = x * x
    return jnp.where(x < 0, -y, y) * y


def decode(u):
    root = lax.rsqrt(lax.rsqrt(jnp.abs(u)))
    return jnp.where(u < 0, -root, root)


def diagonal(block):
    return lax.broadcasted_iota(jnp.int32, (block, block), 0) == lax.broadcasted_iota(
        jnp.int32, (block, block), 1
    )


def local_kernel(groups, slots, code_ref, pick_ref, tail_ref):
    block = code_ref.shape[1]
    owner = code_ref[...] // ROW_CODES
    offset = code_ref[...] % ROW_CODES
    member = lax.broadcasted_iota(jnp.int32, (groups, block), 0) == owner
    before = lax.broadcasted_iota(jnp.int32, (block, block), 0) < lax.broadcasted_iota(
        jnp.int32, (block, block), 1
    )
    ranks = dot(member.astype(BF16), before.astype(BF16))
    rank = jnp.sum(jnp.where(member, ranks, 0.0), axis=0, keepdims=True).astype(jnp.int32)
    high = jnp.broadcast_to((offset // LANES).astype(F32), (TAIL, block)).astype(BF16)
    low = jnp.broadcast_to((offset % LANES).astype(F32), (TAIL, block)).astype(BF16)
    here = lax.broadcasted_iota(jnp.int32, (LANES, block), 0) == rank
    for g in range(groups):
        pick = (here & (owner == g)).astype(F32).astype(BF16)
        pick_ref[g * slots : (g + 1) * slots] = pick[:slots]
        tail_ref[g] = jnp.concatenate([dot(high, pick, NT), dot(low, pick, NT)], axis=1).astype(BF16)


def bias_kernel(n, *refs):
    for b in range(n):
        block = refs[b].shape[1]
        row = jnp.log(refs[b][...].astype(F32)) * LOG2E
        refs[n][b] = jnp.transpose(jnp.broadcast_to(row, (LANES, block)))


def fill_logits(q, item_refs, bias_ref, first, out_ref):
    top = None
    for b, item_ref in enumerate(item_refs):
        logits = dot(item_ref[...], q, NT) * (SCALE * LOG2E)
        logits -= spread(bias_ref[first + b], q.shape[0])
        out_ref[b] = logits
        high = jnp.max(logits, axis=0, keepdims=True)
        top = high if top is None else jnp.maximum(top, high)
    return top


def to_powers(ref, top):
    total = jnp.zeros(top.shape, F32)
    for b in range(ref.shape[0]):
        e = jnp.exp2(ref[b] - top)
        ref[b] = e
        total += jnp.sum(e, axis=0, keepdims=True)
    return total


def diagonal(block):
    return lax.broadcasted_iota(jnp.int32, (block, block), 0) == lax.broadcasted_iota(
        jnp.int32, (block, block), 1
    )


def early_kernel(n, q_ref, *refs):
    item_refs, (bias_ref, e_ref, stats_ref) = refs[:n], refs[n:]
    block = q_ref.shape[0]
    top = fill_logits(q_ref[...], item_refs, bias_ref, 0, e_ref)
    chosen = jnp.sum(jnp.where(diagonal(block), e_ref[0], 0.0), axis=0, keepdims=True)
    stats_ref[0:1] = top
    stats_ref[1:2] = to_powers(e_ref, top)
    stats_ref[2:3] = chosen


def main_kernel(early, late, *refs):
    n = early + late
    q_ref, far_ref, item_refs, refs = refs[0], refs[1], refs[2 : 2 + n], refs[2 + n :]
    bias_ref, e_ref, stats_ref, mine_out, mate_out, loss_ref, late_ref, factor_ref, far_e_ref = refs
    block = q_ref.shape[0]
    q, far = q_ref[...], far_ref[...]
    far_top = fill_logits(far, item_refs, bias_ref, 0, far_e_ref)
    early_top, early_total, chosen = stats_ref[0:1], stats_ref[1:2], stats_ref[2:3]
    top = fill_logits(q, item_refs[early:], bias_ref, early, late_ref)
    top = jnp.maximum(top, early_top)
    far_inverse = 1.0 / to_powers(far_e_ref, far_top)
    shrink = jnp.exp2(early_top - top)
    total = to_powers(late_ref, top) + early_total * shrink
    inverse = 1.0 / total
    factor = shrink * inverse
    mate = dot((e_ref[1] * factor).astype(BF16), q)
    mate_out[...] = mate + dot((far_e_ref[1] * far_inverse).astype(BF16), far)
    weights = e_ref[0] * factor
    weights = jnp.where(diagonal(block), weights - 1.0, weights)
    mine = dot(weights.astype(BF16), q)
    mine_out[...] = mine + dot((far_e_ref[0] * far_inverse).astype(BF16), far)
    loss_ref[...] = ((top + jnp.log2(total) - chosen) * (1.0 / LOG2E))[0]
    factor_ref[0:1] = factor
    factor_ref[1:2] = inverse


def more_kernel(n, q_ref, *refs):
    item_refs, refs = refs[:n], refs[n:]
    bias_ref, mine_ref, mate_ref, mine_out, mate_out, e_ref = refs
    q = q_ref[...]
    inverse = 1.0 / to_powers(e_ref, fill_logits(q, item_refs, bias_ref, 0, e_ref))
    mate_out[...] = mate_ref[...] + dot((e_ref[1] * inverse).astype(BF16), q)
    mine_out[...] = mine_ref[...] + dot((e_ref[0] * inverse).astype(BF16), q)


def query_kernel(early, late, e_ref, late_ref, factor_ref, *refs):
    item_refs, out_ref = refs[:-1], refs[-1]
    total = None
    for b, item_ref in enumerate(item_refs):
        if b < early:
            weights = e_ref[b] * factor_ref[0:1]
        else:
            weights = late_ref[b - early] * factor_ref[1:2]
        if b == 0:
            weights = jnp.where(diagonal(weights.shape[0]), weights - 1.0, weights)
        part = dot(weights.astype(BF16), item_ref[...], TN)
        total = part if total is None else total + part
    out_ref[...] = total * SCALE


def pack_kernel(groups, slots, pick_ref, tail_ref, mine_ref, other_ref, *out_refs):
    grad = code((mine_ref[...] + other_ref[...]) * SCALE).astype(BF16)
    picked = dot(pick_ref[...], grad).astype(BF16)
    for g in range(groups):
        out = out_refs[g] if len(out_refs) == groups else out_refs[0].at[g]
        out[:slots] = picked[g * slots : (g + 1) * slots]
        out[slots:] = tail_ref[g]


def scatter(slots, got_refs, values_ref, ids_ref, rows):
    packets = got_refs
    if len(got_refs[0].shape) == 3:
        packets = [got_refs[0].at[g] for g in range(got_refs[0].shape[0])]
    half = len(packets) * slots
    for g, got in enumerate(packets):
        tail = got[slots : slots + TAIL].astype(F32)
        ids = tail[:, :slots] * LANES + tail[:, LANES : LANES + slots]
        ids_ref[:, g * slots : (g + 1) * slots] = ids
        values = decode(got[:slots].astype(F32))
        high = values.astype(BF16)
        values_ref[g * slots : (g + 1) * slots] = high
        low = (values - high.astype(F32)).astype(BF16)
        values_ref[half + g * slots : half + (g + 1) * slots] = low
    index = lax.broadcasted_iota(jnp.int32, (rows, half), 0).astype(F32)
    put = (index == ids_ref[:1]).astype(F32).astype(BF16)
    return dot(jnp.concatenate([put, put], axis=1), values_ref[...])


def first_kernel(slots, *refs):
    got_refs, (out_ref, values_ref, ids_ref) = refs[:-3], refs[-3:]
    out_ref[...] = scatter(slots, got_refs, values_ref, ids_ref, out_ref.shape[0])


def update_kernel(slots, partial, *refs):
    inputs, refs = refs[:-8], refs[-8:]
    table_ref, accum_ref, table_out, accum_out, values_ref, ids_ref, new_ref, sems = refs
    got_refs = inputs[1:] if partial else inputs
    rows = table_ref.shape[0]
    grad = scatter(slots, got_refs, values_ref, ids_ref, rows)
    if partial:
        grad += inputs[0][...]
    accum_new = accum_ref[...] + grad * grad
    new_ref[1] = accum_new
    first = pltpu.make_async_copy(new_ref.at[1], accum_out, sems.at[1])
    first.start()
    new_ref[0] = table_ref[...] - 0.1 * grad / (jnp.sqrt(accum_new) + 1e-08)
    second = pltpu.make_async_copy(new_ref.at[0], table_out, sems.at[0])
    second.start()
    first.wait()
    second.wait()


def call(kernel, outs, *args, scratch=(), limit=16, flops=0):
    return pl.pallas_call(
        kernel,
        out_shape=[jax.ShapeDtypeStruct(s, t) for s, t in outs],
        scratch_shapes=list(scratch),
        compiler_params=pltpu.CompilerParams(vmem_limit_bytes=limit * MIB),
        cost_estimate=pl.CostEstimate(flops=flops, bytes_accessed=1024, transcendentals=0),
    )(*args)


def shards(queries, items, item_owner, item_offset, sample_counts, table, accum):
    block = queries.shape[0]
    n, groups = lax.axis_size("wide"), lax.axis_size("group")
    capacity = 2 * block // groups
    slots = -(-capacity // TAIL) * TAIL
    paired = groups <= 8

    def swap(x, k, axis="wide"):
        return lax.ppermute(x, axis, [(i, i ^ k) for i in range(lax.axis_size(axis))])

    far_items = [swap(items, k) for k in range(2, n, 2)]
    far_queries = [swap(queries, k) for k in range(2, n, 2)]

    owner = item_owner.reshape(1, block)
    if paired:
        owner = owner ^ lax.axis_index("group")
    pick, tail = call(
        functools.partial(local_kernel, groups, slots),
        [((groups * slots, block), BF16), ((groups, TAIL, D), BF16)],
        owner * ROW_CODES + item_offset.reshape(1, block),
        flops=1 << 30,
    )
    own_counts, tail = lax.optimization_barrier((sample_counts, tail))
    counts = [swap(own_counts, k) for k in range(1, n)]
    far_items, counts, tail = lax.optimization_barrier((far_items, counts, tail))
    item_blocks = [items, swap(items, 1)] + far_items
    early = len(item_blocks)
    item_blocks += [swap(x, 1) for x in far_items]
    late = n - early
    count_blocks = [sample_counts, counts[0]] + counts[1::2] + counts[2::2]
    (bias,) = call(
        functools.partial(bias_kernel, n),
        [((n, block, LANES), F32)],
        *[x.reshape(1, block) for x in count_blocks],
    )

    part = ((block, D), F32)
    square = (block, block)
    powers, stats = call(
        functools.partial(early_kernel, early),
        [((early, *square), F32), ((8, block), F32)],
        queries,
        *item_blocks[:early],
        bias,
        limit=8 + 2 * n,
    )
    mine, mate, loss, late_powers, factors = call(
        functools.partial(main_kernel, early, late),
        [part, part, ((block,), F32), ((late, *square), F32), ((8, block), F32)],
        queries,
        far_queries[0],
        *item_blocks,
        bias,
        powers,
        stats,
        scratch=[pltpu.VMEM((n, *square), F32)],
        limit=8 + 4 * n,
    )
    for far in far_queries[1:]:
        mine, mate = call(
            functools.partial(more_kernel, n),
            [part, part],
            far,
            *item_blocks,
            bias,
            mine,
            mate,
            scratch=[pltpu.VMEM((n, *square), F32)],
            limit=8 + 4 * n,
        )
    other = swap(mate, 1)
    (query_grad,) = call(
        functools.partial(query_kernel, early, late),
        [part],
        powers,
        late_powers,
        factors,
        *item_blocks,
        limit=8 + 2 * n,
        flops=1 << 30,
    )
    other, query_grad = lax.optimization_barrier((other, query_grad))
    if paired:
        packets = [((slots + TAIL, D), BF16)] * groups
    else:
        packets = [((groups, slots + TAIL, D), BF16)]
    packed = call(
        functools.partial(pack_kernel, groups, slots), packets, pick, tail, mine, other
    )
    if paired:
        order = sorted(range(1, groups), key=lambda k: (k < groups // 2, k % 2, k))
        got = [packed[0]] + [swap(packed[k], k, "group") for k in order]
    else:
        got = [lax.all_to_all(packed[0], "group", split_axis=0, concat_axis=0, tiled=True)]
    rows = table.shape[0]

    def scratch(packets):
        return [
            pltpu.VMEM((2 * packets * slots, D), BF16),
            pltpu.VMEM((TAIL, packets * slots), F32),
        ]

    half = groups // 2
    before = []
    if paired:
        before = call(
            functools.partial(first_kernel, slots),
            [((rows, D), F32)],
            *got[:half],
            scratch=scratch(half),
            flops=1 << 28,
        )
        got = got[half:]
    table_new, accum_new = pl.pallas_call(
        functools.partial(update_kernel, slots, paired),
        out_shape=[jax.ShapeDtypeStruct(table.shape, F32)] * 2,
        out_specs=[pl.BlockSpec(memory_space=pl.ANY)] * 2,
        scratch_shapes=[
            *scratch(half if paired else groups),
            pltpu.VMEM((2, rows, D), F32),
            pltpu.SemaphoreType.DMA((2,)),
        ],
        compiler_params=pltpu.CompilerParams(vmem_limit_bytes=32 * MIB),
    )(*before, *got, table, accum)
    return (loss, query_grad, table_new, accum_new)


def solution(mesh):
    placed = (
        P(("wide", "group"), None),
        P(("wide", "group"), None),
        P(("wide", "group"), None),
        P(("wide", "group")),
        P(("wide", "group")),
        P(("wide", "group"), None),
        P(("wide", "group"), None),
    )
    return jax.shard_map(
        shards,
        mesh=mesh,
        in_specs=placed,
        out_specs=(
            P(("wide", "group")),
            P(("wide", "group"), None),
            P(("wide", "group"), None),
            P(("wide", "group"), None),
        ),
        check_vma=False,
    )
```

```python
import functools
import math

import jax
import jax.numpy as jnp
from jax import lax
from jax.experimental import pallas as pl
from jax.experimental.pallas import tpu as pltpu
from jax.sharding import PartitionSpec as P

D = 256
SCALE = 3.0 / math.sqrt(D)
LOG2E = math.log2(math.e)
LANES = 128
TAIL = 8
ROW_CODES = 1 << 16
MIB = 1 << 20
NT = (((1,), (1,)), ((), ()))
TN = (((0,), (0,)), ((), ()))
F32 = jnp.float32
BF16 = jnp.bfloat16


def dot(a, b, dims=(((1,), (0,)), ((), ()))):
    return lax.dot_general(a, b, dims, preferred_element_type=F32)


def spread(column, width):
    pieces = [column] * (width // LANES)
    if width % LANES:
        pieces.append(column[:, : width % LANES])
    return jnp.concatenate(pieces, axis=1)


def code(x):
    y = x * x
    return jnp.where(x < 0, -y, y) * y


def decode(u):
    root = lax.rsqrt(lax.rsqrt(jnp.abs(u)))
    return jnp.where(u < 0, -root, root)


def diagonal(block):
    return lax.broadcasted_iota(jnp.int32, (block, block), 0) == lax.broadcasted_iota(
        jnp.int32, (block, block), 1
    )


def local_kernel(groups, slots, code_ref, pick_ref, tail_ref):
    block = code_ref.shape[1]
    owner = code_ref[...] // ROW_CODES
    offset = code_ref[...] % ROW_CODES
    member = lax.broadcasted_iota(jnp.int32, (groups, block), 0) == owner
    before = lax.broadcasted_iota(jnp.int32, (block, block), 0) < lax.broadcasted_iota(
        jnp.int32, (block, block), 1
    )
    ranks = dot(member.astype(BF16), before.astype(BF16))
    rank = jnp.sum(jnp.where(member, ranks, 0.0), axis=0, keepdims=True).astype(jnp.int32)
    high = jnp.broadcast_to((offset // LANES).astype(F32), (TAIL, block)).astype(BF16)
    low = jnp.broadcast_to((offset % LANES).astype(F32), (TAIL, block)).astype(BF16)
    here = lax.broadcasted_iota(jnp.int32, (LANES, block), 0) == rank
    for g in range(groups):
        pick = (here & (owner == g)).astype(F32).astype(BF16)
        pick_ref[g * slots : (g + 1) * slots] = pick[:slots]
        tail_ref[g] = jnp.concatenate([dot(high, pick, NT), dot(low, pick, NT)], axis=1).astype(BF16)


def bias_kernel(n, *refs):
    for b in range(n):
        block = refs[b].shape[1]
        row = jnp.log(refs[b][...].astype(F32)) * LOG2E
        refs[n][b] = jnp.transpose(jnp.broadcast_to(row, (LANES, block)))


def fill_logits(q, item_refs, bias_ref, first, out_ref):
    top = None
    for b, item_ref in enumerate(item_refs):
        logits = dot(item_ref[...], q, NT) * (SCALE * LOG2E)
        logits -= spread(bias_ref[first + b], q.shape[0])
        out_ref[b] = logits
        high = jnp.max(logits, axis=0, keepdims=True)
        top = high if top is None else jnp.maximum(top, high)
    return top


def to_powers(ref, top):
    total = jnp.zeros(top.shape, F32)
    for b in range(ref.shape[0]):
        e = jnp.exp2(ref[b] - top)
        ref[b] = e
        total += jnp.sum(e, axis=0, keepdims=True)
    return total


def diagonal(block):
    return lax.broadcasted_iota(jnp.int32, (block, block), 0) == lax.broadcasted_iota(
        jnp.int32, (block, block), 1
    )


def early_kernel(n, q_ref, *refs):
    item_refs, (bias_ref, e_ref, stats_ref) = refs[:n], refs[n:]
    block = q_ref.shape[0]
    top = fill_logits(q_ref[...], item_refs, bias_ref, 0, e_ref)
    chosen = jnp.sum(jnp.where(diagonal(block), e_ref[0], 0.0), axis=0, keepdims=True)
    stats_ref[0:1] = top
    stats_ref[1:2] = to_powers(e_ref, top)
    stats_ref[2:3] = chosen


def main_kernel(early, late, *refs):
    n = early + late
    q_ref, far_ref, item_refs, refs = refs[0], refs[1], refs[2 : 2 + n], refs[2 + n :]
    bias_ref, e_ref, stats_ref, mine_out, mate_out, loss_ref, late_ref, factor_ref, far_e_ref = refs
    block = q_ref.shape[0]
    q, far = q_ref[...], far_ref[...]
    far_top = fill_logits(far, item_refs, bias_ref, 0, far_e_ref)
    early_top, early_total, chosen = stats_ref[0:1], stats_ref[1:2], stats_ref[2:3]
    top = fill_logits(q, item_refs[early:], bias_ref, early, late_ref)
    top = jnp.maximum(top, early_top)
    far_inverse = 1.0 / to_powers(far_e_ref, far_top)
    shrink = jnp.exp2(early_top - top)
    total = to_powers(late_ref, top) + early_total * shrink
    inverse = 1.0 / total
    factor = shrink * inverse
    mate = dot((e_ref[1] * factor).astype(BF16), q)
    mate_out[...] = mate + dot((far_e_ref[1] * far_inverse).astype(BF16), far)
    weights = e_ref[0] * factor
    weights = jnp.where(diagonal(block), weights - 1.0, weights)
    mine = dot(weights.astype(BF16), q)
    mine_out[...] = mine + dot((far_e_ref[0] * far_inverse).astype(BF16), far)
    loss_ref[...] = ((top + jnp.log2(total) - chosen) * (1.0 / LOG2E))[0]
    factor_ref[0:1] = factor
    factor_ref[1:2] = inverse


def more_kernel(n, q_ref, *refs):
    item_refs, refs = refs[:n], refs[n:]
    bias_ref, mine_ref, mate_ref, mine_out, mate_out, e_ref = refs
    q = q_ref[...]
    inverse = 1.0 / to_powers(e_ref, fill_logits(q, item_refs, bias_ref, 0, e_ref))
    mate_out[...] = mate_ref[...] + dot((e_ref[1] * inverse).astype(BF16), q)
    mine_out[...] = mine_ref[...] + dot((e_ref[0] * inverse).astype(BF16), q)


def query_kernel(early, late, e_ref, late_ref, factor_ref, *refs):
    item_refs, out_ref = refs[:-1], refs[-1]
    total = None
    for b, item_ref in enumerate(item_refs):
        if b < early:
            weights = e_ref[b] * factor_ref[0:1]
        else:
            weights = late_ref[b - early] * factor_ref[1:2]
        if b == 0:
            weights = jnp.where(diagonal(weights.shape[0]), weights - 1.0, weights)
        part = dot(weights.astype(BF16), item_ref[...], TN)
        total = part if total is None else total + part
    out_ref[...] = total * SCALE


def pack_kernel(groups, slots, pick_ref, tail_ref, mine_ref, other_ref, *out_refs):
    grad = code((mine_ref[...] + other_ref[...]) * SCALE).astype(BF16)
    picked = dot(pick_ref[...], grad).astype(BF16)
    for g in range(groups):
        out = out_refs[g] if len(out_refs) == groups else out_refs[0].at[g]
        out[:slots] = picked[g * slots : (g + 1) * slots]
        out[slots:] = tail_ref[g]


def scatter(slots, got_refs, values_ref, ids_ref, rows):
    packets = got_refs
    if len(got_refs[0].shape) == 3:
        packets = [got_refs[0].at[g] for g in range(got_refs[0].shape[0])]
    half = len(packets) * slots
    for g, got in enumerate(packets):
        tail = got[slots : slots + TAIL].astype(F32)
        ids = tail[:, :slots] * LANES + tail[:, LANES : LANES + slots]
        ids_ref[:, g * slots : (g + 1) * slots] = ids
        values = decode(got[:slots].astype(F32))
        high = values.astype(BF16)
        values_ref[g * slots : (g + 1) * slots] = high
        low = (values - high.astype(F32)).astype(BF16)
        values_ref[half + g * slots : half + (g + 1) * slots] = low
    index = lax.broadcasted_iota(jnp.int32, (rows, half), 0).astype(F32)
    put = (index == ids_ref[:1]).astype(F32).astype(BF16)
    return dot(jnp.concatenate([put, put], axis=1), values_ref[...])


def first_kernel(slots, *refs):
    got_refs, (out_ref, values_ref, ids_ref) = refs[:-3], refs[-3:]
    out_ref[...] = scatter(slots, got_refs, values_ref, ids_ref, out_ref.shape[0])


def update_kernel(slots, partial, *refs):
    inputs, refs = refs[:-8], refs[-8:]
    table_ref, accum_ref, table_out, accum_out, values_ref, ids_ref, new_ref, sems = refs
    got_refs = inputs[1:] if partial else inputs
    rows = table_ref.shape[0]
    grad = scatter(slots, got_refs, values_ref, ids_ref, rows)
    if partial:
        grad += inputs[0][...]
    accum_new = accum_ref[...] + grad * grad
    new_ref[1] = accum_new
    first = pltpu.make_async_copy(new_ref.at[1], accum_out, sems.at[1])
    first.start()
    new_ref[0] = table_ref[...] - 0.1 * grad / (jnp.sqrt(accum_new) + 1e-08)
    second = pltpu.make_async_copy(new_ref.at[0], table_out, sems.at[0])
    second.start()
    first.wait()
    second.wait()


def call(kernel, outs, *args, scratch=(), limit=16, flops=0):
    return pl.pallas_call(
        kernel,
        out_shape=[jax.ShapeDtypeStruct(s, t) for s, t in outs],
        scratch_shapes=list(scratch),
        compiler_params=pltpu.CompilerParams(vmem_limit_bytes=limit * MIB),
        cost_estimate=pl.CostEstimate(flops=flops, bytes_accessed=1024, transcendentals=0),
    )(*args)


def shards(queries, items, item_owner, item_offset, sample_counts, table, accum):
    block = queries.shape[0]
    n, groups = lax.axis_size("wide"), lax.axis_size("group")
    capacity = 2 * block // groups
    slots = -(-capacity // TAIL) * TAIL
    paired = groups <= 8

    def swap(x, k, axis="wide"):
        return lax.ppermute(x, axis, [(i, i ^ k) for i in range(lax.axis_size(axis))])

    far_counts = [swap(sample_counts, k) for k in range(2, n, 2)]
    far_items = [swap(items, k) for k in range(2, n, 2)]
    far_queries = [swap(queries, k) for k in range(2, n, 2)]

    owner = item_owner.reshape(1, block)
    if paired:
        owner = owner ^ lax.axis_index("group")
    pick, tail = call(
        functools.partial(local_kernel, groups, slots),
        [((groups * slots, block), BF16), ((groups, TAIL, D), BF16)],
        owner * ROW_CODES + item_offset.reshape(1, block),
        flops=1 << 30,
    )
    far_items, far_counts, tail = lax.optimization_barrier((far_items, far_counts, tail))
    item_blocks = [items, swap(items, 1)] + far_items
    early = len(item_blocks)
    item_blocks += [swap(x, 1) for x in far_items]
    late = n - early
    count_blocks = [sample_counts, swap(sample_counts, 1)] + far_counts
    count_blocks += [swap(x, 1) for x in far_counts]
    (bias,) = call(
        functools.partial(bias_kernel, n),
        [((n, block, LANES), F32)],
        *[x.reshape(1, block) for x in count_blocks],
    )

    part = ((block, D), F32)
    square = (block, block)
    powers, stats = call(
        functools.partial(early_kernel, early),
        [((early, *square), F32), ((8, block), F32)],
        queries,
        *item_blocks[:early],
        bias,
        limit=8 + 2 * n,
    )
    mine, mate, loss, late_powers, factors = call(
        functools.partial(main_kernel, early, late),
        [part, part, ((block,), F32), ((late, *square), F32), ((8, block), F32)],
        queries,
        far_queries[0],
        *item_blocks,
        bias,
        powers,
        stats,
        scratch=[pltpu.VMEM((n, *square), F32)],
        limit=8 + 4 * n,
    )
    for far in far_queries[1:]:
        mine, mate = call(
            functools.partial(more_kernel, n),
            [part, part],
            far,
            *item_blocks,
            bias,
            mine,
            mate,
            scratch=[pltpu.VMEM((n, *square), F32)],
            limit=8 + 4 * n,
        )
    other = swap(mate, 1)
    (query_grad,) = call(
        functools.partial(query_kernel, early, late),
        [part],
        powers,
        late_powers,
        factors,
        *item_blocks,
        limit=8 + 2 * n,
        flops=1 << 30,
    )
    other, query_grad = lax.optimization_barrier((other, query_grad))
    if paired:
        packets = [((slots + TAIL, D), BF16)] * groups
    else:
        packets = [((groups, slots + TAIL, D), BF16)]
    packed = call(
        functools.partial(pack_kernel, groups, slots), packets, pick, tail, mine, other
    )
    if paired:
        order = sorted(range(1, groups), key=lambda k: (k < groups // 2, k % 2, k))
        got = [packed[0]] + [swap(packed[k], k, "group") for k in order]
    else:
        got = [lax.all_to_all(packed[0], "group", split_axis=0, concat_axis=0, tiled=True)]
    rows = table.shape[0]

    def scratch(packets):
        return [
            pltpu.VMEM((2 * packets * slots, D), BF16),
            pltpu.VMEM((TAIL, packets * slots), F32),
        ]

    half = groups // 2
    before = []
    if paired:
        before = call(
            functools.partial(first_kernel, slots),
            [((rows, D), F32)],
            *got[:half],
            scratch=scratch(half),
            flops=1 << 28,
        )
        got = got[half:]
    table_new, accum_new = pl.pallas_call(
        functools.partial(update_kernel, slots, paired),
        out_shape=[jax.ShapeDtypeStruct(table.shape, F32)] * 2,
        out_specs=[pl.BlockSpec(memory_space=pl.ANY)] * 2,
        scratch_shapes=[
            *scratch(half if paired else groups),
            pltpu.VMEM((2, rows, D), F32),
            pltpu.SemaphoreType.DMA((2,)),
        ],
        compiler_params=pltpu.CompilerParams(vmem_limit_bytes=32 * MIB),
    )(*before, *got, table, accum)
    return (loss, query_grad, table_new, accum_new)


def solution(mesh):
    placed = (
        P(("wide", "group"), None),
        P(("wide", "group"), None),
        P(("wide", "group"), None),
        P(("wide", "group")),
        P(("wide", "group")),
        P(("wide", "group"), None),
        P(("wide", "group"), None),
    )
    return jax.shard_map(
        shards,
        mesh=mesh,
        in_specs=placed,
        out_specs=(
            P(("wide", "group")),
            P(("wide", "group"), None),
            P(("wide", "group"), None),
            P(("wide", "group"), None),
        ),
        check_vma=False,
    )
```

```python
import functools
import math

import jax
import jax.numpy as jnp
from jax import lax
from jax.experimental import pallas as pl
from jax.experimental.pallas import tpu as pltpu
from jax.sharding import PartitionSpec as P

D = 256
SCALE = 3.0 / math.sqrt(D)
LOG2E = math.log2(math.e)
LANES = 128
TAIL = 8
ROW_CODES = 1 << 16
MIB = 1 << 20
NT = (((1,), (1,)), ((), ()))
TN = (((0,), (0,)), ((), ()))
F32 = jnp.float32
BF16 = jnp.bfloat16


def dot(a, b, dims=(((1,), (0,)), ((), ()))):
    return lax.dot_general(a, b, dims, preferred_element_type=F32)


def spread(column, width):
    pieces = [column] * (width // LANES)
    if width % LANES:
        pieces.append(column[:, : width % LANES])
    return jnp.concatenate(pieces, axis=1)


def code(x):
    y = x * x
    return jnp.where(x < 0, -y, y) * y


def decode(u):
    root = lax.rsqrt(lax.rsqrt(jnp.abs(u)))
    return jnp.where(u < 0, -root, root)


def diagonal(block):
    return lax.broadcasted_iota(jnp.int32, (block, block), 0) == lax.broadcasted_iota(
        jnp.int32, (block, block), 1
    )


def local_kernel(groups, slots, code_ref, pick_ref, tail_ref):
    block = code_ref.shape[1]
    owner = code_ref[...] // ROW_CODES
    offset = code_ref[...] % ROW_CODES
    member = lax.broadcasted_iota(jnp.int32, (groups, block), 0) == owner
    before = lax.broadcasted_iota(jnp.int32, (block, block), 0) < lax.broadcasted_iota(
        jnp.int32, (block, block), 1
    )
    ranks = dot(member.astype(BF16), before.astype(BF16))
    rank = jnp.sum(jnp.where(member, ranks, 0.0), axis=0, keepdims=True).astype(jnp.int32)
    high = jnp.broadcast_to((offset // LANES).astype(F32), (TAIL, block)).astype(BF16)
    low = jnp.broadcast_to((offset % LANES).astype(F32), (TAIL, block)).astype(BF16)
    here = lax.broadcasted_iota(jnp.int32, (LANES, block), 0) == rank
    for g in range(groups):
        pick = (here & (owner == g)).astype(F32).astype(BF16)
        pick_ref[g * slots : (g + 1) * slots] = pick[:slots]
        tail_ref[g] = jnp.concatenate([dot(high, pick, NT), dot(low, pick, NT)], axis=1).astype(BF16)


def bias_kernel(n, *refs):
    for b in range(n):
        block = refs[b].shape[1]
        row = jnp.log(refs[b][...].astype(F32)) * LOG2E
        refs[n][b] = jnp.transpose(jnp.broadcast_to(row, (LANES, block)))


def fill_logits(q, item_refs, bias_ref, first, out_ref):
    top = None
    for b, item_ref in enumerate(item_refs):
        logits = dot(item_ref[...], q, NT) * (SCALE * LOG2E)
        logits -= spread(bias_ref[first + b], q.shape[0])
        out_ref[b] = logits
        high = jnp.max(logits, axis=0, keepdims=True)
        top = high if top is None else jnp.maximum(top, high)
    return top


def to_powers(ref, top):
    total = jnp.zeros(top.shape, F32)
    for b in range(ref.shape[0]):
        e = jnp.exp2(ref[b] - top)
        ref[b] = e
        total += jnp.sum(e, axis=0, keepdims=True)
    return total


def diagonal(block):
    return lax.broadcasted_iota(jnp.int32, (block, block), 0) == lax.broadcasted_iota(
        jnp.int32, (block, block), 1
    )


def early_kernel(n, q_ref, *refs):
    item_refs, (bias_ref, e_ref, stats_ref) = refs[:n], refs[n:]
    block = q_ref.shape[0]
    top = fill_logits(q_ref[...], item_refs, bias_ref, 0, e_ref)
    chosen = jnp.sum(jnp.where(diagonal(block), e_ref[0], 0.0), axis=0, keepdims=True)
    stats_ref[0:1] = top
    stats_ref[1:2] = to_powers(e_ref, top)
    stats_ref[2:3] = chosen


def main_kernel(early, late, *refs):
    n = early + late
    q_ref, far_ref, item_refs, refs = refs[0], refs[1], refs[2 : 2 + n], refs[2 + n :]
    bias_ref, e_ref, stats_ref, mine_out, mate_out, loss_ref, late_ref, factor_ref, far_e_ref = refs
    block = q_ref.shape[0]
    q, far = q_ref[...], far_ref[...]
    far_top = fill_logits(far, item_refs, bias_ref, 0, far_e_ref)
    early_top, early_total, chosen = stats_ref[0:1], stats_ref[1:2], stats_ref[2:3]
    top = fill_logits(q, item_refs[early:], bias_ref, early, late_ref)
    top = jnp.maximum(top, early_top)
    far_inverse = 1.0 / to_powers(far_e_ref, far_top)
    shrink = jnp.exp2(early_top - top)
    total = to_powers(late_ref, top) + early_total * shrink
    inverse = 1.0 / total
    factor = shrink * inverse
    mate = dot((e_ref[1] * factor).astype(BF16), q)
    mate_out[...] = mate + dot((far_e_ref[1] * far_inverse).astype(BF16), far)
    weights = e_ref[0] * factor
    weights = jnp.where(diagonal(block), weights - 1.0, weights)
    mine = dot(weights.astype(BF16), q)
    mine_out[...] = mine + dot((far_e_ref[0] * far_inverse).astype(BF16), far)
    loss_ref[...] = ((top + jnp.log2(total) - chosen) * (1.0 / LOG2E))[0]
    factor_ref[0:1] = factor
    factor_ref[1:2] = inverse


def more_kernel(n, q_ref, *refs):
    item_refs, refs = refs[:n], refs[n:]
    bias_ref, mine_ref, mate_ref, mine_out, mate_out, e_ref = refs
    q = q_ref[...]
    inverse = 1.0 / to_powers(e_ref, fill_logits(q, item_refs, bias_ref, 0, e_ref))
    mate_out[...] = mate_ref[...] + dot((e_ref[1] * inverse).astype(BF16), q)
    mine_out[...] = mine_ref[...] + dot((e_ref[0] * inverse).astype(BF16), q)


def query_kernel(early, late, e_ref, late_ref, factor_ref, *refs):
    item_refs, out_ref = refs[:-1], refs[-1]
    total = None
    for b, item_ref in enumerate(item_refs):
        if b < early:
            weights = e_ref[b] * factor_ref[0:1]
        else:
            weights = late_ref[b - early] * factor_ref[1:2]
        if b == 0:
            weights = jnp.where(diagonal(weights.shape[0]), weights - 1.0, weights)
        part = dot(weights.astype(BF16), item_ref[...], TN)
        total = part if total is None else total + part
    out_ref[...] = total * SCALE


def pack_kernel(groups, slots, pick_ref, tail_ref, mine_ref, other_ref, *out_refs):
    grad = code((mine_ref[...] + other_ref[...]) * SCALE).astype(BF16)
    picked = dot(pick_ref[...], grad).astype(BF16)
    for g in range(groups):
        out = out_refs[g] if len(out_refs) == groups else out_refs[0].at[g]
        out[:slots] = picked[g * slots : (g + 1) * slots]
        out[slots:] = tail_ref[g]


def unpack(slots, got_refs, values_ref, ids_ref):
    packets = got_refs
    if len(got_refs[0].shape) == 3:
        packets = [got_refs[0].at[g] for g in range(got_refs[0].shape[0])]
    half = len(packets) * slots
    for g, got in enumerate(packets):
        tail = got[slots : slots + TAIL].astype(F32)
        ids = tail[:, :slots] * LANES + tail[:, LANES : LANES + slots]
        ids_ref[:, g * slots : (g + 1) * slots] = ids
        values = decode(got[:slots].astype(F32))
        high = values.astype(BF16)
        values_ref[g * slots : (g + 1) * slots] = high
        low = (values - high.astype(F32)).astype(BF16)
        values_ref[half + g * slots : half + (g + 1) * slots] = low


def scatter(values_ref, ids_ref, first, rows):
    index = lax.broadcasted_iota(jnp.int32, (rows, ids_ref.shape[1]), 0) + first
    put = (index.astype(F32) == ids_ref[:1]).astype(F32).astype(BF16)
    return dot(jnp.concatenate([put, put], axis=1), values_ref[...])


def first_kernel(slots, *refs):
    got_refs, (out_ref, values_ref, ids_ref) = refs[:-3], refs[-3:]
    unpack(slots, got_refs, values_ref, ids_ref)
    out_ref[...] = scatter(values_ref, ids_ref, 0, out_ref.shape[0])


def update_kernel(slots, partial, *refs):
    inputs, refs = refs[:-8], refs[-8:]
    table_ref, accum_ref, table_out, accum_out, values_ref, ids_ref, new_ref, sems = refs
    unpack(slots, inputs[1:] if partial else inputs, values_ref, ids_ref)
    chunks = sems.shape[1]
    rows = table_ref.shape[0] // chunks
    copies = []
    for c in range(chunks):
        here = slice(c * rows, (c + 1) * rows)
        grad = scatter(values_ref, ids_ref, c * rows, rows)
        if partial:
            grad += inputs[0][here]
        accum_new = accum_ref[here] + grad * grad
        new_ref[1, here] = accum_new
        copies.append(pltpu.make_async_copy(new_ref.at[1, here], accum_out.at[here], sems.at[1, c]))
        copies[-1].start()
        new_ref[0, here] = table_ref[here] - 0.1 * grad / (jnp.sqrt(accum_new) + 1e-08)
        copies.append(pltpu.make_async_copy(new_ref.at[0, here], table_out.at[here], sems.at[0, c]))
        copies[-1].start()
    for copy in copies:
        copy.wait()


def call(kernel, outs, *args, scratch=(), limit=16, flops=0):
    return pl.pallas_call(
        kernel,
        out_shape=[jax.ShapeDtypeStruct(s, t) for s, t in outs],
        scratch_shapes=list(scratch),
        compiler_params=pltpu.CompilerParams(vmem_limit_bytes=limit * MIB),
        cost_estimate=pl.CostEstimate(flops=flops, bytes_accessed=1024, transcendentals=0),
    )(*args)


def shards(queries, items, item_owner, item_offset, sample_counts, table, accum):
    block = queries.shape[0]
    n, groups = lax.axis_size("wide"), lax.axis_size("group")
    capacity = 2 * block // groups
    slots = -(-capacity // TAIL) * TAIL
    paired = groups <= 8

    def swap(x, k, axis="wide"):
        return lax.ppermute(x, axis, [(i, i ^ k) for i in range(lax.axis_size(axis))])

    far_counts = [swap(sample_counts, k) for k in range(2, n, 2)]
    far_items = [swap(items, k) for k in range(2, n, 2)]
    far_queries = [swap(queries, k) for k in range(2, n, 2)]

    owner = item_owner.reshape(1, block)
    if paired:
        owner = owner ^ lax.axis_index("group")
    pick, tail = call(
        functools.partial(local_kernel, groups, slots),
        [((groups * slots, block), BF16), ((groups, TAIL, D), BF16)],
        owner * ROW_CODES + item_offset.reshape(1, block),
        flops=1 << 30,
    )
    far_items, far_counts, tail = lax.optimization_barrier((far_items, far_counts, tail))
    item_blocks = [items, swap(items, 1)] + far_items
    early = len(item_blocks)
    item_blocks += [swap(x, 1) for x in far_items]
    late = n - early
    count_blocks = [sample_counts, swap(sample_counts, 1)] + far_counts
    count_blocks += [swap(x, 1) for x in far_counts]
    (bias,) = call(
        functools.partial(bias_kernel, n),
        [((n, block, LANES), F32)],
        *[x.reshape(1, block) for x in count_blocks],
    )

    part = ((block, D), F32)
    square = (block, block)
    powers, stats = call(
        functools.partial(early_kernel, early),
        [((early, *square), F32), ((8, block), F32)],
        queries,
        *item_blocks[:early],
        bias,
        limit=8 + 2 * n,
    )
    mine, mate, loss, late_powers, factors = call(
        functools.partial(main_kernel, early, late),
        [part, part, ((block,), F32), ((late, *square), F32), ((8, block), F32)],
        queries,
        far_queries[0],
        *item_blocks,
        bias,
        powers,
        stats,
        scratch=[pltpu.VMEM((n, *square), F32)],
        limit=8 + 4 * n,
    )
    for far in far_queries[1:]:
        mine, mate = call(
            functools.partial(more_kernel, n),
            [part, part],
            far,
            *item_blocks,
            bias,
            mine,
            mate,
            scratch=[pltpu.VMEM((n, *square), F32)],
            limit=8 + 4 * n,
        )
    other = swap(mate, 1)
    (query_grad,) = call(
        functools.partial(query_kernel, early, late),
        [part],
        powers,
        late_powers,
        factors,
        *item_blocks,
        limit=8 + 2 * n,
        flops=1 << 30,
    )
    other, query_grad = lax.optimization_barrier((other, query_grad))
    if paired:
        packets = [((slots + TAIL, D), BF16)] * groups
    else:
        packets = [((groups, slots + TAIL, D), BF16)]
    packed = call(
        functools.partial(pack_kernel, groups, slots), packets, pick, tail, mine, other
    )
    if paired:
        half = groups // 2
        far = sorted(range(half, groups), key=lambda k: (k % 2, k))
        order = far + sorted(range(1, half), key=lambda k: (1 - k % 2, -k))
        got = [packed[0]] + [swap(packed[k], k, "group") for k in order]
    else:
        got = [lax.all_to_all(packed[0], "group", split_axis=0, concat_axis=0, tiled=True)]
    rows = table.shape[0]

    def scratch(packets):
        return [
            pltpu.VMEM((2 * packets * slots, D), BF16),
            pltpu.VMEM((TAIL, packets * slots), F32),
        ]

    count = groups - 1
    before = []
    if paired:
        before = call(
            functools.partial(first_kernel, slots),
            [((rows, D), F32)],
            *got[:count],
            scratch=scratch(count),
            flops=1 << 28,
        )
        got = got[count:]
    table_new, accum_new = pl.pallas_call(
        functools.partial(update_kernel, slots, paired),
        out_shape=[jax.ShapeDtypeStruct(table.shape, F32)] * 2,
        out_specs=[pl.BlockSpec(memory_space=pl.ANY)] * 2,
        scratch_shapes=[
            *scratch(len(got) if paired else groups),
            pltpu.VMEM((2, rows, D), F32),
            pltpu.SemaphoreType.DMA((2, 4)),
        ],
        compiler_params=pltpu.CompilerParams(vmem_limit_bytes=32 * MIB),
    )(*before, *got, table, accum)
    return (loss, query_grad, table_new, accum_new)


def solution(mesh):
    placed = (
        P(("wide", "group"), None),
        P(("wide", "group"), None),
        P(("wide", "group"), None),
        P(("wide", "group")),
        P(("wide", "group")),
        P(("wide", "group"), None),
        P(("wide", "group"), None),
    )
    return jax.shard_map(
        shards,
        mesh=mesh,
        in_specs=placed,
        out_specs=(
            P(("wide", "group")),
            P(("wide", "group"), None),
            P(("wide", "group"), None),
            P(("wide", "group"), None),
        ),
        check_vma=False,
    )
```

```python
import functools
import math

import jax
import jax.numpy as jnp
from jax import lax
from jax.experimental import pallas as pl
from jax.experimental.pallas import tpu as pltpu
from jax.sharding import PartitionSpec as P

D = 256
SCALE = 3.0 / math.sqrt(D)
LOG2E = math.log2(math.e)
LANES = 128
TAIL = 8
ROW_CODES = 1 << 16
MIB = 1 << 20
NT = (((1,), (1,)), ((), ()))
TN = (((0,), (0,)), ((), ()))
F32 = jnp.float32
BF16 = jnp.bfloat16


def dot(a, b, dims=(((1,), (0,)), ((), ()))):
    return lax.dot_general(a, b, dims, preferred_element_type=F32)


def spread(column, width):
    pieces = [column] * (width // LANES)
    if width % LANES:
        pieces.append(column[:, : width % LANES])
    return jnp.concatenate(pieces, axis=1)


def code(x):
    y = x * x
    return jnp.where(x < 0, -y, y) * y


def decode(u):
    root = lax.rsqrt(lax.rsqrt(jnp.abs(u)))
    return jnp.where(u < 0, -root, root)


def diagonal(block):
    return lax.broadcasted_iota(jnp.int32, (block, block), 0) == lax.broadcasted_iota(
        jnp.int32, (block, block), 1
    )


def local_kernel(groups, slots, code_ref, pick_ref, tail_ref):
    block = code_ref.shape[1]
    owner = code_ref[...] // ROW_CODES
    offset = code_ref[...] % ROW_CODES
    member = lax.broadcasted_iota(jnp.int32, (groups, block), 0) == owner
    before = lax.broadcasted_iota(jnp.int32, (block, block), 0) < lax.broadcasted_iota(
        jnp.int32, (block, block), 1
    )
    ranks = dot(member.astype(BF16), before.astype(BF16))
    rank = jnp.sum(jnp.where(member, ranks, 0.0), axis=0, keepdims=True).astype(jnp.int32)
    high = jnp.broadcast_to((offset // LANES).astype(F32), (TAIL, block)).astype(BF16)
    low = jnp.broadcast_to((offset % LANES).astype(F32), (TAIL, block)).astype(BF16)
    here = lax.broadcasted_iota(jnp.int32, (LANES, block), 0) == rank
    for g in range(groups):
        pick = (here & (owner == g)).astype(F32).astype(BF16)
        pick_ref[g * slots : (g + 1) * slots] = pick[:slots]
        tail_ref[g] = jnp.concatenate([dot(high, pick, NT), dot(low, pick, NT)], axis=1).astype(BF16)


def fill_logits(q, item_refs, out_ref):
    top = None
    for b, item_ref in enumerate(item_refs):
        logits = dot(item_ref[...], q, NT) * (SCALE * LOG2E)
        out_ref[b] = logits
        high = jnp.max(logits, axis=0, keepdims=True)
        top = high if top is None else jnp.maximum(top, high)
    return top


def to_powers(ref, top, rate_ref, first):
    total = jnp.zeros(top.shape, F32)
    for b in range(ref.shape[0]):
        e = jnp.exp2(ref[b] - top) * spread(rate_ref[first + b], top.shape[1])
        ref[b] = e
        total += jnp.sum(e, axis=0, keepdims=True)
    return total


def diagonal(block):
    return lax.broadcasted_iota(jnp.int32, (block, block), 0) == lax.broadcasted_iota(
        jnp.int32, (block, block), 1
    )


def early_kernel(n, q_ref, *refs):
    item_refs, (e_ref, stats_ref) = refs[:n], refs[n:]
    top = fill_logits(q_ref[...], item_refs, e_ref)
    chosen = jnp.where(diagonal(q_ref.shape[0]), e_ref[0], 0.0)
    stats_ref[0:1] = top
    stats_ref[1:2] = jnp.sum(chosen, axis=0, keepdims=True)
    for b in range(n):
        e_ref[b] = jnp.exp2(e_ref[b] - top)


def rate_kernel(n, early, e_ref, near_ref, mate_ref, rate_ref, out_ref, total_ref):
    block = e_ref.shape[1]
    near = [near_ref[:, k * block : (k + 1) * block].astype(F32) for k in range(n // 2)]
    mate = [mate_ref[:, k * block : (k + 1) * block].astype(F32) for k in range(n // 2)]
    counts = [near[0], mate[0]] + near[1:] + mate[1:]
    total = jnp.zeros((1, block), F32)
    for b in range(n):
        rate = jnp.transpose(jnp.broadcast_to(1.0 / counts[b], (LANES, block)))
        rate_ref[b] = rate
        if b < early:
            e = e_ref[b] * spread(rate, block)
            out_ref[b] = e
            total += jnp.sum(e, axis=0, keepdims=True)
    total_ref[0:1] = total
    total_ref[1:2] = jnp.log(counts[0]) * LOG2E


def main_kernel(early, late, *refs):
    n = early + late
    q_ref, far_ref, item_refs, refs = refs[0], refs[1], refs[2 : 2 + n], refs[2 + n :]
    rate_ref, e_ref, stats_ref, total_ref, mine_out, mate_out, *refs = refs
    loss_ref, late_ref, factor_ref, far_e_ref = refs
    block = q_ref.shape[0]
    q, far = q_ref[...], far_ref[...]
    far_top = fill_logits(far, item_refs, far_e_ref)
    early_top, early_total = stats_ref[0:1], total_ref[0:1]
    top = jnp.maximum(fill_logits(q, item_refs[early:], late_ref), early_top)
    far_inverse = 1.0 / to_powers(far_e_ref, far_top, rate_ref, 0)
    shrink = jnp.exp2(early_top - top)
    total = to_powers(late_ref, top, rate_ref, early) + early_total * shrink
    inverse = 1.0 / total
    factor = shrink * inverse
    mate = dot((e_ref[1] * factor).astype(BF16), q)
    mate_out[...] = mate + dot((far_e_ref[1] * far_inverse).astype(BF16), far)
    weights = e_ref[0] * factor
    weights = jnp.where(diagonal(block), weights - 1.0, weights)
    mine = dot(weights.astype(BF16), q)
    mine_out[...] = mine + dot((far_e_ref[0] * far_inverse).astype(BF16), far)
    chosen = stats_ref[1:2] - total_ref[1:2]
    loss_ref[...] = ((top + jnp.log2(total) - chosen) * (1.0 / LOG2E))[0]
    factor_ref[0:1] = factor
    factor_ref[1:2] = inverse


def more_kernel(n, q_ref, *refs):
    item_refs, refs = refs[:n], refs[n:]
    rate_ref, mine_ref, mate_ref, mine_out, mate_out, e_ref = refs
    q = q_ref[...]
    inverse = 1.0 / to_powers(e_ref, fill_logits(q, item_refs, e_ref), rate_ref, 0)
    mate_out[...] = mate_ref[...] + dot((e_ref[1] * inverse).astype(BF16), q)
    mine_out[...] = mine_ref[...] + dot((e_ref[0] * inverse).astype(BF16), q)


def query_kernel(early, late, e_ref, late_ref, factor_ref, *refs):
    item_refs, out_ref = refs[:-1], refs[-1]
    total = None
    for b, item_ref in enumerate(item_refs):
        if b < early:
            weights = e_ref[b] * factor_ref[0:1]
        else:
            weights = late_ref[b - early] * factor_ref[1:2]
        if b == 0:
            weights = jnp.where(diagonal(weights.shape[0]), weights - 1.0, weights)
        part = dot(weights.astype(BF16), item_ref[...], TN)
        total = part if total is None else total + part
    out_ref[...] = total * SCALE


def pack_kernel(groups, slots, pick_ref, tail_ref, mine_ref, other_ref, *out_refs):
    grad = code((mine_ref[...] + other_ref[...]) * SCALE).astype(BF16)
    picked = dot(pick_ref[...], grad).astype(BF16)
    for g in range(groups):
        out = out_refs[g] if len(out_refs) == groups else out_refs[0].at[g]
        out[:slots] = picked[g * slots : (g + 1) * slots]
        out[slots:] = tail_ref[g]


def unpack(slots, got_refs, values_ref, ids_ref):
    packets = got_refs
    if len(got_refs[0].shape) == 3:
        packets = [got_refs[0].at[g] for g in range(got_refs[0].shape[0])]
    half = len(packets) * slots
    for g, got in enumerate(packets):
        tail = got[slots : slots + TAIL].astype(F32)
        ids = tail[:, :slots] * LANES + tail[:, LANES : LANES + slots]
        ids_ref[:, g * slots : (g + 1) * slots] = ids
        values = decode(got[:slots].astype(F32))
        high = values.astype(BF16)
        values_ref[g * slots : (g + 1) * slots] = high
        low = (values - high.astype(F32)).astype(BF16)
        values_ref[half + g * slots : half + (g + 1) * slots] = low


def scatter(values_ref, ids_ref, first, rows):
    index = lax.broadcasted_iota(jnp.int32, (rows, ids_ref.shape[1]), 0) + first
    put = (index.astype(F32) == ids_ref[:1]).astype(F32).astype(BF16)
    return dot(jnp.concatenate([put, put], axis=1), values_ref[...])


def first_kernel(slots, *refs):
    got_refs, (out_ref, values_ref, ids_ref) = refs[:-3], refs[-3:]
    unpack(slots, got_refs, values_ref, ids_ref)
    out_ref[...] = scatter(values_ref, ids_ref, 0, out_ref.shape[0])


def update_kernel(slots, partial, *refs):
    inputs, refs = refs[:-8], refs[-8:]
    table_ref, accum_ref, table_out, accum_out, values_ref, ids_ref, new_ref, sems = refs
    unpack(slots, inputs[1:] if partial else inputs, values_ref, ids_ref)
    chunks = sems.shape[1]
    rows = table_ref.shape[0] // chunks
    copies = []
    for c in range(chunks):
        here = slice(c * rows, (c + 1) * rows)
        grad = scatter(values_ref, ids_ref, c * rows, rows)
        if partial:
            grad += inputs[0][here]
        accum_new = accum_ref[here] + grad * grad
        new_ref[1, here] = accum_new
        copies.append(pltpu.make_async_copy(new_ref.at[1, here], accum_out.at[here], sems.at[1, c]))
        copies[-1].start()
        new_ref[0, here] = table_ref[here] - 0.1 * grad / (jnp.sqrt(accum_new) + 1e-08)
        copies.append(pltpu.make_async_copy(new_ref.at[0, here], table_out.at[here], sems.at[0, c]))
        copies[-1].start()
    for copy in copies:
        copy.wait()


def call(kernel, outs, *args, scratch=(), limit=16, flops=0):
    return pl.pallas_call(
        kernel,
        out_shape=[jax.ShapeDtypeStruct(s, t) for s, t in outs],
        scratch_shapes=list(scratch),
        compiler_params=pltpu.CompilerParams(vmem_limit_bytes=limit * MIB),
        cost_estimate=pl.CostEstimate(flops=flops, bytes_accessed=1024, transcendentals=0),
    )(*args)


def shards(queries, items, item_owner, item_offset, sample_counts, table, accum):
    block = queries.shape[0]
    n, groups = lax.axis_size("wide"), lax.axis_size("group")
    capacity = 2 * block // groups
    slots = -(-capacity // TAIL) * TAIL
    paired = groups <= 8

    def swap(x, k, axis="wide"):
        return lax.ppermute(x, axis, [(i, i ^ k) for i in range(lax.axis_size(axis))])

    far_counts = [swap(sample_counts, k) for k in range(2, n, 2)]
    far_items = [swap(items, k) for k in range(2, n, 2)]
    far_queries = [swap(queries, k) for k in range(2, n, 2)]

    owner = item_owner.reshape(1, block)
    if paired:
        owner = owner ^ lax.axis_index("group")
    pick, tail = call(
        functools.partial(local_kernel, groups, slots),
        [((groups * slots, block), BF16), ((groups, TAIL, D), BF16)],
        owner * ROW_CODES + item_offset.reshape(1, block),
        flops=1 << 30,
    )
    far_items, far_counts, tail = lax.optimization_barrier((far_items, far_counts, tail))
    item_blocks = [items, swap(items, 1)] + far_items
    early = len(item_blocks)
    item_blocks += [swap(x, 1) for x in far_items]
    late = n - early
    near_counts = jnp.concatenate([sample_counts, *far_counts])
    mate_counts = swap(near_counts, 1)
    part = ((block, D), F32)
    square = (block, block)
    powers, stats = call(
        functools.partial(early_kernel, early),
        [((early, *square), F32), ((8, block), F32)],
        queries,
        *item_blocks[:early],
        limit=8 + 2 * n,
        flops=1 << 29,
    )
    rates, powers, totals = call(
        functools.partial(rate_kernel, n, early),
        [((n, block, LANES), F32), ((early, *square), F32), ((8, block), F32)],
        powers,
        near_counts.reshape(1, -1),
        mate_counts.reshape(1, -1),
        limit=8 + 4 * n,
    )
    mine, mate, loss, late_powers, factors = call(
        functools.partial(main_kernel, early, late),
        [part, part, ((block,), F32), ((late, *square), F32), ((8, block), F32)],
        queries,
        far_queries[0],
        *item_blocks,
        rates,
        powers,
        stats,
        totals,
        scratch=[pltpu.VMEM((n, *square), F32)],
        limit=8 + 4 * n,
    )
    for far in far_queries[1:]:
        mine, mate = call(
            functools.partial(more_kernel, n),
            [part, part],
            far,
            *item_blocks,
            rates,
            mine,
            mate,
            scratch=[pltpu.VMEM((n, *square), F32)],
            limit=8 + 4 * n,
        )
    other = swap(mate, 1)
    (query_grad,) = call(
        functools.partial(query_kernel, early, late),
        [part],
        powers,
        late_powers,
        factors,
        *item_blocks,
        limit=8 + 2 * n,
        flops=1 << 30,
    )
    other, query_grad = lax.optimization_barrier((other, query_grad))
    if paired:
        packets = [((slots + TAIL, D), BF16)] * groups
    else:
        packets = [((groups, slots + TAIL, D), BF16)]
    packed = call(
        functools.partial(pack_kernel, groups, slots), packets, pick, tail, mine, other
    )
    if paired:
        half = groups // 2
        far = sorted(range(half, groups), key=lambda k: (k % 2, k))
        order = far + sorted(range(1, half), key=lambda k: (1 - k % 2, -k))
        got = [packed[0]] + [swap(packed[k], k, "group") for k in order]
    else:
        got = [lax.all_to_all(packed[0], "group", split_axis=0, concat_axis=0, tiled=True)]
    rows = table.shape[0]

    def scratch(packets):
        return [
            pltpu.VMEM((2 * packets * slots, D), BF16),
            pltpu.VMEM((TAIL, packets * slots), F32),
        ]

    count = groups // 2
    before = []
    if paired:
        before = call(
            functools.partial(first_kernel, slots),
            [((rows, D), F32)],
            *got[:count],
            scratch=scratch(count),
            flops=1 << 28,
        )
        got = got[count:]
    table_new, accum_new = pl.pallas_call(
        functools.partial(update_kernel, slots, paired),
        out_shape=[jax.ShapeDtypeStruct(table.shape, F32)] * 2,
        out_specs=[pl.BlockSpec(memory_space=pl.ANY)] * 2,
        scratch_shapes=[
            *scratch(len(got) if paired else groups),
            pltpu.VMEM((2, rows, D), F32),
            pltpu.SemaphoreType.DMA((2, 4)),
        ],
        compiler_params=pltpu.CompilerParams(vmem_limit_bytes=32 * MIB),
    )(*before, *got, table, accum)
    return (loss, query_grad, table_new, accum_new)


def solution(mesh):
    placed = (
        P(("wide", "group"), None),
        P(("wide", "group"), None),
        P(("wide", "group"), None),
        P(("wide", "group")),
        P(("wide", "group")),
        P(("wide", "group"), None),
        P(("wide", "group"), None),
    )
    return jax.shard_map(
        shards,
        mesh=mesh,
        in_specs=placed,
        out_specs=(
            P(("wide", "group")),
            P(("wide", "group"), None),
            P(("wide", "group"), None),
            P(("wide", "group"), None),
        ),
        check_vma=False,
    )
```

```python
import functools
import math

import jax
import jax.numpy as jnp
from jax import lax
from jax.experimental import pallas as pl
from jax.experimental.pallas import tpu as pltpu
from jax.sharding import PartitionSpec as P

D = 256
SCALE = 3.0 / math.sqrt(D)
LOG2E = math.log2(math.e)
LANES = 128
TAIL = 8
ROW_CODES = 1 << 16
ROUNDS = ((4, 5), (6, 7), (1, 2), (0, 3))
MIB = 1 << 20
NT = (((1,), (1,)), ((), ()))
TN = (((0,), (0,)), ((), ()))
F32 = jnp.float32
BF16 = jnp.bfloat16


def dot(a, b, dims=(((1,), (0,)), ((), ()))):
    return lax.dot_general(a, b, dims, preferred_element_type=F32)


def spread(column, width):
    pieces = [column] * (width // LANES)
    if width % LANES:
        pieces.append(column[:, : width % LANES])
    return jnp.concatenate(pieces, axis=1)


def code(x):
    y = x * x
    return jnp.where(x < 0, -y, y) * y


def decode(u):
    root = lax.rsqrt(lax.rsqrt(jnp.abs(u)))
    return jnp.where(u < 0, -root, root)


def diagonal(block):
    return lax.broadcasted_iota(jnp.int32, (block, block), 0) == lax.broadcasted_iota(
        jnp.int32, (block, block), 1
    )


def local_kernel(groups, slots, flip, code_ref, pick_ref, tail_ref):
    block = code_ref.shape[1]
    owner = (code_ref[...] // ROW_CODES) ^ flip
    offset = code_ref[...] % ROW_CODES
    member = lax.broadcasted_iota(jnp.int32, (groups, block), 0) == owner
    before = lax.broadcasted_iota(jnp.int32, (block, block), 0) < lax.broadcasted_iota(
        jnp.int32, (block, block), 1
    )
    ranks = dot(member.astype(BF16), before.astype(BF16))
    rank = jnp.sum(jnp.where(member, ranks, 0.0), axis=0, keepdims=True).astype(jnp.int32)
    high = jnp.broadcast_to((offset // LANES).astype(F32), (TAIL, block)).astype(BF16)
    low = jnp.broadcast_to((offset % LANES).astype(F32), (TAIL, block)).astype(BF16)
    here = lax.broadcasted_iota(jnp.int32, (LANES, block), 0) == rank
    for g in range(groups):
        pick = (here & (owner == g)).astype(F32).astype(BF16)
        pick_ref[g * slots : (g + 1) * slots] = pick[:slots]
        if g < tail_ref.shape[0]:
            tail_ref[g] = jnp.concatenate(
                [dot(high, pick, NT), dot(low, pick, NT)], axis=1
            ).astype(BF16)


def fill_logits(q, item_refs, out_ref):
    top = None
    for b, item_ref in enumerate(item_refs):
        logits = dot(item_ref[...], q, NT) * (SCALE * LOG2E)
        out_ref[b] = logits
        high = jnp.max(logits, axis=0, keepdims=True)
        top = high if top is None else jnp.maximum(top, high)
    return top


def to_powers(ref, top, rate_ref, first):
    total = jnp.zeros(top.shape, F32)
    for b in range(ref.shape[0]):
        e = jnp.exp2(ref[b] - top) * spread(rate_ref[first + b], top.shape[1])
        ref[b] = e
        total += jnp.sum(e, axis=0, keepdims=True)
    return total


def diagonal(block):
    return lax.broadcasted_iota(jnp.int32, (block, block), 0) == lax.broadcasted_iota(
        jnp.int32, (block, block), 1
    )


def early_kernel(n, q_ref, *refs):
    item_refs, (e_ref, stats_ref) = refs[:n], refs[n:]
    top = fill_logits(q_ref[...], item_refs, e_ref)
    chosen = jnp.where(diagonal(q_ref.shape[0]), e_ref[0], 0.0)
    stats_ref[0:1] = top
    stats_ref[1:2] = jnp.sum(chosen, axis=0, keepdims=True)
    for b in range(n):
        e_ref[b] = jnp.exp2(e_ref[b] - top)


def rate_kernel(n, early, e_ref, near_ref, mate_ref, rate_ref, out_ref, total_ref):
    block = e_ref.shape[1]
    near = [near_ref[:, k * block : (k + 1) * block].astype(F32) for k in range(n // 2)]
    mate = [mate_ref[:, k * block : (k + 1) * block].astype(F32) for k in range(n // 2)]
    counts = [near[0], mate[0]] + near[1:] + mate[1:]
    total = jnp.zeros((1, block), F32)
    for b in range(n):
        rate = jnp.transpose(jnp.broadcast_to(1.0 / counts[b], (LANES, block)))
        rate_ref[b] = rate
        if b < early:
            e = e_ref[b] * spread(rate, block)
            out_ref[b] = e
            total += jnp.sum(e, axis=0, keepdims=True)
    total_ref[0:1] = total
    total_ref[1:2] = jnp.log(counts[0]) * LOG2E


def main_kernel(early, late, *refs):
    n = early + late
    q_ref, far_ref, item_refs, refs = refs[0], refs[1], refs[2 : 2 + n], refs[2 + n :]
    rate_ref, e_ref, stats_ref, total_ref, mine_out, mate_out, *refs = refs
    loss_ref, late_ref, factor_ref, far_e_ref = refs
    block = q_ref.shape[0]
    q, far = q_ref[...], far_ref[...]
    far_top = fill_logits(far, item_refs, far_e_ref)
    early_top, early_total = stats_ref[0:1], total_ref[0:1]
    top = jnp.maximum(fill_logits(q, item_refs[early:], late_ref), early_top)
    far_inverse = 1.0 / to_powers(far_e_ref, far_top, rate_ref, 0)
    shrink = jnp.exp2(early_top - top)
    total = to_powers(late_ref, top, rate_ref, early) + early_total * shrink
    inverse = 1.0 / total
    factor = shrink * inverse
    mate = dot((e_ref[1] * factor).astype(BF16), q)
    mate_out[...] = mate + dot((far_e_ref[1] * far_inverse).astype(BF16), far)
    weights = e_ref[0] * factor
    weights = jnp.where(diagonal(block), weights - 1.0, weights)
    mine = dot(weights.astype(BF16), q)
    mine_out[...] = mine + dot((far_e_ref[0] * far_inverse).astype(BF16), far)
    chosen = stats_ref[1:2] - total_ref[1:2]
    loss_ref[...] = ((top + jnp.log2(total) - chosen) * (1.0 / LOG2E))[0]
    factor_ref[0:1] = factor
    factor_ref[1:2] = inverse


def more_kernel(n, q_ref, *refs):
    item_refs, refs = refs[:n], refs[n:]
    rate_ref, mine_ref, mate_ref, mine_out, mate_out, e_ref = refs
    q = q_ref[...]
    inverse = 1.0 / to_powers(e_ref, fill_logits(q, item_refs, e_ref), rate_ref, 0)
    mate_out[...] = mate_ref[...] + dot((e_ref[1] * inverse).astype(BF16), q)
    mine_out[...] = mine_ref[...] + dot((e_ref[0] * inverse).astype(BF16), q)


def query_kernel(early, late, e_ref, late_ref, factor_ref, *refs):
    item_refs, out_ref = refs[:-1], refs[-1]
    total = None
    for b, item_ref in enumerate(item_refs):
        if b < early:
            weights = e_ref[b] * factor_ref[0:1]
        else:
            weights = late_ref[b - early] * factor_ref[1:2]
        if b == 0:
            weights = jnp.where(diagonal(weights.shape[0]), weights - 1.0, weights)
        part = dot(weights.astype(BF16), item_ref[...], TN)
        total = part if total is None else total + part
    out_ref[...] = total * SCALE


def split(x):
    high = x.astype(BF16)
    return jnp.concatenate([high, (x - high.astype(F32)).astype(BF16)], axis=1)


def give_kernel(pick_ref, mate_pick_ref, mine_ref, mate_ref, out_ref):
    half = pick_ref.shape[0] // 2
    for here, (pick, value) in enumerate(((pick_ref, mine_ref), (mate_pick_ref, mate_ref))):
        values = code(value[...] * SCALE).astype(BF16)
        out_ref[here * half : (here + 1) * half] = dot(pick[half:], values).astype(BF16)


def keep_kernel(pick_ref, mate_pick_ref, mine_ref, mate_ref, out_ref):
    half = pick_ref.shape[0] // 2
    for here, (pick, value) in enumerate(((pick_ref, mine_ref), (mate_pick_ref, mate_ref))):
        both = dot(pick[:half], split(value[...] * SCALE))
        out_ref[here * half : (here + 1) * half] = both[:, :D] + both[:, D:]


def pack_kernel(slots, keep_ref, given_ref, tail_ref, mate_tail_ref, *out_refs):
    half = keep_ref.shape[0] // 2
    tails = (tail_ref, mate_tail_ref)
    for p, out in enumerate(out_refs):
        for here in range(2):
            start = here * half + p * slots
            other = (1 - here) * half + p * slots
            given = decode(given_ref[other : other + slots].astype(F32))
            out[here, :slots] = code(keep_ref[start : start + slots] + given).astype(BF16)
            out[here, slots:] = tails[here][p]


def plain_pack_kernel(groups, slots, pick_ref, tail_ref, mine_ref, other_ref, out_ref):
    grad = code((mine_ref[...] + other_ref[...]) * SCALE).astype(BF16)
    picked = dot(pick_ref[...], grad).astype(BF16)
    for g in range(groups):
        out_ref[g, :slots] = picked[g * slots : (g + 1) * slots]
        out_ref[g, slots:] = tail_ref[g]


def unpack(slots, paired, got_refs, values_ref, ids_ref):
    packets = []
    for ref in got_refs:
        if len(ref.shape) == 2:
            packets.append(ref)
        else:
            packets += [ref.at[g] for g in range(1 if paired else ref.shape[0])]
    half = len(packets) * slots
    for g, got in enumerate(packets):
        tail = got[slots : slots + TAIL].astype(F32)
        ids = tail[:, :slots] * LANES + tail[:, LANES : LANES + slots]
        ids_ref[:, g * slots : (g + 1) * slots] = ids
        values = decode(got[:slots].astype(F32))
        high = values.astype(BF16)
        values_ref[g * slots : (g + 1) * slots] = high
        low = (values - high.astype(F32)).astype(BF16)
        values_ref[half + g * slots : half + (g + 1) * slots] = low


def scatter(values_ref, ids_ref, first, rows):
    index = lax.broadcasted_iota(jnp.int32, (rows, ids_ref.shape[1]), 0) + first
    put = (index.astype(F32) == ids_ref[:1]).astype(F32).astype(BF16)
    return dot(jnp.concatenate([put, put], axis=1), values_ref[...])


def first_kernel(slots, partial, *refs):
    inputs, (out_ref, values_ref, ids_ref) = refs[:-3], refs[-3:]
    unpack(slots, True, inputs[partial:], values_ref, ids_ref)
    sums = scatter(values_ref, ids_ref, 0, out_ref.shape[0])
    out_ref[...] = sums + inputs[0][...] if partial else sums


def update_kernel(slots, partial, *refs):
    inputs, refs = refs[:-8], refs[-8:]
    table_ref, accum_ref, table_out, accum_out, values_ref, ids_ref, new_ref, sems = refs
    unpack(slots, partial, inputs[1:] if partial else inputs, values_ref, ids_ref)
    chunks = sems.shape[1]
    rows = table_ref.shape[0] // chunks
    copies = []
    for c in range(chunks):
        here = slice(c * rows, (c + 1) * rows)
        grad = scatter(values_ref, ids_ref, c * rows, rows)
        if partial:
            grad += inputs[0][here]
        accum_new = accum_ref[here] + grad * grad
        new_ref[1, here] = accum_new
        copies.append(pltpu.make_async_copy(new_ref.at[1, here], accum_out.at[here], sems.at[1, c]))
        copies[-1].start()
        new_ref[0, here] = table_ref[here] - 0.1 * grad / (jnp.sqrt(accum_new) + 1e-08)
        copies.append(pltpu.make_async_copy(new_ref.at[0, here], table_out.at[here], sems.at[0, c]))
        copies[-1].start()
    for copy in copies:
        copy.wait()


def call(kernel, outs, *args, scratch=(), limit=16, flops=0):
    return pl.pallas_call(
        kernel,
        out_shape=[jax.ShapeDtypeStruct(s, t) for s, t in outs],
        scratch_shapes=list(scratch),
        compiler_params=pltpu.CompilerParams(vmem_limit_bytes=limit * MIB),
        cost_estimate=pl.CostEstimate(flops=flops, bytes_accessed=1024, transcendentals=0),
    )(*args)


def shards(queries, items, item_owner, item_offset, sample_counts, table, accum):
    block = queries.shape[0]
    n, groups = lax.axis_size("wide"), lax.axis_size("group")
    capacity = 2 * block // groups
    slots = -(-capacity // TAIL) * TAIL
    paired = groups == 2 * len(ROUNDS)

    def swap(x, k, axis="wide"):
        return lax.ppermute(x, axis, [(i, i ^ k) for i in range(lax.axis_size(axis))])

    far_counts = [swap(sample_counts, k) for k in range(2, n, 2)]
    far_items = [swap(items, k) for k in range(2, n, 2)]
    far_queries = [swap(queries, k) for k in range(2, n, 2)]

    owner = item_owner.reshape(1, block)
    if paired:
        partner = owner ^ lax.axis_index("group")
        owner = jnp.zeros_like(partner)
        for core in range(2):
            for k in range(len(ROUNDS)):
                place = core * len(ROUNDS) + k
                owner = jnp.where(partner == ROUNDS[k][core], place, owner)
        owner = owner ^ (lax.axis_index("wide") % 2 * len(ROUNDS))
    codes = owner * ROW_CODES + item_offset.reshape(1, block)

    def route(codes, flip, flops):
        return call(
            functools.partial(local_kernel, groups, slots, flip),
            [
                ((groups * slots, block), BF16),
                ((len(ROUNDS) if paired else groups, TAIL, D), BF16),
            ],
            codes,
            flops=flops,
        )

    pick, tail = route(codes, 0, 0)
    tails, own_items = [tail], items
    if paired:
        mate_codes, own_items = lax.optimization_barrier((swap(codes, 1), items))
        mate_pick, mate_tail = route(mate_codes, len(ROUNDS), 1 << 30)
        tails.append(mate_tail)
    far_items, far_counts, tails = lax.optimization_barrier((far_items, far_counts, tails))
    item_blocks = [items, swap(own_items, 1)] + far_items
    early = len(item_blocks)
    item_blocks += [swap(x, 1) for x in far_items]
    late = n - early
    near_counts = jnp.concatenate([sample_counts, *far_counts])
    mate_counts = swap(near_counts, 1)
    part = ((block, D), F32)
    square = (block, block)
    powers, stats = call(
        functools.partial(early_kernel, early),
        [((early, *square), F32), ((8, block), F32)],
        queries,
        *item_blocks[:early],
        limit=8 + 2 * n,
        flops=1 << 29,
    )
    rates, powers, totals = call(
        functools.partial(rate_kernel, n, early),
        [((n, block, LANES), F32), ((early, *square), F32), ((8, block), F32)],
        powers,
        near_counts.reshape(1, -1),
        mate_counts.reshape(1, -1),
        limit=8 + 4 * n,
    )
    mine, mate, loss, late_powers, factors = call(
        functools.partial(main_kernel, early, late),
        [part, part, ((block,), F32), ((late, *square), F32), ((8, block), F32)],
        queries,
        far_queries[0],
        *item_blocks,
        rates,
        powers,
        stats,
        totals,
        scratch=[pltpu.VMEM((n, *square), F32)],
        limit=8 + 4 * n,
    )
    for far in far_queries[1:]:
        mine, mate = call(
            functools.partial(more_kernel, n),
            [part, part],
            far,
            *item_blocks,
            rates,
            mine,
            mate,
            scratch=[pltpu.VMEM((n, *square), F32)],
            limit=8 + 4 * n,
        )
    if paired:
        parts = [((groups * slots, D), BF16)]
        (give,) = call(give_kernel, parts, pick, mate_pick, mine, mate)
        given = swap(give, 1)
        (query_grad,) = call(
            functools.partial(query_kernel, early, late),
            [part],
            powers,
            late_powers,
            factors,
            *item_blocks,
            limit=8 + 2 * n,
            flops=1 << 30,
        )
        given, query_grad = lax.optimization_barrier((given, query_grad))
        (keep,) = call(
            keep_kernel,
            [((groups * slots, D), F32)],
            pick,
            mate_pick,
            mine,
            mate,
            flops=1 << 29,
        )
        packed = call(
            functools.partial(pack_kernel, slots),
            [((2, slots + TAIL, D), BF16)] * len(ROUNDS),
            keep,
            given,
            *tails,
        )
        got = []
        for partners, packet in zip(ROUNDS, packed):
            pairs = [
                (w * groups + g, w * groups + (g ^ partners[w % 2]))
                for w in range(n)
                for g in range(groups)
            ]
            got.append(lax.ppermute(packet, ("wide", "group"), pairs))
        forwarded = [swap(x[1], 1) for x in got]
    else:
        (query_grad,) = call(
            functools.partial(query_kernel, early, late),
            [part],
            powers,
            late_powers,
            factors,
            *item_blocks,
            limit=8 + 2 * n,
            flops=1 << 30,
        )
        (packed,) = call(
            functools.partial(plain_pack_kernel, groups, slots),
            [((groups, slots + TAIL, D), BF16)],
            pick,
            *tails,
            mine,
            swap(mate, 1),
        )
        got = [lax.all_to_all(packed, "group", split_axis=0, concat_axis=0, tiled=True)]

    rows = table.shape[0]

    def scratch(packets):
        return [
            pltpu.VMEM((2 * packets * slots, D), BF16),
            pltpu.VMEM((TAIL, packets * slots), F32),
        ]

    before = []
    if paired:
        for pair in (got[:2], got[2:]):
            before = call(
                functools.partial(first_kernel, slots, len(before)),
                [((rows, D), F32)],
                *before,
                *pair,
                scratch=scratch(2),
                flops=1 << 28,
            )
        got = forwarded
    table_new, accum_new = pl.pallas_call(
        functools.partial(update_kernel, slots, paired),
        out_shape=[jax.ShapeDtypeStruct(table.shape, F32)] * 2,
        out_specs=[pl.BlockSpec(memory_space=pl.ANY)] * 2,
        scratch_shapes=[
            *scratch(len(got) if paired else groups),
            pltpu.VMEM((2, rows, D), F32),
            pltpu.SemaphoreType.DMA((2, 4)),
        ],
        compiler_params=pltpu.CompilerParams(vmem_limit_bytes=32 * MIB),
    )(*before, *got, table, accum)
    return (loss, query_grad, table_new, accum_new)


def solution(mesh):
    placed = (
        P(("wide", "group"), None),
        P(("wide", "group"), None),
        P(("wide", "group"), None),
        P(("wide", "group")),
        P(("wide", "group")),
        P(("wide", "group"), None),
        P(("wide", "group"), None),
    )
    return jax.shard_map(
        shards,
        mesh=mesh,
        in_specs=placed,
        out_specs=(
            P(("wide", "group")),
            P(("wide", "group"), None),
            P(("wide", "group"), None),
            P(("wide", "group"), None),
        ),
        check_vma=False,
    )
```

```python
import functools
import math

import jax
import jax.numpy as jnp
from jax import lax
from jax.experimental import pallas as pl
from jax.experimental.pallas import tpu as pltpu
from jax.sharding import PartitionSpec as P

D = 256
SCALE = 3.0 / math.sqrt(D)
LOG2E = math.log2(math.e)
LANES = 128
TAIL = 8
ROW_CODES = 1 << 16
MIB = 1 << 20
NT = (((1,), (1,)), ((), ()))
TN = (((0,), (0,)), ((), ()))
F32 = jnp.float32
BF16 = jnp.bfloat16


def dot(a, b, dims=(((1,), (0,)), ((), ()))):
    return lax.dot_general(a, b, dims, preferred_element_type=F32)


def spread(column, width):
    pieces = [column] * (width // LANES)
    if width % LANES:
        pieces.append(column[:, : width % LANES])
    return jnp.concatenate(pieces, axis=1)


def code(x):
    y = x * x
    return jnp.where(x < 0, -y, y) * y


def decode(u):
    root = lax.rsqrt(lax.rsqrt(jnp.abs(u)))
    return jnp.where(u < 0, -root, root)


def diagonal(block):
    return lax.broadcasted_iota(jnp.int32, (block, block), 0) == lax.broadcasted_iota(
        jnp.int32, (block, block), 1
    )


def local_kernel(groups, slots, code_ref, pick_ref, tail_ref):
    block = code_ref.shape[1]
    owner = code_ref[...] // ROW_CODES
    offset = code_ref[...] % ROW_CODES
    member = lax.broadcasted_iota(jnp.int32, (groups, block), 0) == owner
    before = lax.broadcasted_iota(jnp.int32, (block, block), 0) < lax.broadcasted_iota(
        jnp.int32, (block, block), 1
    )
    ranks = dot(member.astype(BF16), before.astype(BF16))
    rank = jnp.sum(jnp.where(member, ranks, 0.0), axis=0, keepdims=True).astype(jnp.int32)
    high = jnp.broadcast_to((offset // LANES).astype(F32), (TAIL, block)).astype(BF16)
    low = jnp.broadcast_to((offset % LANES).astype(F32), (TAIL, block)).astype(BF16)
    here = lax.broadcasted_iota(jnp.int32, (LANES, block), 0) == rank
    for g in range(groups):
        pick = (here & (owner == g)).astype(F32).astype(BF16)
        pick_ref[g * slots : (g + 1) * slots] = pick[:slots]
        tail_ref[g] = jnp.concatenate([dot(high, pick, NT), dot(low, pick, NT)], axis=1).astype(BF16)


def fill_logits(q, item_refs, out_ref):
    top = None
    for b, item_ref in enumerate(item_refs):
        logits = dot(item_ref[...], q, NT) * (SCALE * LOG2E)
        out_ref[b] = logits
        high = jnp.max(logits, axis=0, keepdims=True)
        top = high if top is None else jnp.maximum(top, high)
    return top


def to_powers(ref, top, rate_ref, first):
    total = jnp.zeros(top.shape, F32)
    for b in range(ref.shape[0]):
        e = jnp.exp2(ref[b] - top) * spread(rate_ref[first + b], top.shape[1])
        ref[b] = e
        total += jnp.sum(e, axis=0, keepdims=True)
    return total


def diagonal(block):
    return lax.broadcasted_iota(jnp.int32, (block, block), 0) == lax.broadcasted_iota(
        jnp.int32, (block, block), 1
    )


def early_kernel(n, q_ref, *refs):
    item_refs, (e_ref, stats_ref) = refs[:n], refs[n:]
    top = fill_logits(q_ref[...], item_refs, e_ref)
    chosen = jnp.where(diagonal(q_ref.shape[0]), e_ref[0], 0.0)
    stats_ref[0:1] = top
    stats_ref[1:2] = jnp.sum(chosen, axis=0, keepdims=True)
    for b in range(n):
        e_ref[b] = jnp.exp2(e_ref[b] - top)


def rate_kernel(n, early, e_ref, near_ref, mate_ref, rate_ref, out_ref, total_ref):
    block = e_ref.shape[1]
    near = [near_ref[:, k * block : (k + 1) * block].astype(F32) for k in range(n // 2)]
    mate = [mate_ref[:, k * block : (k + 1) * block].astype(F32) for k in range(n // 2)]
    counts = [near[0], mate[0]] + near[1:] + mate[1:]
    total = jnp.zeros((1, block), F32)
    for b in range(n):
        rate = jnp.transpose(jnp.broadcast_to(1.0 / counts[b], (LANES, block)))
        rate_ref[b] = rate
        if b < early:
            e = e_ref[b] * spread(rate, block)
            out_ref[b] = e
            total += jnp.sum(e, axis=0, keepdims=True)
    total_ref[0:1] = total
    total_ref[1:2] = jnp.log(counts[0]) * LOG2E


def main_kernel(early, late, *refs):
    n = early + late
    q_ref, far_ref, item_refs, refs = refs[0], refs[1], refs[2 : 2 + n], refs[2 + n :]
    rate_ref, e_ref, stats_ref, total_ref, mate_out, weights_ref, *refs = refs
    loss_ref, late_ref, factor_ref, far_e_ref = refs
    q, far = q_ref[...], far_ref[...]
    far_top = fill_logits(far, item_refs, far_e_ref)
    early_top, early_total = stats_ref[0:1], total_ref[0:1]
    top = jnp.maximum(fill_logits(q, item_refs[early:], late_ref), early_top)
    far_inverse = 1.0 / to_powers(far_e_ref, far_top, rate_ref, 0)
    shrink = jnp.exp2(early_top - top)
    total = to_powers(late_ref, top, rate_ref, early) + early_total * shrink
    inverse = 1.0 / total
    factor = shrink * inverse
    mate = dot((e_ref[1] * factor).astype(BF16), q)
    mate += dot((far_e_ref[1] * far_inverse).astype(BF16), far)
    mate_out[...] = code(mate * SCALE).astype(BF16) if mate_out.dtype == BF16 else mate
    weights_ref[...] = (far_e_ref[0] * far_inverse).astype(BF16)
    chosen = stats_ref[1:2] - total_ref[1:2]
    loss_ref[...] = ((top + jnp.log2(total) - chosen) * (1.0 / LOG2E))[0]
    factor_ref[0:1] = factor
    factor_ref[1:2] = inverse


def mine_kernel(e_ref, factor_ref, weights_ref, q_ref, far_ref, out_ref):
    weights = e_ref[0] * factor_ref[0:1]
    weights = jnp.where(diagonal(weights.shape[0]), weights - 1.0, weights)
    out_ref[...] = dot(weights.astype(BF16), q_ref[...]) + dot(weights_ref[...], far_ref[...])


def more_kernel(n, last, q_ref, *refs):
    item_refs, refs = refs[:n], refs[n:]
    rate_ref, mine_ref, mate_ref, mine_out, mate_out, e_ref = refs
    q = q_ref[...]
    inverse = 1.0 / to_powers(e_ref, fill_logits(q, item_refs, e_ref), rate_ref, 0)
    mate = mate_ref[...] + dot((e_ref[1] * inverse).astype(BF16), q)
    mate_out[...] = code(mate * SCALE).astype(BF16) if last else mate
    mine_out[...] = mine_ref[...] + dot((e_ref[0] * inverse).astype(BF16), q)


def transpose_kernel(*refs):
    for b, ref in enumerate(refs[:-1]):
        refs[-1][b] = jnp.transpose(ref[...])


def query_kernel(early, late, e_ref, late_ref, factor_ref, turned_ref, *refs):
    late_items, out_ref = refs[:-1], refs[-1]
    total = None
    for b in range(early + late):
        if b < early:
            weights, items = e_ref[b] * factor_ref[0:1], turned_ref[b]
        else:
            weights = late_ref[b - early] * factor_ref[1:2]
            items = jnp.transpose(late_items[b - early][...])
        if b == 0:
            weights = jnp.where(diagonal(weights.shape[0]), weights - 1.0, weights)
        part = dot(items, weights.astype(BF16))
        total = part if total is None else total + part
    out_ref[...] = jnp.transpose(total * SCALE)


def pack_kernel(groups, slots, pick_ref, tail_ref, mine_ref, other_ref, *out_refs):
    grad = mine_ref[...] * SCALE + decode(other_ref[...].astype(F32))
    grad = code(grad).astype(BF16)
    picked = dot(pick_ref[...], grad).astype(BF16)
    for g in range(groups):
        out = out_refs[g] if len(out_refs) == groups else out_refs[0].at[g]
        out[:slots] = picked[g * slots : (g + 1) * slots]
        out[slots:] = tail_ref[g]


def unpack(slots, got_refs, values_ref, ids_ref):
    packets = got_refs
    if len(got_refs[0].shape) == 3:
        packets = [got_refs[0].at[g] for g in range(got_refs[0].shape[0])]
    half = len(packets) * slots
    for g, got in enumerate(packets):
        tail = got[slots : slots + TAIL].astype(F32)
        ids = tail[:, :slots] * LANES + tail[:, LANES : LANES + slots]
        ids_ref[:, g * slots : (g + 1) * slots] = ids
        values = decode(got[:slots].astype(F32))
        high = values.astype(BF16)
        values_ref[g * slots : (g + 1) * slots] = high
        low = (values - high.astype(F32)).astype(BF16)
        values_ref[half + g * slots : half + (g + 1) * slots] = low


def scatter(values_ref, ids_ref, first, rows):
    index = lax.broadcasted_iota(jnp.int32, (rows, ids_ref.shape[1]), 0) + first
    put = (index.astype(F32) == ids_ref[:1]).astype(F32).astype(BF16)
    return dot(jnp.concatenate([put, put], axis=1), values_ref[...])


def first_kernel(slots, partial, *refs):
    inputs, (out_ref, values_ref, ids_ref) = refs[:-3], refs[-3:]
    unpack(slots, inputs[partial:], values_ref, ids_ref)
    sums = scatter(values_ref, ids_ref, 0, out_ref.shape[0])
    out_ref[...] = sums + inputs[0][...] if partial else sums


def update_kernel(slots, partial, *refs):
    inputs, refs = refs[:-8], refs[-8:]
    table_ref, accum_ref, table_out, accum_out, values_ref, ids_ref, new_ref, sems = refs
    unpack(slots, inputs[1:] if partial else inputs, values_ref, ids_ref)
    chunks = sems.shape[1]
    rows = table_ref.shape[0] // chunks
    copies = []
    for c in range(chunks):
        here = slice(c * rows, (c + 1) * rows)
        grad = scatter(values_ref, ids_ref, c * rows, rows)
        if partial:
            grad += inputs[0][here]
        accum_new = accum_ref[here] + grad * grad
        new_ref[1, here] = accum_new
        copies.append(pltpu.make_async_copy(new_ref.at[1, here], accum_out.at[here], sems.at[1, c]))
        copies[-1].start()
        new_ref[0, here] = table_ref[here] - 0.1 * grad / (jnp.sqrt(accum_new) + 1e-08)
        copies.append(pltpu.make_async_copy(new_ref.at[0, here], table_out.at[here], sems.at[0, c]))
        copies[-1].start()
    for copy in copies:
        copy.wait()


def call(kernel, outs, *args, scratch=(), limit=16, flops=0):
    return pl.pallas_call(
        kernel,
        out_shape=[jax.ShapeDtypeStruct(s, t) for s, t in outs],
        scratch_shapes=list(scratch),
        compiler_params=pltpu.CompilerParams(vmem_limit_bytes=limit * MIB),
        cost_estimate=pl.CostEstimate(flops=flops, bytes_accessed=1024, transcendentals=0),
    )(*args)


def shards(queries, items, item_owner, item_offset, sample_counts, table, accum):
    block = queries.shape[0]
    n, groups = lax.axis_size("wide"), lax.axis_size("group")
    capacity = 2 * block // groups
    slots = -(-capacity // TAIL) * TAIL
    paired = groups == 8

    def swap(x, k, axis="wide"):
        return lax.ppermute(x, axis, [(i, i ^ k) for i in range(lax.axis_size(axis))])

    far_counts = [swap(sample_counts, k) for k in range(2, n, 2)]
    far_items = [swap(items, k) for k in range(2, n, 2)]
    far_queries = [swap(queries, k) for k in range(2, n, 2)]

    owner = item_owner.reshape(1, block)
    if paired:
        owner = owner ^ lax.axis_index("group")
    pick, tail = call(
        functools.partial(local_kernel, groups, slots),
        [((groups * slots, block), BF16), ((groups, TAIL, D), BF16)],
        owner * ROW_CODES + item_offset.reshape(1, block),
        flops=1 << 30,
    )
    far_items, far_counts, tail = lax.optimization_barrier((far_items, far_counts, tail))
    item_blocks = [items, swap(items, 1)] + far_items
    early = len(item_blocks)
    item_blocks += [swap(x, 1) for x in far_items]
    late = n - early
    near_counts = jnp.concatenate([sample_counts, *far_counts])
    mate_counts = swap(near_counts, 1)
    part = ((block, D), F32)
    square = (block, block)
    powers, stats = call(
        functools.partial(early_kernel, early),
        [((early, *square), F32), ((8, block), F32)],
        queries,
        *item_blocks[:early],
        limit=8 + 2 * n,
        flops=1 << 29,
    )
    rates, powers, totals = call(
        functools.partial(rate_kernel, n, early),
        [((n, block, LANES), F32), ((early, *square), F32), ((8, block), F32)],
        powers,
        near_counts.reshape(1, -1),
        mate_counts.reshape(1, -1),
        limit=8 + 4 * n,
    )
    (turned,) = call(
        transpose_kernel, [((early, D, block), BF16)], *item_blocks[:early], limit=8 + n
    )
    far_queries[0], turned, rates = lax.optimization_barrier((far_queries[0], turned, rates))
    mate, weights, loss, late_powers, factors = call(
        functools.partial(main_kernel, early, late),
        [
            ((block, D), BF16 if len(far_queries) == 1 else F32),
            (square, BF16),
            ((block,), F32),
            ((late, *square), F32),
            ((8, block), F32),
        ],
        queries,
        far_queries[0],
        *item_blocks,
        rates,
        powers,
        stats,
        totals,
        scratch=[pltpu.VMEM((n, *square), F32)],
        limit=8 + 4 * n,
    )

    def sum_mine():
        return call(mine_kernel, [part], powers, factors, weights, queries, far_queries[0])[0]

    if len(far_queries) == 1:
        other = swap(mate, 1)
        mine = sum_mine()
    else:
        mine = sum_mine()
        for k, far in enumerate(far_queries[1:]):
            last = k == len(far_queries) - 2
            mine, mate = call(
                functools.partial(more_kernel, n, last),
                [part, ((block, D), BF16 if last else F32)],
                far,
                *item_blocks,
                rates,
                mine,
                mate,
                scratch=[pltpu.VMEM((n, *square), F32)],
                limit=8 + 4 * n,
            )
        other = swap(mate, 1)
    (query_grad,) = call(
        functools.partial(query_kernel, early, late),
        [part],
        powers,
        late_powers,
        factors,
        turned,
        *item_blocks[early:],
        limit=8 + 2 * n,
        flops=1 << 30,
    )
    other, query_grad = lax.optimization_barrier((other, query_grad))
    if paired:
        packets = [((slots + TAIL, D), BF16)] * groups
    else:
        packets = [((groups, slots + TAIL, D), BF16)]
    packed = call(
        functools.partial(pack_kernel, groups, slots), packets, pick, tail, mine, other
    )
    if paired:
        half = groups // 2
        far = sorted(range(half, groups), key=lambda k: (k % 2, k))
        order = far + sorted(range(1, half), key=lambda k: (1 - k % 2, -k))
        got = [packed[0]] + [swap(packed[k], k, "group") for k in order]
    else:
        got = [lax.all_to_all(packed[0], "group", split_axis=0, concat_axis=0, tiled=True)]
    rows = table.shape[0]

    def scratch(packets):
        return [
            pltpu.VMEM((2 * packets * slots, D), BF16),
            pltpu.VMEM((TAIL, packets * slots), F32),
        ]

    before = []
    if paired:
        for part_of in (got[:4], got[4:6]):
            before = call(
                functools.partial(first_kernel, slots, len(before)),
                [((rows, D), F32)],
                *before,
                *part_of,
                scratch=scratch(len(part_of)),
                flops=1 << 28,
            )
        got = got[6:]
    table_new, accum_new = pl.pallas_call(
        functools.partial(update_kernel, slots, paired),
        out_shape=[jax.ShapeDtypeStruct(table.shape, F32)] * 2,
        out_specs=[pl.BlockSpec(memory_space=pl.ANY)] * 2,
        scratch_shapes=[
            *scratch(len(got) if paired else groups),
            pltpu.VMEM((2, rows, D), F32),
            pltpu.SemaphoreType.DMA((2, 4)),
        ],
        compiler_params=pltpu.CompilerParams(vmem_limit_bytes=32 * MIB),
    )(*before, *got, table, accum)
    return (loss, query_grad, table_new, accum_new)


def solution(mesh):
    placed = (
        P(("wide", "group"), None),
        P(("wide", "group"), None),
        P(("wide", "group"), None),
        P(("wide", "group")),
        P(("wide", "group")),
        P(("wide", "group"), None),
        P(("wide", "group"), None),
    )
    return jax.shard_map(
        shards,
        mesh=mesh,
        in_specs=placed,
        out_specs=(
            P(("wide", "group")),
            P(("wide", "group"), None),
            P(("wide", "group"), None),
            P(("wide", "group"), None),
        ),
        check_vma=False,
    )
```

```python
import functools
import math

import jax
import jax.numpy as jnp
from jax import lax
from jax.experimental import pallas as pl
from jax.experimental.pallas import tpu as pltpu
from jax.sharding import PartitionSpec as P

D = 256
SCALE = 3.0 / math.sqrt(D)
LOG2E = math.log2(math.e)
LANES = 128
TAIL = 8
ROW_CODES = 1 << 16
MIB = 1 << 20
NT = (((1,), (1,)), ((), ()))
TN = (((0,), (0,)), ((), ()))
F32 = jnp.float32
BF16 = jnp.bfloat16


def dot(a, b, dims=(((1,), (0,)), ((), ()))):
    return lax.dot_general(a, b, dims, preferred_element_type=F32)


def spread(column, width):
    pieces = [column] * (width // LANES)
    if width % LANES:
        pieces.append(column[:, : width % LANES])
    return jnp.concatenate(pieces, axis=1)


def code(x):
    y = x * x
    return jnp.where(x < 0, -y, y) * y


def decode(u):
    root = lax.rsqrt(lax.rsqrt(jnp.abs(u)))
    return jnp.where(u < 0, -root, root)


def diagonal(block):
    return lax.broadcasted_iota(jnp.int32, (block, block), 0) == lax.broadcasted_iota(
        jnp.int32, (block, block), 1
    )


def local_kernel(groups, slots, code_ref, pick_ref, tail_ref):
    block = code_ref.shape[1]
    owner = code_ref[...] // ROW_CODES
    offset = code_ref[...] % ROW_CODES
    member = lax.broadcasted_iota(jnp.int32, (groups, block), 0) == owner
    before = lax.broadcasted_iota(jnp.int32, (block, block), 0) < lax.broadcasted_iota(
        jnp.int32, (block, block), 1
    )
    ranks = dot(member.astype(BF16), before.astype(BF16))
    rank = jnp.sum(jnp.where(member, ranks, 0.0), axis=0, keepdims=True).astype(jnp.int32)
    high = jnp.broadcast_to((offset // LANES).astype(F32), (TAIL, block)).astype(BF16)
    low = jnp.broadcast_to((offset % LANES).astype(F32), (TAIL, block)).astype(BF16)
    here = lax.broadcasted_iota(jnp.int32, (LANES, block), 0) == rank
    for g in range(groups):
        pick = (here & (owner == g)).astype(F32).astype(BF16)
        pick_ref[g * slots : (g + 1) * slots] = pick[:slots]
        tail_ref[g] = jnp.concatenate([dot(high, pick, NT), dot(low, pick, NT)], axis=1).astype(BF16)


def powers_of(q, item_ref, rate_ref=None):
    logits = dot(item_ref[...], q, NT) * (SCALE * LOG2E)
    top = jnp.max(logits, axis=0, keepdims=True)
    e = jnp.exp2(logits - top)
    return (e if rate_ref is None else e * spread(rate_ref[...], q.shape[0])), top, logits


def column_sum(x):
    return jnp.sum(x, axis=0, keepdims=True)


def join(tops, sums):
    top = functools.reduce(jnp.maximum, tops)
    shrinks = [jnp.exp2(t - top) for t in tops]
    total = sum(x * s for x, s in zip(sums, shrinks))
    inverse = 1.0 / total
    return top, total, [s * inverse for s in shrinks]


def diagonal(block):
    return lax.broadcasted_iota(jnp.int32, (block, block), 0) == lax.broadcasted_iota(
        jnp.int32, (block, block), 1
    )


def early_kernel(n, q_ref, *refs):
    item_refs, (e_ref, tops_ref) = refs[:n], refs[n:]
    q = q_ref[...]
    for b in range(n):
        e, tops_ref[b : b + 1], logits = powers_of(q, item_refs[b])
        e_ref[b] = e
        if b == 0:
            tops_ref[n : n + 1] = column_sum(jnp.where(diagonal(q.shape[0]), logits, 0.0))


def rate_kernel(n, early, e_ref, near_ref, mate_ref, rate_ref, out_ref, sums_ref):
    block = e_ref.shape[1]
    near = [near_ref[:, k * block : (k + 1) * block].astype(F32) for k in range(n // 2)]
    mate = [mate_ref[:, k * block : (k + 1) * block].astype(F32) for k in range(n // 2)]
    counts = [near[0], mate[0]] + near[1:] + mate[1:]
    for b in range(n):
        rate = jnp.transpose(jnp.broadcast_to(1.0 / counts[b], (LANES, block)))
        rate_ref[b] = rate
        if b < early:
            e = e_ref[b] * spread(rate, block)
            out_ref[b] = e
            sums_ref[b : b + 1] = column_sum(e)
    sums_ref[early : early + 1] = jnp.log(counts[0]) * LOG2E


def far_powers(n, q, item_refs, rate_ref, e_ref):
    tops, sums = [], []
    for b in range(n):
        e, top, _ = powers_of(q, item_refs[b], rate_ref.at[b])
        if b < 2:
            e_ref[b] = e
        tops.append(top)
        sums.append(column_sum(e))
    return join(tops, sums)[2]


def main_kernel(early, late, *refs):
    n = early + late
    q_ref, far_ref, item_refs, refs = refs[0], refs[1], refs[2 : 2 + n], refs[2 + n :]
    rate_ref, e_ref, tops_ref, sums_ref, mine_out, mate_out, *refs = refs
    loss_ref, late_ref, factor_ref, far_e_ref = refs
    q, far = q_ref[...], far_ref[...]
    tops = [tops_ref[b : b + 1] for b in range(early)]
    sums = [sums_ref[b : b + 1] for b in range(early)]
    for b in range(late):
        e, top, _ = powers_of(q, item_refs[early + b], rate_ref.at[early + b])
        late_ref[b] = e
        tops.append(top)
        sums.append(column_sum(e))
    top, total, factors = join(tops, sums)
    far_factors = far_powers(n, far, item_refs, rate_ref, far_e_ref)
    mate = dot((e_ref[1] * factors[1]).astype(BF16), q)
    mate += dot((far_e_ref[1] * far_factors[1]).astype(BF16), far)
    mate_out[...] = code(mate * SCALE).astype(BF16) if mate_out.dtype == BF16 else mate
    weights = e_ref[0] * factors[0]
    weights = jnp.where(diagonal(q.shape[0]), weights - 1.0, weights)
    mine = dot(weights.astype(BF16), q)
    mine_out[...] = mine + dot((far_e_ref[0] * far_factors[0]).astype(BF16), far)
    chosen = tops_ref[early : early + 1] - sums_ref[early : early + 1]
    loss_ref[...] = ((top + jnp.log2(total) - chosen) * (1.0 / LOG2E))[0]
    for b in range(n):
        factor_ref[b : b + 1] = factors[b]


def more_kernel(n, q_ref, *refs):
    item_refs, refs = refs[:n], refs[n:]
    rate_ref, mine_ref, mate_ref, mine_out, mate_out, e_ref = refs
    q = q_ref[...]
    factors = far_powers(n, q, item_refs, rate_ref, e_ref)
    mate = mate_ref[...] + dot((e_ref[1] * factors[1]).astype(BF16), q)
    mate_out[...] = code(mate * SCALE).astype(BF16) if mate_out.dtype == BF16 else mate
    mine_out[...] = mine_ref[...] + dot((e_ref[0] * factors[0]).astype(BF16), q)


def query_kernel(early, late, e_ref, late_ref, factor_ref, *refs):
    item_refs, out_ref = refs[:-1], refs[-1]
    total = None
    for b, item_ref in enumerate(item_refs):
        e = e_ref[b] if b < early else late_ref[b - early]
        weights = e * factor_ref[b : b + 1]
        if b == 0:
            weights = jnp.where(diagonal(weights.shape[0]), weights - 1.0, weights)
        part = dot(weights.astype(BF16), item_ref[...], TN)
        total = part if total is None else total + part
    out_ref[...] = total * SCALE


def pack_kernel(groups, slots, pick_ref, tail_ref, mine_ref, other_ref, *out_refs):
    grad = mine_ref[...] * SCALE + decode(other_ref[...].astype(F32))
    grad = code(grad).astype(BF16)
    picked = dot(pick_ref[...], grad).astype(BF16)
    for g in range(groups):
        out = out_refs[g] if len(out_refs) == groups else out_refs[0].at[g]
        out[:slots] = picked[g * slots : (g + 1) * slots]
        out[slots:] = tail_ref[g]


def unpack(slots, got_refs, values_ref, ids_ref):
    packets = got_refs
    if len(got_refs[0].shape) == 3:
        packets = [got_refs[0].at[g] for g in range(got_refs[0].shape[0])]
    half = len(packets) * slots
    for g, got in enumerate(packets):
        tail = got[slots : slots + TAIL].astype(F32)
        ids = tail[:, :slots] * LANES + tail[:, LANES : LANES + slots]
        ids_ref[:, g * slots : (g + 1) * slots] = ids
        values = decode(got[:slots].astype(F32))
        high = values.astype(BF16)
        values_ref[g * slots : (g + 1) * slots] = high
        low = (values - high.astype(F32)).astype(BF16)
        values_ref[half + g * slots : half + (g + 1) * slots] = low


def scatter(values_ref, ids_ref, first, rows):
    index = lax.broadcasted_iota(jnp.int32, (rows, ids_ref.shape[1]), 0) + first
    put = (index.astype(F32) == ids_ref[:1]).astype(F32).astype(BF16)
    return dot(jnp.concatenate([put, put], axis=1), values_ref[...])


def first_kernel(slots, *refs):
    got_refs, (out_ref, values_ref, ids_ref) = refs[:-3], refs[-3:]
    unpack(slots, got_refs, values_ref, ids_ref)
    out_ref[...] = scatter(values_ref, ids_ref, 0, out_ref.shape[0])


def update_kernel(slots, partial, *refs):
    inputs, refs = refs[:-8], refs[-8:]
    table_ref, accum_ref, table_out, accum_out, values_ref, ids_ref, new_ref, sems = refs
    unpack(slots, inputs[1:] if partial else inputs, values_ref, ids_ref)
    chunks = sems.shape[1]
    rows = table_ref.shape[0] // chunks
    copies = []
    for c in range(chunks):
        here = slice(c * rows, (c + 1) * rows)
        grad = scatter(values_ref, ids_ref, c * rows, rows)
        if partial:
            grad += inputs[0][here]
        accum_new = accum_ref[here] + grad * grad
        new_ref[1, here] = accum_new
        copies.append(pltpu.make_async_copy(new_ref.at[1, here], accum_out.at[here], sems.at[1, c]))
        copies[-1].start()
        new_ref[0, here] = table_ref[here] - 0.1 * grad / (jnp.sqrt(accum_new) + 1e-08)
        copies.append(pltpu.make_async_copy(new_ref.at[0, here], table_out.at[here], sems.at[0, c]))
        copies[-1].start()
    for copy in copies:
        copy.wait()


def call(kernel, outs, *args, scratch=(), limit=16, flops=0):
    return pl.pallas_call(
        kernel,
        out_shape=[jax.ShapeDtypeStruct(s, t) for s, t in outs],
        scratch_shapes=list(scratch),
        compiler_params=pltpu.CompilerParams(vmem_limit_bytes=limit * MIB),
        cost_estimate=pl.CostEstimate(flops=flops, bytes_accessed=1024, transcendentals=0),
    )(*args)


def shards(queries, items, item_owner, item_offset, sample_counts, table, accum):
    block = queries.shape[0]
    n, groups = lax.axis_size("wide"), lax.axis_size("group")
    capacity = 2 * block // groups
    slots = -(-capacity // TAIL) * TAIL
    paired = groups <= 8

    def swap(x, k, axis="wide"):
        return lax.ppermute(x, axis, [(i, i ^ k) for i in range(lax.axis_size(axis))])

    far_counts = [swap(sample_counts, k) for k in range(2, n, 2)]
    far_items = [swap(items, k) for k in range(2, n, 2)]
    far_queries = [swap(queries, k) for k in range(2, n, 2)]

    owner = item_owner.reshape(1, block)
    if paired:
        owner = owner ^ lax.axis_index("group")
    pick, tail = call(
        functools.partial(local_kernel, groups, slots),
        [((groups * slots, block), BF16), ((groups, TAIL, D), BF16)],
        owner * ROW_CODES + item_offset.reshape(1, block),
        flops=1 << 30,
    )
    far_items, far_counts, tail = lax.optimization_barrier((far_items, far_counts, tail))
    item_blocks = [items, swap(items, 1)] + far_items
    early = len(item_blocks)
    item_blocks += [swap(x, 1) for x in far_items]
    late = n - early
    near_counts = jnp.concatenate([sample_counts, *far_counts])
    mate_counts = swap(near_counts, 1)
    part = ((block, D), F32)
    square = (block, block)
    rows_of = ((-(-(n + 1) // TAIL) * TAIL, block), F32)
    sent = ((block, D), BF16)
    powers, stats = call(
        functools.partial(early_kernel, early),
        [((early, *square), F32), rows_of],
        queries,
        *item_blocks[:early],
        limit=8 + 2 * n,
        flops=1 << 29,
    )
    rates, powers, totals = call(
        functools.partial(rate_kernel, n, early),
        [((n, block, LANES), F32), ((early, *square), F32), rows_of],
        powers,
        near_counts.reshape(1, -1),
        mate_counts.reshape(1, -1),
        limit=8 + 4 * n,
    )
    mine, mate, loss, late_powers, factors = call(
        functools.partial(main_kernel, early, late),
        [
            part,
            part if far_queries[1:] else sent,
            ((block,), F32),
            ((late, *square), F32),
            rows_of,
        ],
        queries,
        far_queries[0],
        *item_blocks,
        rates,
        powers,
        stats,
        totals,
        scratch=[pltpu.VMEM((2, *square), F32)],
        limit=8 + 4 * n,
    )
    for k, far in enumerate(far_queries[1:], 2):
        mine, mate = call(
            functools.partial(more_kernel, n),
            [part, part if k < len(far_queries) else sent],
            far,
            *item_blocks,
            rates,
            mine,
            mate,
            scratch=[pltpu.VMEM((2, *square), F32)],
            limit=8 + 4 * n,
        )
    other = swap(mate, 1)
    (query_grad,) = call(
        functools.partial(query_kernel, early, late),
        [part],
        powers,
        late_powers,
        factors,
        *item_blocks,
        limit=8 + 2 * n,
        flops=1 << 30,
    )
    other, query_grad = lax.optimization_barrier((other, query_grad))
    if paired:
        packets = [((slots + TAIL, D), BF16)] * groups
    else:
        packets = [((groups, slots + TAIL, D), BF16)]
    packed = call(
        functools.partial(pack_kernel, groups, slots), packets, pick, tail, mine, other
    )
    if paired:
        half = groups // 2
        far = sorted(range(half, groups), key=lambda k: (k % 2, k))
        order = far + sorted(range(1, half), key=lambda k: (1 - k % 2, -k))
        got = [packed[0]] + [swap(packed[k], k, "group") for k in order]
    else:
        got = [lax.all_to_all(packed[0], "group", split_axis=0, concat_axis=0, tiled=True)]
    rows = table.shape[0]

    def scratch(packets):
        return [
            pltpu.VMEM((2 * packets * slots, D), BF16),
            pltpu.VMEM((TAIL, packets * slots), F32),
        ]

    count = groups // 2
    before = []
    if paired:
        before = call(
            functools.partial(first_kernel, slots),
            [((rows, D), F32)],
            *got[:count],
            scratch=scratch(count),
            flops=1 << 28,
        )
        got = got[count:]
    table_new, accum_new = pl.pallas_call(
        functools.partial(update_kernel, slots, paired),
        out_shape=[jax.ShapeDtypeStruct(table.shape, F32)] * 2,
        out_specs=[pl.BlockSpec(memory_space=pl.ANY)] * 2,
        scratch_shapes=[
            *scratch(len(got) if paired else groups),
            pltpu.VMEM((2, rows, D), F32),
            pltpu.SemaphoreType.DMA((2, 4)),
        ],
        compiler_params=pltpu.CompilerParams(vmem_limit_bytes=32 * MIB),
    )(*before, *got, table, accum)
    return (loss, query_grad, table_new, accum_new)


def solution(mesh):
    placed = (
        P(("wide", "group"), None),
        P(("wide", "group"), None),
        P(("wide", "group"), None),
        P(("wide", "group")),
        P(("wide", "group")),
        P(("wide", "group"), None),
        P(("wide", "group"), None),
    )
    return jax.shard_map(
        shards,
        mesh=mesh,
        in_specs=placed,
        out_specs=(
            P(("wide", "group")),
            P(("wide", "group"), None),
            P(("wide", "group"), None),
            P(("wide", "group"), None),
        ),
        check_vma=False,
    )
```

```python
import functools
import math

import jax
import jax.numpy as jnp
from jax import lax
from jax.experimental import pallas as pl
from jax.experimental.pallas import tpu as pltpu
from jax.sharding import PartitionSpec as P

D = 256
SCALE = 3.0 / math.sqrt(D)
LOG2E = math.log2(math.e)
LANES = 128
TAIL = 8
ROW_CODES = 1 << 16
MIB = 1 << 20
NT = (((1,), (1,)), ((), ()))
TN = (((0,), (0,)), ((), ()))
F32 = jnp.float32
BF16 = jnp.bfloat16


def dot(a, b, dims=(((1,), (0,)), ((), ()))):
    return lax.dot_general(a, b, dims, preferred_element_type=F32)


def spread(column, width):
    pieces = [column] * (width // LANES)
    if width % LANES:
        pieces.append(column[:, : width % LANES])
    return jnp.concatenate(pieces, axis=1)


def code(x):
    y = x * x
    return jnp.where(x < 0, -y, y) * y


def decode(u):
    root = lax.rsqrt(lax.rsqrt(jnp.abs(u)))
    return jnp.where(u < 0, -root, root)


def diagonal(block):
    return lax.broadcasted_iota(jnp.int32, (block, block), 0) == lax.broadcasted_iota(
        jnp.int32, (block, block), 1
    )


def local_kernel(groups, slots, code_ref, pick_ref, tail_ref):
    block = code_ref.shape[1]
    owner = code_ref[...] // ROW_CODES
    offset = code_ref[...] % ROW_CODES
    member = lax.broadcasted_iota(jnp.int32, (groups, block), 0) == owner
    before = lax.broadcasted_iota(jnp.int32, (block, block), 0) < lax.broadcasted_iota(
        jnp.int32, (block, block), 1
    )
    ranks = dot(member.astype(BF16), before.astype(BF16))
    rank = jnp.sum(jnp.where(member, ranks, 0.0), axis=0, keepdims=True).astype(jnp.int32)
    high = jnp.broadcast_to((offset // LANES).astype(F32), (TAIL, block)).astype(BF16)
    low = jnp.broadcast_to((offset % LANES).astype(F32), (TAIL, block)).astype(BF16)
    here = lax.broadcasted_iota(jnp.int32, (LANES, block), 0) == rank
    for g in range(groups):
        pick = (here & (owner == g)).astype(F32).astype(BF16)
        pick_ref[g * slots : (g + 1) * slots] = pick[:slots]
        tail_ref[g] = jnp.concatenate([dot(high, pick, NT), dot(low, pick, NT)], axis=1).astype(BF16)


def powers_of(q, item_ref, rate_ref=None):
    logits = dot(item_ref[...], q, NT) * (SCALE * LOG2E)
    top = jnp.max(logits, axis=0, keepdims=True)
    e = jnp.exp2(logits - top)
    return (e if rate_ref is None else e * spread(rate_ref[...], q.shape[0])), top, logits


def column_sum(x):
    return jnp.sum(x, axis=0, keepdims=True)


def join(tops, sums):
    top = functools.reduce(jnp.maximum, tops)
    shrinks = [jnp.exp2(t - top) for t in tops]
    total = sum(x * s for x, s in zip(sums, shrinks))
    inverse = 1.0 / total
    return top, total, [s * inverse for s in shrinks]


def diagonal(block):
    return lax.broadcasted_iota(jnp.int32, (block, block), 0) == lax.broadcasted_iota(
        jnp.int32, (block, block), 1
    )


def early_kernel(n, q_ref, *refs):
    item_refs, (e_ref, tops_ref) = refs[:n], refs[n:]
    q = q_ref[...]
    for b in range(n):
        e, tops_ref[b : b + 1], logits = powers_of(q, item_refs[b])
        e_ref[b] = e
        if b == 0:
            tops_ref[n : n + 1] = column_sum(jnp.where(diagonal(q.shape[0]), logits, 0.0))


def rate_kernel(n, early, e_ref, near_ref, mate_ref, rate_ref, out_ref, sums_ref):
    block = e_ref.shape[1]
    near = [near_ref[:, k * block : (k + 1) * block].astype(F32) for k in range(n // 2)]
    mate = [mate_ref[:, k * block : (k + 1) * block].astype(F32) for k in range(n // 2)]
    counts = [near[0], mate[0]] + near[1:] + mate[1:]
    for b in range(n):
        rate = jnp.transpose(jnp.broadcast_to(1.0 / counts[b], (LANES, block)))
        rate_ref[b] = rate
        if b < early:
            e = e_ref[b] * spread(rate, block)
            out_ref[b] = e
            sums_ref[b : b + 1] = column_sum(e)
    sums_ref[early : early + 1] = jnp.log(counts[0]) * LOG2E


def far_powers(n, q, item_refs, rate_ref, e_ref):
    tops, sums = [], []
    for b in range(n):
        e, top, _ = powers_of(q, item_refs[b], rate_ref.at[b])
        if b < 2:
            e_ref[b] = e
        tops.append(top)
        sums.append(column_sum(e))
    return join(tops, sums)[2]


def main_kernel(early, late, *refs):
    n = early + late
    q_ref, far_ref, item_refs, refs = refs[0], refs[1], refs[2 : 2 + n], refs[2 + n :]
    rate_ref, e_ref, tops_ref, sums_ref, mine_out, mate_out, *refs = refs
    late_ref, factor_ref, far_e_ref = refs
    q, far = q_ref[...], far_ref[...]
    tops = [tops_ref[b : b + 1] for b in range(early)]
    sums = [sums_ref[b : b + 1] for b in range(early)]
    for b in range(late):
        e, top, _ = powers_of(q, item_refs[early + b], rate_ref.at[early + b])
        late_ref[b] = e
        tops.append(top)
        sums.append(column_sum(e))
    top, total, factors = join(tops, sums)
    far_factors = far_powers(n, far, item_refs, rate_ref, far_e_ref)
    mate = dot((e_ref[1] * factors[1]).astype(BF16), q)
    mate += dot((far_e_ref[1] * far_factors[1]).astype(BF16), far)
    mate_out[...] = code(mate * SCALE).astype(BF16) if mate_out.dtype == BF16 else mate
    weights = e_ref[0] * factors[0]
    weights = jnp.where(diagonal(q.shape[0]), weights - 1.0, weights)
    mine = dot(weights.astype(BF16), q)
    mine_out[...] = mine + dot((far_e_ref[0] * far_factors[0]).astype(BF16), far)
    chosen = tops_ref[early : early + 1] - sums_ref[early : early + 1]
    factor_ref[n : n + 1] = (top + jnp.log2(total) - chosen) * (1.0 / LOG2E)
    for b in range(n):
        factor_ref[b : b + 1] = factors[b]


def more_kernel(n, q_ref, *refs):
    item_refs, refs = refs[:n], refs[n:]
    rate_ref, mine_ref, mate_ref, mine_out, mate_out, e_ref = refs
    q = q_ref[...]
    factors = far_powers(n, q, item_refs, rate_ref, e_ref)
    mate = mate_ref[...] + dot((e_ref[1] * factors[1]).astype(BF16), q)
    mate_out[...] = code(mate * SCALE).astype(BF16) if mate_out.dtype == BF16 else mate
    mine_out[...] = mine_ref[...] + dot((e_ref[0] * factors[0]).astype(BF16), q)


def query_kernel(early, late, e_ref, late_ref, factor_ref, *refs):
    item_refs, out_ref, loss_ref = refs[:-2], refs[-2], refs[-1]
    loss_ref[...] = factor_ref[early + late]
    total = None
    for b, item_ref in enumerate(item_refs):
        e = e_ref[b] if b < early else late_ref[b - early]
        weights = e * factor_ref[b : b + 1]
        if b == 0:
            weights = jnp.where(diagonal(weights.shape[0]), weights - 1.0, weights)
        part = dot(weights.astype(BF16), item_ref[...], TN)
        total = part if total is None else total + part
    out_ref[...] = total * SCALE


def pack_kernel(groups, slots, pick_ref, tail_ref, mine_ref, other_ref, *out_refs):
    grad = mine_ref[...] * SCALE + decode(other_ref[...].astype(F32))
    grad = code(grad).astype(BF16)
    picked = dot(pick_ref[...], grad).astype(BF16)
    for g in range(groups):
        out = out_refs[g] if len(out_refs) == groups else out_refs[0].at[g]
        out[:slots] = picked[g * slots : (g + 1) * slots]
        out[slots:] = tail_ref[g]


def unpack(slots, got_refs, values_ref, ids_ref):
    packets = got_refs
    if len(got_refs[0].shape) == 3:
        packets = [got_refs[0].at[g] for g in range(got_refs[0].shape[0])]
    half = len(packets) * slots
    for g, got in enumerate(packets):
        tail = got[slots : slots + TAIL].astype(F32)
        ids = tail[:, :slots] * LANES + tail[:, LANES : LANES + slots]
        ids_ref[:, g * slots : (g + 1) * slots] = ids
        values = decode(got[:slots].astype(F32))
        high = values.astype(BF16)
        values_ref[g * slots : (g + 1) * slots] = high
        low = (values - high.astype(F32)).astype(BF16)
        values_ref[half + g * slots : half + (g + 1) * slots] = low


def scatter(values_ref, ids_ref, first, rows):
    index = lax.broadcasted_iota(jnp.int32, (rows, ids_ref.shape[1]), 0) + first
    put = (index.astype(F32) == ids_ref[:1]).astype(F32).astype(BF16)
    return dot(jnp.concatenate([put, put], axis=1), values_ref[...])


def first_kernel(slots, *refs):
    got_refs, (out_ref, values_ref, ids_ref) = refs[:-3], refs[-3:]
    unpack(slots, got_refs, values_ref, ids_ref)
    out_ref[...] = scatter(values_ref, ids_ref, 0, out_ref.shape[0])


def update_kernel(slots, partial, *refs):
    inputs, refs = refs[:-8], refs[-8:]
    table_ref, accum_ref, table_out, accum_out, values_ref, ids_ref, new_ref, sems = refs
    unpack(slots, inputs[1:] if partial else inputs, values_ref, ids_ref)
    chunks = sems.shape[1]
    rows = table_ref.shape[0] // chunks
    copies = []
    for c in range(chunks):
        here = slice(c * rows, (c + 1) * rows)
        grad = scatter(values_ref, ids_ref, c * rows, rows)
        if partial:
            grad += inputs[0][here]
        accum_new = accum_ref[here] + grad * grad
        new_ref[1, here] = accum_new
        copies.append(pltpu.make_async_copy(new_ref.at[1, here], accum_out.at[here], sems.at[1, c]))
        copies[-1].start()
        new_ref[0, here] = table_ref[here] - 0.1 * grad / (jnp.sqrt(accum_new) + 1e-08)
        copies.append(pltpu.make_async_copy(new_ref.at[0, here], table_out.at[here], sems.at[0, c]))
        copies[-1].start()
    for copy in copies:
        copy.wait()


def call(kernel, outs, *args, scratch=(), limit=16, flops=0):
    return pl.pallas_call(
        kernel,
        out_shape=[jax.ShapeDtypeStruct(s, t) for s, t in outs],
        scratch_shapes=list(scratch),
        compiler_params=pltpu.CompilerParams(vmem_limit_bytes=limit * MIB),
        cost_estimate=pl.CostEstimate(flops=flops, bytes_accessed=1024, transcendentals=0),
    )(*args)


def shards(queries, items, item_owner, item_offset, sample_counts, table, accum):
    block = queries.shape[0]
    n, groups = lax.axis_size("wide"), lax.axis_size("group")
    capacity = 2 * block // groups
    slots = -(-capacity // TAIL) * TAIL
    paired = groups <= 8

    def swap(x, k, axis="wide"):
        return lax.ppermute(x, axis, [(i, i ^ k) for i in range(lax.axis_size(axis))])

    far_counts = [swap(sample_counts, k) for k in range(2, n, 2)]
    far_items = [swap(items, k) for k in range(2, n, 2)]
    far_queries = [swap(queries, k) for k in range(2, n, 2)]

    owner = item_owner.reshape(1, block)
    if paired:
        owner = owner ^ lax.axis_index("group")
    pick, tail = call(
        functools.partial(local_kernel, groups, slots),
        [((groups * slots, block), BF16), ((groups, TAIL, D), BF16)],
        owner * ROW_CODES + item_offset.reshape(1, block),
        flops=1 << 30,
    )
    far_items, far_counts, tail = lax.optimization_barrier((far_items, far_counts, tail))
    item_blocks = [items, swap(items, 1)] + far_items
    early = len(item_blocks)
    item_blocks += [swap(x, 1) for x in far_items]
    late = n - early
    near_counts = jnp.concatenate([sample_counts, *far_counts])
    mate_counts = swap(near_counts, 1)
    part = ((block, D), F32)
    square = (block, block)
    rows_of = ((-(-(n + 1) // TAIL) * TAIL, block), F32)
    sent = ((block, D), BF16)
    powers, stats = call(
        functools.partial(early_kernel, early),
        [((early, *square), F32), rows_of],
        queries,
        *item_blocks[:early],
        limit=8 + 2 * n,
        flops=1 << 29,
    )
    rates, powers, totals = call(
        functools.partial(rate_kernel, n, early),
        [((n, block, LANES), F32), ((early, *square), F32), rows_of],
        powers,
        near_counts.reshape(1, -1),
        mate_counts.reshape(1, -1),
        limit=8 + 4 * n,
    )
    mine, mate, late_powers, factors = call(
        functools.partial(main_kernel, early, late),
        [
            part,
            part if far_queries[1:] else sent,
            ((late, *square), F32),
            rows_of,
        ],
        queries,
        far_queries[0],
        *item_blocks,
        rates,
        powers,
        stats,
        totals,
        scratch=[pltpu.VMEM((2, *square), F32)],
        limit=8 + 4 * n,
    )
    for k, far in enumerate(far_queries[1:], 2):
        mine, mate = call(
            functools.partial(more_kernel, n),
            [part, part if k < len(far_queries) else sent],
            far,
            *item_blocks,
            rates,
            mine,
            mate,
            scratch=[pltpu.VMEM((2, *square), F32)],
            limit=8 + 4 * n,
        )
    other = swap(mate, 1)
    query_grad, loss = call(
        functools.partial(query_kernel, early, late),
        [part, ((block,), F32)],
        powers,
        late_powers,
        factors,
        *item_blocks,
        limit=8 + 2 * n,
        flops=1 << 30,
    )
    other, query_grad = lax.optimization_barrier((other, query_grad))
    if paired:
        packets = [((slots + TAIL, D), BF16)] * groups
    else:
        packets = [((groups, slots + TAIL, D), BF16)]
    packed = call(
        functools.partial(pack_kernel, groups, slots), packets, pick, tail, mine, other
    )
    if paired:
        half = groups // 2
        far = sorted(range(half, groups), key=lambda k: (k % 2, k))
        order = far + sorted(range(1, half), key=lambda k: (1 - k % 2, -k))
        got = [packed[0]] + [swap(packed[k], k, "group") for k in order]
    else:
        got = [lax.all_to_all(packed[0], "group", split_axis=0, concat_axis=0, tiled=True)]
    rows = table.shape[0]

    def scratch(packets):
        return [
            pltpu.VMEM((2 * packets * slots, D), BF16),
            pltpu.VMEM((TAIL, packets * slots), F32),
        ]

    count = groups // 2
    before = []
    if paired:
        before = call(
            functools.partial(first_kernel, slots),
            [((rows, D), F32)],
            *got[:count],
            scratch=scratch(count),
            flops=1 << 28,
        )
        got = got[count:]
    table_new, accum_new = pl.pallas_call(
        functools.partial(update_kernel, slots, paired),
        out_shape=[jax.ShapeDtypeStruct(table.shape, F32)] * 2,
        out_specs=[pl.BlockSpec(memory_space=pl.ANY)] * 2,
        scratch_shapes=[
            *scratch(len(got) if paired else groups),
            pltpu.VMEM((2, rows, D), F32),
            pltpu.SemaphoreType.DMA((2, 4)),
        ],
        compiler_params=pltpu.CompilerParams(vmem_limit_bytes=32 * MIB),
    )(*before, *got, table, accum)
    return (loss, query_grad, table_new, accum_new)


def solution(mesh):
    placed = (
        P(("wide", "group"), None),
        P(("wide", "group"), None),
        P(("wide", "group"), None),
        P(("wide", "group")),
        P(("wide", "group")),
        P(("wide", "group"), None),
        P(("wide", "group"), None),
    )
    return jax.shard_map(
        shards,
        mesh=mesh,
        in_specs=placed,
        out_specs=(
            P(("wide", "group")),
            P(("wide", "group"), None),
            P(("wide", "group"), None),
            P(("wide", "group"), None),
        ),
        check_vma=False,
    )
```

```python
import functools
import math

import jax
import jax.numpy as jnp
from jax import lax
from jax.experimental import pallas as pl
from jax.experimental.pallas import tpu as pltpu
from jax.sharding import PartitionSpec as P

D = 256
SCALE = 3.0 / math.sqrt(D)
LOG2E = math.log2(math.e)
LANES = 128
TAIL = 8
ROW_CODES = 1 << 16
MIB = 1 << 20
NT = (((1,), (1,)), ((), ()))
TN = (((0,), (0,)), ((), ()))
F32 = jnp.float32
BF16 = jnp.bfloat16


def dot(a, b, dims=(((1,), (0,)), ((), ()))):
    return lax.dot_general(a, b, dims, preferred_element_type=F32)


def spread(column, width):
    pieces = [column] * (width // LANES)
    if width % LANES:
        pieces.append(column[:, : width % LANES])
    return jnp.concatenate(pieces, axis=1)


def code(x):
    y = x * x
    return jnp.where(x < 0, -y, y) * y


def decode(u):
    root = lax.rsqrt(lax.rsqrt(jnp.abs(u)))
    return jnp.where(u < 0, -root, root)


def diagonal(block):
    return lax.broadcasted_iota(jnp.int32, (block, block), 0) == lax.broadcasted_iota(
        jnp.int32, (block, block), 1
    )


def local_kernel(groups, slots, code_ref, pick_ref, tail_ref):
    block = code_ref.shape[1]
    owner = code_ref[...] // ROW_CODES
    offset = code_ref[...] % ROW_CODES
    member = lax.broadcasted_iota(jnp.int32, (groups, block), 0) == owner
    before = lax.broadcasted_iota(jnp.int32, (block, block), 0) < lax.broadcasted_iota(
        jnp.int32, (block, block), 1
    )
    ranks = dot(member.astype(BF16), before.astype(BF16))
    rank = jnp.sum(jnp.where(member, ranks, 0.0), axis=0, keepdims=True).astype(jnp.int32)
    high = jnp.broadcast_to((offset // LANES).astype(F32), (TAIL, block)).astype(BF16)
    low = jnp.broadcast_to((offset % LANES).astype(F32), (TAIL, block)).astype(BF16)
    here = lax.broadcasted_iota(jnp.int32, (LANES, block), 0) == rank
    for g in range(groups):
        pick = (here & (owner == g)).astype(F32).astype(BF16)
        pick_ref[g * slots : (g + 1) * slots] = pick[:slots]
        tail_ref[g] = jnp.concatenate([dot(high, pick, NT), dot(low, pick, NT)], axis=1).astype(BF16)


def powers_of(q, item_ref, rate_ref=None):
    logits = dot(item_ref[...], q, NT) * (SCALE * LOG2E)
    top = jnp.max(logits, axis=0, keepdims=True)
    e = jnp.exp2(logits - top)
    return (e if rate_ref is None else e * spread(rate_ref[...], q.shape[0])), top, logits


def column_sum(x):
    return jnp.sum(x, axis=0, keepdims=True)


def join(tops, sums):
    top = functools.reduce(jnp.maximum, tops)
    shrinks = [jnp.exp2(t - top) for t in tops]
    total = sum(x * s for x, s in zip(sums, shrinks))
    inverse = 1.0 / total
    return top, total, [s * inverse for s in shrinks]


def diagonal(block):
    return lax.broadcasted_iota(jnp.int32, (block, block), 0) == lax.broadcasted_iota(
        jnp.int32, (block, block), 1
    )


def early_kernel(n, q_ref, *refs):
    item_refs, (e_ref, tops_ref) = refs[:n], refs[n:]
    q = q_ref[...]
    for b in range(n):
        e, tops_ref[b : b + 1], logits = powers_of(q, item_refs[b])
        e_ref[b] = e
        if b == 0:
            tops_ref[n : n + 1] = column_sum(jnp.where(diagonal(q.shape[0]), logits, 0.0))


def rate_kernel(n, early, e_ref, near_ref, mate_ref, rate_ref, out_ref, sums_ref):
    block = e_ref.shape[1]
    near = [near_ref[:, k * block : (k + 1) * block].astype(F32) for k in range(n // 2)]
    mate = [mate_ref[:, k * block : (k + 1) * block].astype(F32) for k in range(n // 2)]
    counts = [near[0], mate[0]] + near[1:] + mate[1:]
    for b in range(n):
        rate = jnp.transpose(jnp.broadcast_to(1.0 / counts[b], (LANES, block)))
        rate_ref[b] = rate
        if b < early:
            e = e_ref[b] * spread(rate, block)
            out_ref[b] = e
            sums_ref[b : b + 1] = column_sum(e)
    sums_ref[early : early + 1] = jnp.log(counts[0]) * LOG2E


def far_powers(n, q, item_refs, rate_ref, e_ref):
    tops, sums = [], []
    for b in range(n):
        e, top, _ = powers_of(q, item_refs[b], rate_ref.at[b])
        if b < 2:
            e_ref[b] = e
        tops.append(top)
        sums.append(column_sum(e))
    return join(tops, sums)[2]


def main_kernel(early, late, *refs):
    n = early + late
    q_ref, far_ref, item_refs, refs = refs[0], refs[1], refs[2 : 2 + n], refs[2 + n :]
    rate_ref, e_ref, tops_ref, sums_ref, weights_ref, mate_out, *refs = refs
    late_ref, factor_ref, far_e_ref = refs
    q, far = q_ref[...], far_ref[...]
    tops = [tops_ref[b : b + 1] for b in range(early)]
    sums = [sums_ref[b : b + 1] for b in range(early)]
    for b in range(late):
        e, top, _ = powers_of(q, item_refs[early + b], rate_ref.at[early + b])
        late_ref[b] = e
        tops.append(top)
        sums.append(column_sum(e))
    top, total, factors = join(tops, sums)
    far_factors = far_powers(n, far, item_refs, rate_ref, far_e_ref)
    mate = dot((e_ref[1] * factors[1]).astype(BF16), q)
    mate += dot((far_e_ref[1] * far_factors[1]).astype(BF16), far)
    mate_out[...] = code(mate * SCALE).astype(BF16) if mate_out.dtype == BF16 else mate
    weights_ref[...] = (far_e_ref[0] * far_factors[0]).astype(BF16)
    chosen = tops_ref[early : early + 1] - sums_ref[early : early + 1]
    factor_ref[n : n + 1] = (top + jnp.log2(total) - chosen) * (1.0 / LOG2E)
    for b in range(n):
        factor_ref[b : b + 1] = factors[b]


def mine_kernel(e_ref, factor_ref, weights_ref, q_ref, far_ref, out_ref):
    weights = e_ref[0] * factor_ref[0:1]
    weights = jnp.where(diagonal(weights.shape[0]), weights - 1.0, weights)
    out_ref[...] = dot(weights.astype(BF16), q_ref[...]) + dot(weights_ref[...], far_ref[...])


def more_kernel(n, q_ref, *refs):
    item_refs, refs = refs[:n], refs[n:]
    rate_ref, mine_ref, mate_ref, mine_out, mate_out, e_ref = refs
    q = q_ref[...]
    factors = far_powers(n, q, item_refs, rate_ref, e_ref)
    mate = mate_ref[...] + dot((e_ref[1] * factors[1]).astype(BF16), q)
    mate_out[...] = code(mate * SCALE).astype(BF16) if mate_out.dtype == BF16 else mate
    mine_out[...] = mine_ref[...] + dot((e_ref[0] * factors[0]).astype(BF16), q)


def query_kernel(early, late, e_ref, late_ref, factor_ref, *refs):
    item_refs, out_ref, loss_ref = refs[:-2], refs[-2], refs[-1]
    loss_ref[...] = factor_ref[early + late]
    total = None
    for b, item_ref in enumerate(item_refs):
        e = e_ref[b] if b < early else late_ref[b - early]
        weights = e * factor_ref[b : b + 1]
        if b == 0:
            weights = jnp.where(diagonal(weights.shape[0]), weights - 1.0, weights)
        part = dot(weights.astype(BF16), item_ref[...], TN)
        total = part if total is None else total + part
    out_ref[...] = total * SCALE


def pack_kernel(groups, slots, pick_ref, tail_ref, mine_ref, other_ref, *out_refs):
    grad = mine_ref[...] * SCALE + decode(other_ref[...].astype(F32))
    grad = code(grad).astype(BF16)
    picked = dot(pick_ref[...], grad).astype(BF16)
    for g in range(groups):
        out = out_refs[g] if len(out_refs) == groups else out_refs[0].at[g]
        out[:slots] = picked[g * slots : (g + 1) * slots]
        out[slots:] = tail_ref[g]


def unpack(slots, got_refs, values_ref, ids_ref):
    packets = got_refs
    if len(got_refs[0].shape) == 3:
        packets = [got_refs[0].at[g] for g in range(got_refs[0].shape[0])]
    half = len(packets) * slots
    for g, got in enumerate(packets):
        tail = got[slots : slots + TAIL].astype(F32)
        ids = tail[:, :slots] * LANES + tail[:, LANES : LANES + slots]
        ids_ref[:, g * slots : (g + 1) * slots] = ids
        values = decode(got[:slots].astype(F32))
        high = values.astype(BF16)
        values_ref[g * slots : (g + 1) * slots] = high
        low = (values - high.astype(F32)).astype(BF16)
        values_ref[half + g * slots : half + (g + 1) * slots] = low


def scatter(values_ref, ids_ref, first, rows):
    index = lax.broadcasted_iota(jnp.int32, (rows, ids_ref.shape[1]), 0) + first
    put = (index.astype(F32) == ids_ref[:1]).astype(F32).astype(BF16)
    return dot(jnp.concatenate([put, put], axis=1), values_ref[...])


def first_kernel(slots, *refs):
    got_refs, (out_ref, values_ref, ids_ref) = refs[:-3], refs[-3:]
    unpack(slots, got_refs, values_ref, ids_ref)
    out_ref[...] = scatter(values_ref, ids_ref, 0, out_ref.shape[0])


def update_kernel(slots, partial, *refs):
    inputs, refs = refs[:-8], refs[-8:]
    table_ref, accum_ref, table_out, accum_out, values_ref, ids_ref, new_ref, sems = refs
    unpack(slots, inputs[1:] if partial else inputs, values_ref, ids_ref)
    chunks = sems.shape[1]
    rows = table_ref.shape[0] // chunks
    copies = []
    for c in range(chunks):
        here = slice(c * rows, (c + 1) * rows)
        grad = scatter(values_ref, ids_ref, c * rows, rows)
        if partial:
            grad += inputs[0][here]
        accum_new = accum_ref[here] + grad * grad
        new_ref[1, here] = accum_new
        copies.append(pltpu.make_async_copy(new_ref.at[1, here], accum_out.at[here], sems.at[1, c]))
        copies[-1].start()
        new_ref[0, here] = table_ref[here] - 0.1 * grad / (accum_new * lax.rsqrt(accum_new) + 1e-08)
        copies.append(pltpu.make_async_copy(new_ref.at[0, here], table_out.at[here], sems.at[0, c]))
        copies[-1].start()
    for copy in copies:
        copy.wait()


def call(kernel, outs, *args, scratch=(), limit=16, flops=0):
    return pl.pallas_call(
        kernel,
        out_shape=[jax.ShapeDtypeStruct(s, t) for s, t in outs],
        scratch_shapes=list(scratch),
        compiler_params=pltpu.CompilerParams(vmem_limit_bytes=limit * MIB),
        cost_estimate=pl.CostEstimate(flops=flops, bytes_accessed=1024, transcendentals=0),
    )(*args)


def shards(queries, items, item_owner, item_offset, sample_counts, table, accum):
    block = queries.shape[0]
    n, groups = lax.axis_size("wide"), lax.axis_size("group")
    capacity = 2 * block // groups
    slots = -(-capacity // TAIL) * TAIL
    paired = groups <= 8

    def swap(x, k, axis="wide"):
        return lax.ppermute(x, axis, [(i, i ^ k) for i in range(lax.axis_size(axis))])

    far_counts = [swap(sample_counts, k) for k in range(2, n, 2)]
    far_items = [swap(items, k) for k in range(2, n, 2)]
    far_queries = [swap(queries, k) for k in range(2, n, 2)]

    owner = item_owner.reshape(1, block)
    if paired:
        owner = owner ^ lax.axis_index("group")
    pick, tail = call(
        functools.partial(local_kernel, groups, slots),
        [((groups * slots, block), BF16), ((groups, TAIL, D), BF16)],
        owner * ROW_CODES + item_offset.reshape(1, block),
        flops=1 << 30,
    )
    far_items, far_counts, tail = lax.optimization_barrier((far_items, far_counts, tail))
    item_blocks = [items, swap(items, 1)] + far_items
    early = len(item_blocks)
    item_blocks += [swap(x, 1) for x in far_items]
    late = n - early
    near_counts = jnp.concatenate([sample_counts, *far_counts])
    mate_counts = swap(near_counts, 1)
    part = ((block, D), F32)
    square = (block, block)
    rows_of = ((-(-(n + 1) // TAIL) * TAIL, block), F32)
    sent = ((block, D), BF16)
    powers, stats = call(
        functools.partial(early_kernel, early),
        [((early, *square), F32), rows_of],
        queries,
        *item_blocks[:early],
        limit=8 + 2 * n,
        flops=1 << 29,
    )
    rates, powers, totals = call(
        functools.partial(rate_kernel, n, early),
        [((n, block, LANES), F32), ((early, *square), F32), rows_of],
        powers,
        near_counts.reshape(1, -1),
        mate_counts.reshape(1, -1),
        limit=8 + 4 * n,
    )
    weights, mate, late_powers, factors = call(
        functools.partial(main_kernel, early, late),
        [
            (square, BF16),
            part if far_queries[1:] else sent,
            ((late, *square), F32),
            rows_of,
        ],
        queries,
        far_queries[0],
        *item_blocks,
        rates,
        powers,
        stats,
        totals,
        scratch=[pltpu.VMEM((2, *square), F32)],
        limit=8 + 4 * n,
    )
    (mine,) = call(
        mine_kernel, [part], powers, factors, weights, queries, far_queries[0], flops=1 << 28
    )
    for k, far in enumerate(far_queries[1:], 2):
        mine, mate = call(
            functools.partial(more_kernel, n),
            [part, part if k < len(far_queries) else sent],
            far,
            *item_blocks,
            rates,
            mine,
            mate,
            scratch=[pltpu.VMEM((2, *square), F32)],
            limit=8 + 4 * n,
        )
    other = swap(mate, 1)
    query_grad, loss = call(
        functools.partial(query_kernel, early, late),
        [part, ((block,), F32)],
        powers,
        late_powers,
        factors,
        *item_blocks,
        limit=8 + 2 * n,
        flops=1 << 30,
    )
    if paired:
        packets = [((slots + TAIL, D), BF16)] * groups
    else:
        packets = [((groups, slots + TAIL, D), BF16)]
    packed = call(
        functools.partial(pack_kernel, groups, slots), packets, pick, tail, mine, other
    )
    if paired:
        half = groups // 2
        far = sorted(range(half, groups), key=lambda k: (k % 2, k))
        order = far + sorted(range(1, half), key=lambda k: (1 - k % 2, -k))
        got = [packed[0]] + [swap(packed[k], k, "group") for k in order]
    else:
        got = [lax.all_to_all(packed[0], "group", split_axis=0, concat_axis=0, tiled=True)]
    rows = table.shape[0]

    def scratch(packets):
        return [
            pltpu.VMEM((2 * packets * slots, D), BF16),
            pltpu.VMEM((TAIL, packets * slots), F32),
        ]

    count = groups // 2
    before = []
    if paired:
        before = call(
            functools.partial(first_kernel, slots),
            [((rows, D), F32)],
            *got[:count],
            scratch=scratch(count),
            flops=1 << 28,
        )
        got = got[count:]
    table_new, accum_new = pl.pallas_call(
        functools.partial(update_kernel, slots, paired),
        out_shape=[jax.ShapeDtypeStruct(table.shape, F32)] * 2,
        out_specs=[pl.BlockSpec(memory_space=pl.ANY)] * 2,
        scratch_shapes=[
            *scratch(len(got) if paired else groups),
            pltpu.VMEM((2, rows, D), F32),
            pltpu.SemaphoreType.DMA((2, 4)),
        ],
        compiler_params=pltpu.CompilerParams(vmem_limit_bytes=32 * MIB),
    )(*before, *got, table, accum)
    return (loss, query_grad, table_new, accum_new)


def solution(mesh):
    placed = (
        P(("wide", "group"), None),
        P(("wide", "group"), None),
        P(("wide", "group"), None),
        P(("wide", "group")),
        P(("wide", "group")),
        P(("wide", "group"), None),
        P(("wide", "group"), None),
    )
    return jax.shard_map(
        shards,
        mesh=mesh,
        in_specs=placed,
        out_specs=(
            P(("wide", "group")),
            P(("wide", "group"), None),
            P(("wide", "group"), None),
            P(("wide", "group"), None),
        ),
        check_vma=False,
    )
```

```python
import functools
import math

import jax
import jax.numpy as jnp
from jax import lax
from jax.experimental import pallas as pl
from jax.experimental.pallas import tpu as pltpu
from jax.sharding import PartitionSpec as P

D = 256
SCALE = 3.0 / math.sqrt(D)
LOG2E = math.log2(math.e)
LANES = 128
TAIL = 8
ROW_CODES = 1 << 16
MIB = 1 << 20
NT = (((1,), (1,)), ((), ()))
TN = (((0,), (0,)), ((), ()))
F32 = jnp.float32
BF16 = jnp.bfloat16


def dot(a, b, dims=(((1,), (0,)), ((), ()))):
    return lax.dot_general(a, b, dims, preferred_element_type=F32)


def spread(column, width):
    pieces = [column] * (width // LANES)
    if width % LANES:
        pieces.append(column[:, : width % LANES])
    return jnp.concatenate(pieces, axis=1)


def code(x):
    y = x * x
    return jnp.where(x < 0, -y, y) * y


def decode(u):
    root = lax.rsqrt(lax.rsqrt(jnp.abs(u)))
    return jnp.where(u < 0, -root, root)


def diagonal(block):
    return lax.broadcasted_iota(jnp.int32, (block, block), 0) == lax.broadcasted_iota(
        jnp.int32, (block, block), 1
    )


def local_kernel(groups, slots, code_ref, pick_ref, tail_ref):
    block = code_ref.shape[1]
    owner = code_ref[...] // ROW_CODES
    offset = code_ref[...] % ROW_CODES
    member = lax.broadcasted_iota(jnp.int32, (groups, block), 0) == owner
    before = lax.broadcasted_iota(jnp.int32, (block, block), 0) < lax.broadcasted_iota(
        jnp.int32, (block, block), 1
    )
    ranks = dot(member.astype(BF16), before.astype(BF16))
    rank = jnp.sum(jnp.where(member, ranks, 0.0), axis=0, keepdims=True).astype(jnp.int32)
    high = jnp.broadcast_to((offset // LANES).astype(F32), (TAIL, block)).astype(BF16)
    low = jnp.broadcast_to((offset % LANES).astype(F32), (TAIL, block)).astype(BF16)
    here = lax.broadcasted_iota(jnp.int32, (LANES, block), 0) == rank
    for g in range(groups):
        pick = (here & (owner == g)).astype(F32).astype(BF16)
        pick_ref[g * slots : (g + 1) * slots] = pick[:slots]
        tail_ref[g] = jnp.concatenate([dot(high, pick, NT), dot(low, pick, NT)], axis=1).astype(BF16)


def powers_of(q, item_ref, rate_ref=None):
    logits = dot(item_ref[...], q, NT) * (SCALE * LOG2E)
    top = jnp.max(logits, axis=0, keepdims=True)
    e = jnp.exp2(logits - top)
    return (e if rate_ref is None else e * spread(rate_ref[...], q.shape[0])), top, logits


def column_sum(x):
    return jnp.sum(x, axis=0, keepdims=True)


def join(tops, sums):
    top = functools.reduce(jnp.maximum, tops)
    shrinks = [jnp.exp2(t - top) for t in tops]
    total = sum(x * s for x, s in zip(sums, shrinks))
    inverse = 1.0 / total
    return top, total, [s * inverse for s in shrinks]


def diagonal(block):
    return lax.broadcasted_iota(jnp.int32, (block, block), 0) == lax.broadcasted_iota(
        jnp.int32, (block, block), 1
    )


def early_kernel(n, q_ref, *refs):
    item_refs, (e_ref, tops_ref) = refs[:n], refs[n:]
    q = q_ref[...]
    for b in range(n):
        e, tops_ref[b : b + 1], logits = powers_of(q, item_refs[b])
        e_ref[b] = e
        if b == 0:
            tops_ref[n : n + 1] = column_sum(jnp.where(diagonal(q.shape[0]), logits, 0.0))


def rate_kernel(n, early, e_ref, near_ref, mate_ref, rate_ref, out_ref, sums_ref):
    block = e_ref.shape[1]
    near = [near_ref[:, k * block : (k + 1) * block].astype(F32) for k in range(n // 2)]
    mate = [mate_ref[:, k * block : (k + 1) * block].astype(F32) for k in range(n // 2)]
    counts = [near[0], mate[0]] + near[1:] + mate[1:]
    for b in range(n):
        rate = jnp.transpose(jnp.broadcast_to(1.0 / counts[b], (LANES, block)))
        rate_ref[b] = rate
        if b < early:
            e = e_ref[b] * spread(rate, block)
            out_ref[b] = e
            sums_ref[b : b + 1] = column_sum(e)
    sums_ref[early : early + 1] = jnp.log(counts[0]) * LOG2E


def far_powers(n, q, item_refs, rate_ref, e_ref):
    tops, sums = [], []
    for b in range(n):
        e, top, _ = powers_of(q, item_refs[b], rate_ref.at[b])
        if b < 2:
            e_ref[b] = e
        tops.append(top)
        sums.append(column_sum(e))
    return join(tops, sums)[2]


def main_kernel(early, late, *refs):
    n = early + late
    q_ref, far_ref, item_refs, refs = refs[0], refs[1], refs[2 : 2 + n], refs[2 + n :]
    rate_ref, e_ref, tops_ref, sums_ref, mine_out, mate_out, *refs = refs
    late_ref, factor_ref, far_e_ref = refs
    q, far = q_ref[...], far_ref[...]
    tops = [tops_ref[b : b + 1] for b in range(early)]
    sums = [sums_ref[b : b + 1] for b in range(early)]
    for b in range(late):
        e, top, _ = powers_of(q, item_refs[early + b], rate_ref.at[early + b])
        late_ref[b] = e
        tops.append(top)
        sums.append(column_sum(e))
    top, total, factors = join(tops, sums)
    far_factors = far_powers(n, far, item_refs, rate_ref, far_e_ref)
    mate = dot((e_ref[1] * factors[1]).astype(BF16), q)
    mate += dot((far_e_ref[1] * far_factors[1]).astype(BF16), far)
    mate_out[...] = code(mate * SCALE).astype(BF16) if mate_out.dtype == BF16 else mate
    weights = e_ref[0] * factors[0]
    weights = jnp.where(diagonal(q.shape[0]), weights - 1.0, weights)
    mine = dot(weights.astype(BF16), q)
    mine_out[...] = mine + dot((far_e_ref[0] * far_factors[0]).astype(BF16), far)
    chosen = tops_ref[early : early + 1] - sums_ref[early : early + 1]
    factor_ref[n : n + 1] = (top + jnp.log2(total) - chosen) * (1.0 / LOG2E)
    for b in range(n):
        factor_ref[b : b + 1] = factors[b]


def more_kernel(n, q_ref, *refs):
    item_refs, refs = refs[:n], refs[n:]
    rate_ref, mine_ref, mate_ref, mine_out, mate_out, e_ref = refs
    q = q_ref[...]
    factors = far_powers(n, q, item_refs, rate_ref, e_ref)
    mate = mate_ref[...] + dot((e_ref[1] * factors[1]).astype(BF16), q)
    mate_out[...] = code(mate * SCALE).astype(BF16) if mate_out.dtype == BF16 else mate
    mine_out[...] = mine_ref[...] + dot((e_ref[0] * factors[0]).astype(BF16), q)


def query_kernel(early, late, e_ref, late_ref, factor_ref, *refs):
    item_refs, out_ref, loss_ref = refs[:-2], refs[-2], refs[-1]
    loss_ref[...] = factor_ref[early + late]
    total = None
    for b, item_ref in enumerate(item_refs):
        e = e_ref[b] if b < early else late_ref[b - early]
        weights = e * factor_ref[b : b + 1]
        if b == 0:
            weights = jnp.where(diagonal(weights.shape[0]), weights - 1.0, weights)
        part = dot(weights.astype(BF16), item_ref[...], TN)
        total = part if total is None else total + part
    out_ref[...] = total * SCALE


def pack_kernel(groups, slots, pick_ref, tail_ref, mine_ref, other_ref, *out_refs):
    grad = mine_ref[...] * SCALE + decode(other_ref[...].astype(F32))
    grad = code(grad).astype(BF16)
    picked = dot(pick_ref[...], grad).astype(BF16)
    for g in range(groups):
        out = out_refs[g] if len(out_refs) == groups else out_refs[0].at[g]
        out[:slots] = picked[g * slots : (g + 1) * slots]
        out[slots:] = tail_ref[g]


def unpack(slots, got_refs, values_ref, ids_ref):
    packets = got_refs
    if len(got_refs[0].shape) == 3:
        packets = [got_refs[0].at[g] for g in range(got_refs[0].shape[0])]
    half = len(packets) * slots
    for g, got in enumerate(packets):
        tail = got[slots : slots + TAIL].astype(F32)
        ids = tail[:, :slots] * LANES + tail[:, LANES : LANES + slots]
        ids_ref[:, g * slots : (g + 1) * slots] = ids
        values = decode(got[:slots].astype(F32))
        high = values.astype(BF16)
        values_ref[g * slots : (g + 1) * slots] = high
        low = (values - high.astype(F32)).astype(BF16)
        values_ref[half + g * slots : half + (g + 1) * slots] = low


def scatter(values_ref, ids_ref, first, rows):
    index = lax.broadcasted_iota(jnp.int32, (rows, ids_ref.shape[1]), 0) + first
    put = (index.astype(F32) == ids_ref[:1]).astype(F32).astype(BF16)
    return dot(jnp.concatenate([put, put], axis=1), values_ref[...])


def first_kernel(slots, *refs):
    got_refs, (out_ref, values_ref, ids_ref) = refs[:-3], refs[-3:]
    unpack(slots, got_refs, values_ref, ids_ref)
    out_ref[...] = scatter(values_ref, ids_ref, 0, out_ref.shape[0])


def update_kernel(slots, partial, *refs):
    inputs, refs = refs[:-8], refs[-8:]
    table_ref, accum_ref, table_out, accum_out, values_ref, ids_ref, new_ref, sems = refs
    unpack(slots, inputs[1:] if partial else inputs, values_ref, ids_ref)
    chunks = sems.shape[1]
    rows = table_ref.shape[0] // chunks
    copies = []
    for c in range(chunks):
        here = slice(c * rows, (c + 1) * rows)
        grad = scatter(values_ref, ids_ref, c * rows, rows)
        if partial:
            grad += inputs[0][here]
        accum_new = accum_ref[here] + grad * grad
        new_ref[1, here] = accum_new
        copies.append(pltpu.make_async_copy(new_ref.at[1, here], accum_out.at[here], sems.at[1, c]))
        copies[-1].start()
        new_ref[0, here] = table_ref[here] - 0.1 * grad / (accum_new * lax.rsqrt(accum_new) + 1e-08)
        copies.append(pltpu.make_async_copy(new_ref.at[0, here], table_out.at[here], sems.at[0, c]))
        copies[-1].start()
    for copy in copies:
        copy.wait()


def call(kernel, outs, *args, scratch=(), limit=16, flops=0):
    return pl.pallas_call(
        kernel,
        out_shape=[jax.ShapeDtypeStruct(s, t) for s, t in outs],
        scratch_shapes=list(scratch),
        compiler_params=pltpu.CompilerParams(vmem_limit_bytes=limit * MIB),
        cost_estimate=pl.CostEstimate(flops=flops, bytes_accessed=1024, transcendentals=0),
    )(*args)


def shards(queries, items, item_owner, item_offset, sample_counts, table, accum):
    block = queries.shape[0]
    n, groups = lax.axis_size("wide"), lax.axis_size("group")
    capacity = 2 * block // groups
    slots = -(-capacity // TAIL) * TAIL
    paired = groups <= 8

    def swap(x, k, axis="wide"):
        return lax.ppermute(x, axis, [(i, i ^ k) for i in range(lax.axis_size(axis))])

    far_counts = [swap(sample_counts, k) for k in range(2, n, 2)]
    far_items = [swap(items, k) for k in range(2, n, 2)]
    far_queries = [swap(queries, k) for k in range(2, n, 2)]

    owner = item_owner.reshape(1, block)
    if paired:
        owner = owner ^ lax.axis_index("group")
    codes = owner * ROW_CODES + item_offset.reshape(1, block)
    codes, own_items = lax.optimization_barrier((codes, items))
    pick, tail = call(
        functools.partial(local_kernel, groups, slots),
        [((groups * slots, block), BF16), ((groups, TAIL, D), BF16)],
        codes,
        flops=1 << 30,
    )
    far_items, far_counts, tail = lax.optimization_barrier((far_items, far_counts, tail))
    item_blocks = [items, swap(own_items, 1)] + far_items
    early = len(item_blocks)
    item_blocks += [swap(x, 1) for x in far_items]
    late = n - early
    near_counts = jnp.concatenate([sample_counts, *far_counts])
    mate_counts = swap(near_counts, 1)
    part = ((block, D), F32)
    square = (block, block)
    rows_of = ((-(-(n + 1) // TAIL) * TAIL, block), F32)
    sent = ((block, D), BF16)
    powers, stats = call(
        functools.partial(early_kernel, early),
        [((early, *square), F32), rows_of],
        queries,
        *item_blocks[:early],
        limit=8 + 2 * n,
        flops=1 << 29,
    )
    rates, powers, totals = call(
        functools.partial(rate_kernel, n, early),
        [((n, block, LANES), F32), ((early, *square), F32), rows_of],
        powers,
        near_counts.reshape(1, -1),
        mate_counts.reshape(1, -1),
        limit=8 + 4 * n,
    )
    mine, mate, late_powers, factors = call(
        functools.partial(main_kernel, early, late),
        [
            part,
            part if far_queries[1:] else sent,
            ((late, *square), F32),
            rows_of,
        ],
        queries,
        far_queries[0],
        *item_blocks,
        rates,
        powers,
        stats,
        totals,
        scratch=[pltpu.VMEM((2, *square), F32)],
        limit=8 + 4 * n,
    )
    for k, far in enumerate(far_queries[1:], 2):
        mine, mate = call(
            functools.partial(more_kernel, n),
            [part, part if k < len(far_queries) else sent],
            far,
            *item_blocks,
            rates,
            mine,
            mate,
            scratch=[pltpu.VMEM((2, *square), F32)],
            limit=8 + 4 * n,
        )
    other = swap(mate, 1)
    query_grad, loss = call(
        functools.partial(query_kernel, early, late),
        [part, ((block,), F32)],
        powers,
        late_powers,
        factors,
        *item_blocks,
        limit=8 + 2 * n,
        flops=1 << 30,
    )
    other, query_grad = lax.optimization_barrier((other, query_grad))
    if paired:
        packets = [((slots + TAIL, D), BF16)] * groups
    else:
        packets = [((groups, slots + TAIL, D), BF16)]
    packed = call(
        functools.partial(pack_kernel, groups, slots), packets, pick, tail, mine, other
    )
    if paired:
        half = groups // 2
        far = sorted(range(half, groups), key=lambda k: (k % 2, k))
        order = far + sorted(range(1, half), key=lambda k: (1 - k % 2, -k))
        got = [packed[0]] + [swap(packed[k], k, "group") for k in order]
    else:
        got = [lax.all_to_all(packed[0], "group", split_axis=0, concat_axis=0, tiled=True)]
    rows = table.shape[0]

    def scratch(packets):
        return [
            pltpu.VMEM((2 * packets * slots, D), BF16),
            pltpu.VMEM((TAIL, packets * slots), F32),
        ]

    count = groups // 2
    before = []
    if paired:
        before = call(
            functools.partial(first_kernel, slots),
            [((rows, D), F32)],
            *got[:count],
            scratch=scratch(count),
            flops=1 << 28,
        )
        got = got[count:]
    table_new, accum_new = pl.pallas_call(
        functools.partial(update_kernel, slots, paired),
        out_shape=[jax.ShapeDtypeStruct(table.shape, F32)] * 2,
        out_specs=[pl.BlockSpec(memory_space=pl.ANY)] * 2,
        scratch_shapes=[
            *scratch(len(got) if paired else groups),
            pltpu.VMEM((2, rows, D), F32),
            pltpu.SemaphoreType.DMA((2, 4)),
        ],
        compiler_params=pltpu.CompilerParams(vmem_limit_bytes=32 * MIB),
    )(*before, *got, table, accum)
    return (loss, query_grad, table_new, accum_new)


def solution(mesh):
    placed = (
        P(("wide", "group"), None),
        P(("wide", "group"), None),
        P(("wide", "group"), None),
        P(("wide", "group")),
        P(("wide", "group")),
        P(("wide", "group"), None),
        P(("wide", "group"), None),
    )
    return jax.shard_map(
        shards,
        mesh=mesh,
        in_specs=placed,
        out_specs=(
            P(("wide", "group")),
            P(("wide", "group"), None),
            P(("wide", "group"), None),
            P(("wide", "group"), None),
        ),
        check_vma=False,
    )
```

```python
import functools
import math

import jax
import jax.numpy as jnp
from jax import lax
from jax.experimental import pallas as pl
from jax.experimental.pallas import tpu as pltpu
from jax.sharding import PartitionSpec as P

D = 256
SCALE = 3.0 / math.sqrt(D)
LOG2E = math.log2(math.e)
LANES = 128
TAIL = 8
ROW_CODES = 1 << 16
FAR = ((4, 5), (6, 7))
NEAR = (0, 3, 1, 2)
MIB = 1 << 20
NT = (((1,), (1,)), ((), ()))
TN = (((0,), (0,)), ((), ()))
F32 = jnp.float32
BF16 = jnp.bfloat16


def dot(a, b, dims=(((1,), (0,)), ((), ()))):
    return lax.dot_general(a, b, dims, preferred_element_type=F32)


def spread(column, width):
    pieces = [column] * (width // LANES)
    if width % LANES:
        pieces.append(column[:, : width % LANES])
    return jnp.concatenate(pieces, axis=1)


def code(x):
    y = x * x
    return jnp.where(x < 0, -y, y) * y


def decode(u):
    root = lax.rsqrt(lax.rsqrt(jnp.abs(u)))
    return jnp.where(u < 0, -root, root)


def diagonal(block):
    return lax.broadcasted_iota(jnp.int32, (block, block), 0) == lax.broadcasted_iota(
        jnp.int32, (block, block), 1
    )


def local_kernel(groups, slots, flip, code_ref, pick_ref, tail_ref):
    block = code_ref.shape[1]
    owner = code_ref[...] // ROW_CODES
    owner = jnp.where(owner < groups // 2, owner ^ flip, owner)
    offset = code_ref[...] % ROW_CODES
    member = lax.broadcasted_iota(jnp.int32, (groups, block), 0) == owner
    before = lax.broadcasted_iota(jnp.int32, (block, block), 0) < lax.broadcasted_iota(
        jnp.int32, (block, block), 1
    )
    ranks = dot(member.astype(BF16), before.astype(BF16))
    rank = jnp.sum(jnp.where(member, ranks, 0.0), axis=0, keepdims=True).astype(jnp.int32)
    high = jnp.broadcast_to((offset // LANES).astype(F32), (TAIL, block)).astype(BF16)
    low = jnp.broadcast_to((offset % LANES).astype(F32), (TAIL, block)).astype(BF16)
    here = lax.broadcasted_iota(jnp.int32, (LANES, block), 0) == rank
    for g in range(groups):
        pick = (here & (owner == g)).astype(F32).astype(BF16)
        pick_ref[g * slots : (g + 1) * slots] = pick[:slots]
        tail_ref[g] = jnp.concatenate([dot(high, pick, NT), dot(low, pick, NT)], axis=1).astype(BF16)


def powers_of(q, item_ref, rate_ref=None):
    logits = dot(item_ref[...], q, NT) * (SCALE * LOG2E)
    top = jnp.max(logits, axis=0, keepdims=True)
    e = jnp.exp2(logits - top)
    return (e if rate_ref is None else e * spread(rate_ref[...], q.shape[0])), top, logits


def column_sum(x):
    return jnp.sum(x, axis=0, keepdims=True)


def join(tops, sums):
    top = functools.reduce(jnp.maximum, tops)
    shrinks = [jnp.exp2(t - top) for t in tops]
    total = sum(x * s for x, s in zip(sums, shrinks))
    inverse = 1.0 / total
    return top, total, [s * inverse for s in shrinks]


def diagonal(block):
    return lax.broadcasted_iota(jnp.int32, (block, block), 0) == lax.broadcasted_iota(
        jnp.int32, (block, block), 1
    )


def early_kernel(n, q_ref, *refs):
    item_refs, (e_ref, tops_ref) = refs[:n], refs[n:]
    q = q_ref[...]
    for b in range(n):
        e, tops_ref[b : b + 1], logits = powers_of(q, item_refs[b])
        e_ref[b] = e
        if b == 0:
            tops_ref[n : n + 1] = column_sum(jnp.where(diagonal(q.shape[0]), logits, 0.0))


def rate_kernel(n, early, e_ref, near_ref, mate_ref, rate_ref, out_ref, sums_ref):
    block = e_ref.shape[1]
    near = [near_ref[:, k * block : (k + 1) * block].astype(F32) for k in range(n // 2)]
    mate = [mate_ref[:, k * block : (k + 1) * block].astype(F32) for k in range(n // 2)]
    counts = [near[0], mate[0]] + near[1:] + mate[1:]
    for b in range(n):
        rate = jnp.transpose(jnp.broadcast_to(1.0 / counts[b], (LANES, block)))
        rate_ref[b] = rate
        if b < early:
            e = e_ref[b] * spread(rate, block)
            out_ref[b] = e
            sums_ref[b : b + 1] = column_sum(e)
    sums_ref[early : early + 1] = jnp.log(counts[0]) * LOG2E


def far_powers(n, q, item_refs, rate_ref, e_ref):
    tops, sums = [], []
    for b in range(n):
        e, top, _ = powers_of(q, item_refs[b], rate_ref.at[b])
        if b < 2:
            e_ref[b] = e
        tops.append(top)
        sums.append(column_sum(e))
    return join(tops, sums)[2]


def main_kernel(early, late, *refs):
    n = early + late
    q_ref, far_ref, item_refs, refs = refs[0], refs[1], refs[2 : 2 + n], refs[2 + n :]
    rate_ref, e_ref, tops_ref, sums_ref, mine_out, mate_out, *refs = refs
    late_ref, factor_ref, far_e_ref = refs
    q, far = q_ref[...], far_ref[...]
    tops = [tops_ref[b : b + 1] for b in range(early)]
    sums = [sums_ref[b : b + 1] for b in range(early)]
    for b in range(late):
        e, top, _ = powers_of(q, item_refs[early + b], rate_ref.at[early + b])
        late_ref[b] = e
        tops.append(top)
        sums.append(column_sum(e))
    top, total, factors = join(tops, sums)
    far_factors = far_powers(n, far, item_refs, rate_ref, far_e_ref)
    mate = dot((e_ref[1] * factors[1]).astype(BF16), q)
    mate += dot((far_e_ref[1] * far_factors[1]).astype(BF16), far)
    mate_out[...] = code(mate * SCALE).astype(BF16) if mate_out.dtype == BF16 else mate
    weights = e_ref[0] * factors[0]
    weights = jnp.where(diagonal(q.shape[0]), weights - 1.0, weights)
    mine = dot(weights.astype(BF16), q)
    mine_out[...] = mine + dot((far_e_ref[0] * far_factors[0]).astype(BF16), far)
    chosen = tops_ref[early : early + 1] - sums_ref[early : early + 1]
    factor_ref[n : n + 1] = (top + jnp.log2(total) - chosen) * (1.0 / LOG2E)
    for b in range(n):
        factor_ref[b : b + 1] = factors[b]


def more_kernel(n, q_ref, *refs):
    item_refs, refs = refs[:n], refs[n:]
    rate_ref, mine_ref, mate_ref, mine_out, mate_out, e_ref = refs
    q = q_ref[...]
    factors = far_powers(n, q, item_refs, rate_ref, e_ref)
    mate = mate_ref[...] + dot((e_ref[1] * factors[1]).astype(BF16), q)
    mate_out[...] = code(mate * SCALE).astype(BF16) if mate_out.dtype == BF16 else mate
    mine_out[...] = mine_ref[...] + dot((e_ref[0] * factors[0]).astype(BF16), q)


def query_kernel(early, late, e_ref, late_ref, factor_ref, *refs):
    item_refs, out_ref, loss_ref = refs[:-2], refs[-2], refs[-1]
    loss_ref[...] = factor_ref[early + late]
    total = None
    for b, item_ref in enumerate(item_refs):
        e = e_ref[b] if b < early else late_ref[b - early]
        weights = e * factor_ref[b : b + 1]
        if b == 0:
            weights = jnp.where(diagonal(weights.shape[0]), weights - 1.0, weights)
        part = dot(weights.astype(BF16), item_ref[...], TN)
        total = part if total is None else total + part
    out_ref[...] = total * SCALE


def split(x):
    high = x.astype(BF16)
    return jnp.concatenate([high, (x - high.astype(F32)).astype(BF16)], axis=1)


def give_kernel(slots, pick_ref, mate_pick_ref, mine_ref, mate_ref, out_ref):
    mate = code(mate_ref[...] * SCALE).astype(BF16)
    out_ref[: 6 * slots] = dot(mate_pick_ref[2 * slots :], mate).astype(BF16)
    mine = code(mine_ref[...] * SCALE).astype(BF16)
    out_ref[6 * slots :] = dot(pick_ref[2 * slots : 4 * slots], mine).astype(BF16)


def keep_kernel(slots, pick_ref, mate_pick_ref, mine_ref, mate_ref, out_ref):
    mine = split(mine_ref[...] * SCALE)
    both = dot(pick_ref[: 2 * slots], mine)
    out_ref[: 2 * slots] = both[:, :D] + both[:, D:]
    both = dot(pick_ref[4 * slots :], mine)
    out_ref[2 * slots : 6 * slots] = both[:, :D] + both[:, D:]
    both = dot(mate_pick_ref[: 2 * slots], split(mate_ref[...] * SCALE))
    out_ref[6 * slots :] = both[:, :D] + both[:, D:]


def pack_kernel(slots, keep_ref, given_ref, tail_ref, mate_tail_ref, *out_refs):
    def rows(k):
        here = slice(k * slots, (k + 1) * slots)
        return code(keep_ref[here] + decode(given_ref[here].astype(F32))).astype(BF16)

    for p in range(2):
        out_refs[p][0, :slots] = rows(p)
        out_refs[p][0, slots:] = tail_ref[p]
        out_refs[p][1, :slots] = rows(6 + p)
        out_refs[p][1, slots:] = mate_tail_ref[p]
    for p in range(4):
        out_refs[2 + p][:slots] = rows(2 + p)
        out_refs[2 + p][slots:] = tail_ref[4 + p]


def plain_pack_kernel(groups, slots, pick_ref, tail_ref, mine_ref, other_ref, out_ref):
    grad = mine_ref[...] * SCALE + decode(other_ref[...].astype(F32))
    picked = dot(pick_ref[...], code(grad).astype(BF16)).astype(BF16)
    for g in range(groups):
        out_ref[g, :slots] = picked[g * slots : (g + 1) * slots]
        out_ref[g, slots:] = tail_ref[g]


def unpack(slots, paired, got_refs, values_ref, ids_ref):
    packets = []
    for ref in got_refs:
        if len(ref.shape) == 2:
            packets.append(ref)
        else:
            packets += [ref.at[g] for g in range(1 if paired else ref.shape[0])]
    half = len(packets) * slots
    for g, got in enumerate(packets):
        tail = got[slots : slots + TAIL].astype(F32)
        ids = tail[:, :slots] * LANES + tail[:, LANES : LANES + slots]
        ids_ref[:, g * slots : (g + 1) * slots] = ids
        values = decode(got[:slots].astype(F32))
        high = values.astype(BF16)
        values_ref[g * slots : (g + 1) * slots] = high
        low = (values - high.astype(F32)).astype(BF16)
        values_ref[half + g * slots : half + (g + 1) * slots] = low


def scatter(values_ref, ids_ref, first, rows):
    index = lax.broadcasted_iota(jnp.int32, (rows, ids_ref.shape[1]), 0) + first
    put = (index.astype(F32) == ids_ref[:1]).astype(F32).astype(BF16)
    return dot(jnp.concatenate([put, put], axis=1), values_ref[...])


def first_kernel(slots, *refs):
    got_refs, (out_ref, values_ref, ids_ref) = refs[:-3], refs[-3:]
    unpack(slots, True, got_refs, values_ref, ids_ref)
    out_ref[...] = scatter(values_ref, ids_ref, 0, out_ref.shape[0])


def update_kernel(slots, partial, *refs):
    inputs, refs = refs[:-8], refs[-8:]
    table_ref, accum_ref, table_out, accum_out, values_ref, ids_ref, new_ref, sems = refs
    unpack(slots, partial, inputs[1:] if partial else inputs, values_ref, ids_ref)
    chunks = sems.shape[1]
    rows = table_ref.shape[0] // chunks
    copies = []
    for c in range(chunks):
        here = slice(c * rows, (c + 1) * rows)
        grad = scatter(values_ref, ids_ref, c * rows, rows)
        if partial:
            grad += inputs[0][here]
        accum_new = accum_ref[here] + grad * grad
        new_ref[1, here] = accum_new
        copies.append(pltpu.make_async_copy(new_ref.at[1, here], accum_out.at[here], sems.at[1, c]))
        copies[-1].start()
        new_ref[0, here] = table_ref[here] - 0.1 * grad / (jnp.sqrt(accum_new) + 1e-08)
        copies.append(pltpu.make_async_copy(new_ref.at[0, here], table_out.at[here], sems.at[0, c]))
        copies[-1].start()
    for copy in copies:
        copy.wait()


def call(kernel, outs, *args, scratch=(), limit=16, flops=0):
    return pl.pallas_call(
        kernel,
        out_shape=[jax.ShapeDtypeStruct(s, t) for s, t in outs],
        scratch_shapes=list(scratch),
        compiler_params=pltpu.CompilerParams(vmem_limit_bytes=limit * MIB),
        cost_estimate=pl.CostEstimate(flops=flops, bytes_accessed=1024, transcendentals=0),
    )(*args)


def shards(queries, items, item_owner, item_offset, sample_counts, table, accum):
    block = queries.shape[0]
    n, groups = lax.axis_size("wide"), lax.axis_size("group")
    capacity = 2 * block // groups
    slots = -(-capacity // TAIL) * TAIL
    paired = groups == 8 and n == 4

    def swap(x, k, axis="wide"):
        return lax.ppermute(x, axis, [(i, i ^ k) for i in range(lax.axis_size(axis))])

    far_counts = [swap(sample_counts, k) for k in range(2, n, 2)]
    far_items = [swap(items, k) for k in range(2, n, 2)]
    far_queries = [swap(queries, k) for k in range(2, n, 2)]

    owner = item_owner.reshape(1, block)
    if paired:
        partner = owner ^ lax.axis_index("group")
        flip = lax.axis_index("wide") % 2 * 2
        owner = jnp.zeros_like(partner)
        for core in range(2):
            for k in range(2):
                place = (2 * core + k) ^ flip
                owner = jnp.where(partner == FAR[k][core], place, owner)
        for k in range(4):
            owner = jnp.where(partner == NEAR[k], 4 + k, owner)
    codes = owner * ROW_CODES + item_offset.reshape(1, block)

    def route(codes, flip, flops):
        return call(
            functools.partial(local_kernel, groups, slots, flip),
            [((groups * slots, block), BF16), ((groups, TAIL, D), BF16)],
            codes,
            flops=flops,
        )

    pick, tail = route(codes, 0, 0)
    tails, own_items = [tail], items
    if paired:
        mate_codes, own_items = lax.optimization_barrier((swap(codes, 1), items))
        mate_pick, mate_tail = route(mate_codes, 2, 1 << 30)
        tails.append(mate_tail)
    far_items, far_counts, tails = lax.optimization_barrier((far_items, far_counts, tails))
    item_blocks = [items, swap(own_items, 1)] + far_items
    early = len(item_blocks)
    item_blocks += [swap(x, 1) for x in far_items]
    late = n - early
    near_counts = jnp.concatenate([sample_counts, *far_counts])
    mate_counts = swap(near_counts, 1)
    part = ((block, D), F32)
    square = (block, block)
    rows_of = ((-(-(n + 1) // TAIL) * TAIL, block), F32)
    sent = ((block, D), BF16)
    powers, stats = call(
        functools.partial(early_kernel, early),
        [((early, *square), F32), rows_of],
        queries,
        *item_blocks[:early],
        limit=8 + 2 * n,
        flops=1 << 29,
    )
    rates, powers, totals = call(
        functools.partial(rate_kernel, n, early),
        [((n, block, LANES), F32), ((early, *square), F32), rows_of],
        powers,
        near_counts.reshape(1, -1),
        mate_counts.reshape(1, -1),
        limit=8 + 4 * n,
    )
    mine, mate, late_powers, factors = call(
        functools.partial(main_kernel, early, late),
        [
            part,
            part if paired or far_queries[1:] else sent,
            ((late, *square), F32),
            rows_of,
        ],
        queries,
        far_queries[0],
        *item_blocks,
        rates,
        powers,
        stats,
        totals,
        scratch=[pltpu.VMEM((2, *square), F32)],
        limit=8 + 4 * n,
    )
    for k, far in enumerate(far_queries[1:], 2):
        mine, mate = call(
            functools.partial(more_kernel, n),
            [part, part if k < len(far_queries) else sent],
            far,
            *item_blocks,
            rates,
            mine,
            mate,
            scratch=[pltpu.VMEM((2, *square), F32)],
            limit=8 + 4 * n,
        )
    query_grad, loss = call(
        functools.partial(query_kernel, early, late),
        [part, ((block,), F32)],
        powers,
        late_powers,
        factors,
        *item_blocks,
        limit=8 + 2 * n,
        flops=1 << 30,
    )
    if paired:
        sums = ((groups * slots, D), BF16)
        partials = (pick, mate_pick, mine, mate)
        (give,) = call(functools.partial(give_kernel, slots), [sums], *partials)
        given = swap(give, 1)
        (keep,) = call(
            functools.partial(keep_kernel, slots), [(sums[0], F32)], *partials, flops=1 << 29
        )
        packet = (slots + TAIL, D)
        packed = call(
            functools.partial(pack_kernel, slots),
            [((2, *packet), BF16)] * 2 + [(packet, BF16)] * 4,
            keep,
            given,
            *tails,
        )
        far = []
        for p in range(2):
            pairs = [
                (w * groups + g, w * groups + (g ^ FAR[p][w % 2]))
                for w in range(n)
                for g in range(groups)
            ]
            far.append(lax.ppermute(packed[p], ("wide", "group"), pairs))
        near = [swap(packed[2 + k], NEAR[k], "group") for k in range(1, 4)]
        forwarded = [swap(x[1], 1) for x in far]
        got = [packed[2], *far, *near, *forwarded]
    else:
        (packed,) = call(
            functools.partial(plain_pack_kernel, groups, slots),
            [((groups, slots + TAIL, D), BF16)],
            pick,
            *tails,
            mine,
            swap(mate, 1),
        )
        got = [lax.all_to_all(packed, "group", split_axis=0, concat_axis=0, tiled=True)]

    rows = table.shape[0]

    def scratch(packets):
        return [
            pltpu.VMEM((2 * packets * slots, D), BF16),
            pltpu.VMEM((TAIL, packets * slots), F32),
        ]

    count = 6
    before = []
    if paired:
        before = call(
            functools.partial(first_kernel, slots),
            [((rows, D), F32)],
            *got[:count],
            scratch=scratch(count),
            flops=1 << 28,
        )
        got = got[count:]
    table_new, accum_new = pl.pallas_call(
        functools.partial(update_kernel, slots, paired),
        out_shape=[jax.ShapeDtypeStruct(table.shape, F32)] * 2,
        out_specs=[pl.BlockSpec(memory_space=pl.ANY)] * 2,
        scratch_shapes=[
            *scratch(len(got) if paired else groups),
            pltpu.VMEM((2, rows, D), F32),
            pltpu.SemaphoreType.DMA((2, 4)),
        ],
        compiler_params=pltpu.CompilerParams(vmem_limit_bytes=32 * MIB),
    )(*before, *got, table, accum)
    return (loss, query_grad, table_new, accum_new)


def solution(mesh):
    placed = (
        P(("wide", "group"), None),
        P(("wide", "group"), None),
        P(("wide", "group"), None),
        P(("wide", "group")),
        P(("wide", "group")),
        P(("wide", "group"), None),
        P(("wide", "group"), None),
    )
    return jax.shard_map(
        shards,
        mesh=mesh,
        in_specs=placed,
        out_specs=(
            P(("wide", "group")),
            P(("wide", "group"), None),
            P(("wide", "group"), None),
            P(("wide", "group"), None),
        ),
        check_vma=False,
    )
```

```python
import functools
import math

import jax
import jax.numpy as jnp
from jax import lax
from jax.experimental import pallas as pl
from jax.experimental.pallas import tpu as pltpu
from jax.sharding import PartitionSpec as P

D = 256
SCALE = 3.0 / math.sqrt(D)
LOG2E = math.log2(math.e)
LANES = 128
TAIL = 8
ROW_CODES = 1 << 16
FAR = ((4, 5), (6, 7))
NEAR = (0, 3, 1, 2)
MIB = 1 << 20
NT = (((1,), (1,)), ((), ()))
TN = (((0,), (0,)), ((), ()))
F32 = jnp.float32
BF16 = jnp.bfloat16


def dot(a, b, dims=(((1,), (0,)), ((), ()))):
    return lax.dot_general(a, b, dims, preferred_element_type=F32)


def spread(column, width):
    pieces = [column] * (width // LANES)
    if width % LANES:
        pieces.append(column[:, : width % LANES])
    return jnp.concatenate(pieces, axis=1)


def code(x):
    y = x * x
    return jnp.where(x < 0, -y, y) * y


def decode(u):
    root = lax.rsqrt(lax.rsqrt(jnp.abs(u)))
    return jnp.where(u < 0, -root, root)


def diagonal(block):
    return lax.broadcasted_iota(jnp.int32, (block, block), 0) == lax.broadcasted_iota(
        jnp.int32, (block, block), 1
    )


def local_kernel(groups, slots, flip, code_ref, pick_ref, tail_ref):
    block = code_ref.shape[1]
    owner = code_ref[...] // ROW_CODES
    owner = jnp.where(owner < groups // 2, owner ^ flip, owner)
    offset = code_ref[...] % ROW_CODES
    member = lax.broadcasted_iota(jnp.int32, (groups, block), 0) == owner
    before = lax.broadcasted_iota(jnp.int32, (block, block), 0) < lax.broadcasted_iota(
        jnp.int32, (block, block), 1
    )
    ranks = dot(member.astype(BF16), before.astype(BF16))
    rank = jnp.sum(jnp.where(member, ranks, 0.0), axis=0, keepdims=True).astype(jnp.int32)
    high = jnp.broadcast_to((offset // LANES).astype(F32), (TAIL, block)).astype(BF16)
    low = jnp.broadcast_to((offset % LANES).astype(F32), (TAIL, block)).astype(BF16)
    here = lax.broadcasted_iota(jnp.int32, (LANES, block), 0) == rank
    for g in range(groups):
        pick = (here & (owner == g)).astype(F32).astype(BF16)
        pick_ref[g * slots : (g + 1) * slots] = pick[:slots]
        tail_ref[g] = jnp.concatenate([dot(high, pick, NT), dot(low, pick, NT)], axis=1).astype(BF16)


def powers_of(q, item_ref, rate_ref=None):
    logits = dot(item_ref[...], q, NT) * (SCALE * LOG2E)
    top = jnp.max(logits, axis=0, keepdims=True)
    e = jnp.exp2(logits - top)
    return (e if rate_ref is None else e * spread(rate_ref[...], q.shape[0])), top, logits


def column_sum(x):
    return jnp.sum(x, axis=0, keepdims=True)


def join(tops, sums):
    top = functools.reduce(jnp.maximum, tops)
    shrinks = [jnp.exp2(t - top) for t in tops]
    total = sum(x * s for x, s in zip(sums, shrinks))
    inverse = 1.0 / total
    return top, total, [s * inverse for s in shrinks]


def diagonal(block):
    return lax.broadcasted_iota(jnp.int32, (block, block), 0) == lax.broadcasted_iota(
        jnp.int32, (block, block), 1
    )


def early_kernel(n, q_ref, *refs):
    item_refs, (e_ref, tops_ref) = refs[:n], refs[n:]
    q = q_ref[...]
    for b in range(n):
        e, tops_ref[b : b + 1], logits = powers_of(q, item_refs[b])
        e_ref[b] = e
        if b == 0:
            tops_ref[n : n + 1] = column_sum(jnp.where(diagonal(q.shape[0]), logits, 0.0))


def rate_kernel(n, early, e_ref, near_ref, mate_ref, rate_ref, out_ref, sums_ref):
    block = e_ref.shape[1]
    near = [near_ref[:, k * block : (k + 1) * block].astype(F32) for k in range(n // 2)]
    mate = [mate_ref[:, k * block : (k + 1) * block].astype(F32) for k in range(n // 2)]
    counts = [near[0], mate[0]] + near[1:] + mate[1:]
    for b in range(n):
        rate = jnp.transpose(jnp.broadcast_to(1.0 / counts[b], (LANES, block)))
        rate_ref[b] = rate
        if b < early:
            e = e_ref[b] * spread(rate, block)
            out_ref[b] = e
            sums_ref[b : b + 1] = column_sum(e)
    sums_ref[early : early + 1] = jnp.log(counts[0]) * LOG2E


def far_powers(n, q, item_refs, rate_ref, e_ref):
    tops, sums = [], []
    for b in range(n):
        e, top, _ = powers_of(q, item_refs[b], rate_ref.at[b])
        if b < 2:
            e_ref[b] = e
        tops.append(top)
        sums.append(column_sum(e))
    return join(tops, sums)[2]


def main_kernel(early, late, *refs):
    n = early + late
    q_ref, far_ref, item_refs, refs = refs[0], refs[1], refs[2 : 2 + n], refs[2 + n :]
    rate_ref, e_ref, tops_ref, sums_ref, mine_out, mate_out, *refs = refs
    late_ref, factor_ref, far_e_ref = refs
    q, far = q_ref[...], far_ref[...]
    tops = [tops_ref[b : b + 1] for b in range(early)]
    sums = [sums_ref[b : b + 1] for b in range(early)]
    for b in range(late):
        e, top, _ = powers_of(q, item_refs[early + b], rate_ref.at[early + b])
        late_ref[b] = e
        tops.append(top)
        sums.append(column_sum(e))
    top, total, factors = join(tops, sums)
    far_factors = far_powers(n, far, item_refs, rate_ref, far_e_ref)
    mate = dot((e_ref[1] * factors[1]).astype(BF16), q)
    mate += dot((far_e_ref[1] * far_factors[1]).astype(BF16), far)
    mate_out[...] = code(mate * SCALE).astype(BF16) if mate_out.dtype == BF16 else mate
    weights = e_ref[0] * factors[0]
    weights = jnp.where(diagonal(q.shape[0]), weights - 1.0, weights)
    mine = dot(weights.astype(BF16), q)
    mine_out[...] = mine + dot((far_e_ref[0] * far_factors[0]).astype(BF16), far)
    chosen = tops_ref[early : early + 1] - sums_ref[early : early + 1]
    factor_ref[n : n + 1] = (top + jnp.log2(total) - chosen) * (1.0 / LOG2E)
    for b in range(n):
        factor_ref[b : b + 1] = factors[b]


def more_kernel(n, q_ref, *refs):
    item_refs, refs = refs[:n], refs[n:]
    rate_ref, mine_ref, mate_ref, mine_out, mate_out, e_ref = refs
    q = q_ref[...]
    factors = far_powers(n, q, item_refs, rate_ref, e_ref)
    mate = mate_ref[...] + dot((e_ref[1] * factors[1]).astype(BF16), q)
    mate_out[...] = code(mate * SCALE).astype(BF16) if mate_out.dtype == BF16 else mate
    mine_out[...] = mine_ref[...] + dot((e_ref[0] * factors[0]).astype(BF16), q)


def query_kernel(early, late, e_ref, late_ref, factor_ref, *refs):
    item_refs, out_ref, loss_ref = refs[:-2], refs[-2], refs[-1]
    loss_ref[...] = factor_ref[early + late]
    total = None
    for b, item_ref in enumerate(item_refs):
        e = e_ref[b] if b < early else late_ref[b - early]
        weights = e * factor_ref[b : b + 1]
        if b == 0:
            weights = jnp.where(diagonal(weights.shape[0]), weights - 1.0, weights)
        part = dot(weights.astype(BF16), item_ref[...], TN)
        total = part if total is None else total + part
    out_ref[...] = total * SCALE


def split(x):
    high = x.astype(BF16)
    return jnp.concatenate([high, (x - high.astype(F32)).astype(BF16)], axis=1)


def give_kernel(slots, pick_ref, mate_pick_ref, mine_ref, mate_ref, out_ref):
    mate = code(mate_ref[...] * SCALE).astype(BF16)
    out_ref[: 6 * slots] = dot(mate_pick_ref[2 * slots :], mate).astype(BF16)
    mine = code(mine_ref[...] * SCALE).astype(BF16)
    out_ref[6 * slots :] = dot(pick_ref[2 * slots : 4 * slots], mine).astype(BF16)


def keep_kernel(slots, pick_ref, mate_pick_ref, mine_ref, mate_ref, out_ref):
    mine = split(mine_ref[...] * SCALE)
    both = dot(pick_ref[: 2 * slots], mine)
    out_ref[: 2 * slots] = both[:, :D] + both[:, D:]
    both = dot(pick_ref[4 * slots :], mine)
    out_ref[2 * slots : 6 * slots] = both[:, :D] + both[:, D:]
    both = dot(mate_pick_ref[: 2 * slots], split(mate_ref[...] * SCALE))
    out_ref[6 * slots :] = both[:, :D] + both[:, D:]


def pack_kernel(slots, keep_ref, given_ref, tail_ref, mate_tail_ref, *out_refs):
    def rows(k):
        here = slice(k * slots, (k + 1) * slots)
        return code(keep_ref[here] + decode(given_ref[here].astype(F32))).astype(BF16)

    for p in range(2):
        out_refs[p][0, :slots] = rows(p)
        out_refs[p][0, slots:] = tail_ref[p]
        out_refs[p][1, :slots] = rows(6 + p)
        out_refs[p][1, slots:] = mate_tail_ref[p]
    for p in range(4):
        out_refs[2 + p][:slots] = rows(2 + p)
        out_refs[2 + p][slots:] = tail_ref[4 + p]


def plain_pack_kernel(groups, slots, pick_ref, tail_ref, mine_ref, other_ref, out_ref):
    grad = mine_ref[...] * SCALE + decode(other_ref[...].astype(F32))
    picked = dot(pick_ref[...], code(grad).astype(BF16)).astype(BF16)
    for g in range(groups):
        out_ref[g, :slots] = picked[g * slots : (g + 1) * slots]
        out_ref[g, slots:] = tail_ref[g]


def unpack(slots, paired, got_refs, values_ref, ids_ref):
    packets = []
    for ref in got_refs:
        if len(ref.shape) == 2:
            packets.append(ref)
        else:
            packets += [ref.at[g] for g in range(1 if paired else ref.shape[0])]
    half = len(packets) * slots
    for g, got in enumerate(packets):
        tail = got[slots : slots + TAIL].astype(F32)
        ids = tail[:, :slots] * LANES + tail[:, LANES : LANES + slots]
        ids_ref[:, g * slots : (g + 1) * slots] = ids
        values = decode(got[:slots].astype(F32))
        high = values.astype(BF16)
        values_ref[g * slots : (g + 1) * slots] = high
        low = (values - high.astype(F32)).astype(BF16)
        values_ref[half + g * slots : half + (g + 1) * slots] = low


def scatter(values_ref, ids_ref, first, rows):
    index = lax.broadcasted_iota(jnp.int32, (rows, ids_ref.shape[1]), 0) + first
    put = (index.astype(F32) == ids_ref[:1]).astype(F32).astype(BF16)
    return dot(jnp.concatenate([put, put], axis=1), values_ref[...])


def first_kernel(slots, *refs):
    got_refs, (out_ref, values_ref, ids_ref) = refs[:-3], refs[-3:]
    unpack(slots, True, got_refs, values_ref, ids_ref)
    out_ref[...] = scatter(values_ref, ids_ref, 0, out_ref.shape[0])


def update_kernel(slots, partial, *refs):
    inputs, refs = refs[:-8], refs[-8:]
    table_ref, accum_ref, table_out, accum_out, values_ref, ids_ref, new_ref, sems = refs
    unpack(slots, partial, inputs[1:] if partial else inputs, values_ref, ids_ref)
    chunks = sems.shape[1]
    rows = table_ref.shape[0] // chunks
    copies = []
    for c in range(chunks):
        here = slice(c * rows, (c + 1) * rows)
        grad = scatter(values_ref, ids_ref, c * rows, rows)
        if partial:
            grad += inputs[0][here]
        accum_new = accum_ref[here] + grad * grad
        new_ref[1, here] = accum_new
        copies.append(pltpu.make_async_copy(new_ref.at[1, here], accum_out.at[here], sems.at[1, c]))
        copies[-1].start()
        new_ref[0, here] = table_ref[here] - 0.1 * grad / (jnp.sqrt(accum_new) + 1e-08)
        copies.append(pltpu.make_async_copy(new_ref.at[0, here], table_out.at[here], sems.at[0, c]))
        copies[-1].start()
    for copy in copies:
        copy.wait()


def call(kernel, outs, *args, scratch=(), limit=16, flops=0):
    return pl.pallas_call(
        kernel,
        out_shape=[jax.ShapeDtypeStruct(s, t) for s, t in outs],
        scratch_shapes=list(scratch),
        compiler_params=pltpu.CompilerParams(vmem_limit_bytes=limit * MIB),
        cost_estimate=pl.CostEstimate(flops=flops, bytes_accessed=1024, transcendentals=0),
    )(*args)


def shards(queries, items, item_owner, item_offset, sample_counts, table, accum):
    block = queries.shape[0]
    n, groups = lax.axis_size("wide"), lax.axis_size("group")
    capacity = 2 * block // groups
    slots = -(-capacity // TAIL) * TAIL
    paired = groups == 8 and n == 4

    def swap(x, k, axis="wide"):
        return lax.ppermute(x, axis, [(i, i ^ k) for i in range(lax.axis_size(axis))])

    far_counts = [swap(sample_counts, k) for k in range(2, n, 2)]
    far_items = [swap(items, k) for k in range(2, n, 2)]
    far_queries = [swap(queries, k) for k in range(2, n, 2)]

    owner = item_owner.reshape(1, block)
    if paired:
        partner = owner ^ lax.axis_index("group")
        flip = lax.axis_index("wide") % 2 * 2
        owner = jnp.zeros_like(partner)
        for core in range(2):
            for k in range(2):
                place = (2 * core + k) ^ flip
                owner = jnp.where(partner == FAR[k][core], place, owner)
        for k in range(4):
            owner = jnp.where(partner == NEAR[k], 4 + k, owner)
    codes = owner * ROW_CODES + item_offset.reshape(1, block)

    def route(codes, flip, flops):
        return call(
            functools.partial(local_kernel, groups, slots, flip),
            [((groups * slots, block), BF16), ((groups, TAIL, D), BF16)],
            codes,
            flops=flops,
        )

    pick, tail = route(codes, 0, 0)
    tails, own_items = [tail], items
    if paired:
        mate_codes, own_items = lax.optimization_barrier((swap(codes, 1), items))
        mate_pick, mate_tail = route(mate_codes, 2, 1 << 30)
        tails.append(mate_tail)
    far_items, far_counts, tails = lax.optimization_barrier((far_items, far_counts, tails))
    item_blocks = [items, swap(own_items, 1)] + far_items
    early = len(item_blocks)
    item_blocks += [swap(x, 1) for x in far_items]
    late = n - early
    near_counts = jnp.concatenate([sample_counts, *far_counts])
    mate_counts = swap(near_counts, 1)
    part = ((block, D), F32)
    square = (block, block)
    rows_of = ((-(-(n + 1) // TAIL) * TAIL, block), F32)
    sent = ((block, D), BF16)
    powers, stats = call(
        functools.partial(early_kernel, early),
        [((early, *square), F32), rows_of],
        queries,
        *item_blocks[:early],
        limit=8 + 2 * n,
        flops=1 << 29,
    )
    rates, powers, totals = call(
        functools.partial(rate_kernel, n, early),
        [((n, block, LANES), F32), ((early, *square), F32), rows_of],
        powers,
        near_counts.reshape(1, -1),
        mate_counts.reshape(1, -1),
        limit=8 + 4 * n,
    )
    mine, mate, late_powers, factors = call(
        functools.partial(main_kernel, early, late),
        [
            part,
            part if paired or far_queries[1:] else sent,
            ((late, *square), F32),
            rows_of,
        ],
        queries,
        far_queries[0],
        *item_blocks,
        rates,
        powers,
        stats,
        totals,
        scratch=[pltpu.VMEM((2, *square), F32)],
        limit=8 + 4 * n,
    )
    for k, far in enumerate(far_queries[1:], 2):
        mine, mate = call(
            functools.partial(more_kernel, n),
            [part, part if k < len(far_queries) else sent],
            far,
            *item_blocks,
            rates,
            mine,
            mate,
            scratch=[pltpu.VMEM((2, *square), F32)],
            limit=8 + 4 * n,
        )
    if paired:
        sums = ((groups * slots, D), BF16)
        partials = (pick, mate_pick, mine, mate)
        (give,) = call(functools.partial(give_kernel, slots), [sums], *partials)
        given = swap(give, 1)
        (keep,) = call(
            functools.partial(keep_kernel, slots), [(sums[0], F32)], *partials, flops=1 << 29
        )
        query_grad, loss = call(
            functools.partial(query_kernel, early, late),
            [part, ((block,), F32)],
            powers,
            late_powers,
            factors,
            *item_blocks,
            limit=8 + 2 * n,
            flops=1 << 30,
        )
        given, query_grad = lax.optimization_barrier((given, query_grad))
        packet = (slots + TAIL, D)
        packed = call(
            functools.partial(pack_kernel, slots),
            [((2, *packet), BF16)] * 2 + [(packet, BF16)] * 4,
            keep,
            given,
            *tails,
        )
        far = []
        for p in range(2):
            pairs = [
                (w * groups + g, w * groups + (g ^ FAR[p][w % 2]))
                for w in range(n)
                for g in range(groups)
            ]
            far.append(lax.ppermute(packed[p], ("wide", "group"), pairs))
        near = [swap(packed[2 + k], NEAR[k], "group") for k in range(1, 4)]
        forwarded = [swap(x[1], 1) for x in far]
        got = [packed[2], *far, *near, *forwarded]
    else:
        query_grad, loss = call(
            functools.partial(query_kernel, early, late),
            [part, ((block,), F32)],
            powers,
            late_powers,
            factors,
            *item_blocks,
            limit=8 + 2 * n,
            flops=1 << 30,
        )
        (packed,) = call(
            functools.partial(plain_pack_kernel, groups, slots),
            [((groups, slots + TAIL, D), BF16)],
            pick,
            *tails,
            mine,
            swap(mate, 1),
        )
        got = [lax.all_to_all(packed, "group", split_axis=0, concat_axis=0, tiled=True)]

    rows = table.shape[0]

    def scratch(packets):
        return [
            pltpu.VMEM((2 * packets * slots, D), BF16),
            pltpu.VMEM((TAIL, packets * slots), F32),
        ]

    count = 3
    before = []
    if paired:
        before = call(
            functools.partial(first_kernel, slots),
            [((rows, D), F32)],
            *got[:count],
            scratch=scratch(count),
            flops=1 << 28,
        )
        got = got[count:]
    table_new, accum_new = pl.pallas_call(
        functools.partial(update_kernel, slots, paired),
        out_shape=[jax.ShapeDtypeStruct(table.shape, F32)] * 2,
        out_specs=[pl.BlockSpec(memory_space=pl.ANY)] * 2,
        scratch_shapes=[
            *scratch(len(got) if paired else groups),
            pltpu.VMEM((2, rows, D), F32),
            pltpu.SemaphoreType.DMA((2, 4)),
        ],
        compiler_params=pltpu.CompilerParams(vmem_limit_bytes=32 * MIB),
    )(*before, *got, table, accum)
    return (loss, query_grad, table_new, accum_new)


def solution(mesh):
    placed = (
        P(("wide", "group"), None),
        P(("wide", "group"), None),
        P(("wide", "group"), None),
        P(("wide", "group")),
        P(("wide", "group")),
        P(("wide", "group"), None),
        P(("wide", "group"), None),
    )
    return jax.shard_map(
        shards,
        mesh=mesh,
        in_specs=placed,
        out_specs=(
            P(("wide", "group")),
            P(("wide", "group"), None),
            P(("wide", "group"), None),
            P(("wide", "group"), None),
        ),
        check_vma=False,
    )
```

```python
import functools
import math

import jax
import jax.numpy as jnp
from jax import lax
from jax.experimental import pallas as pl
from jax.experimental.pallas import tpu as pltpu
from jax.sharding import PartitionSpec as P

D = 256
SCALE = 3.0 / math.sqrt(D)
LOG2E = math.log2(math.e)
LANES = 128
TAIL = 8
ROW_CODES = 1 << 16
FAR = ((4, 5), (6, 7))
NEAR = (0, 3, 1, 2)
MIB = 1 << 20
NT = (((1,), (1,)), ((), ()))
TN = (((0,), (0,)), ((), ()))
F32 = jnp.float32
BF16 = jnp.bfloat16


def dot(a, b, dims=(((1,), (0,)), ((), ()))):
    return lax.dot_general(a, b, dims, preferred_element_type=F32)


def spread(column, width):
    pieces = [column] * (width // LANES)
    if width % LANES:
        pieces.append(column[:, : width % LANES])
    return jnp.concatenate(pieces, axis=1)


def code(x):
    y = x * x
    return jnp.where(x < 0, -y, y) * y


def decode(u):
    root = lax.rsqrt(lax.rsqrt(jnp.abs(u)))
    return jnp.where(u < 0, -root, root)


def diagonal(block):
    return lax.broadcasted_iota(jnp.int32, (block, block), 0) == lax.broadcasted_iota(
        jnp.int32, (block, block), 1
    )


def local_kernel(groups, slots, flip, code_ref, pick_ref, tail_ref):
    block = code_ref.shape[1]
    owner = code_ref[...] // ROW_CODES
    owner = jnp.where(owner < groups // 2, owner ^ flip, owner)
    offset = code_ref[...] % ROW_CODES
    member = lax.broadcasted_iota(jnp.int32, (groups, block), 0) == owner
    before = lax.broadcasted_iota(jnp.int32, (block, block), 0) < lax.broadcasted_iota(
        jnp.int32, (block, block), 1
    )
    ranks = dot(member.astype(BF16), before.astype(BF16))
    rank = jnp.sum(jnp.where(member, ranks, 0.0), axis=0, keepdims=True).astype(jnp.int32)
    high = jnp.broadcast_to((offset // LANES).astype(F32), (TAIL, block)).astype(BF16)
    low = jnp.broadcast_to((offset % LANES).astype(F32), (TAIL, block)).astype(BF16)
    here = lax.broadcasted_iota(jnp.int32, (LANES, block), 0) == rank
    for g in range(groups):
        pick = (here & (owner == g)).astype(F32).astype(BF16)
        pick_ref[g * slots : (g + 1) * slots] = pick[:slots]
        tail_ref[g] = jnp.concatenate([dot(high, pick, NT), dot(low, pick, NT)], axis=1).astype(BF16)


def powers_of(q, item_ref, rate_ref=None):
    logits = dot(item_ref[...], q, NT) * (SCALE * LOG2E)
    top = jnp.max(logits, axis=0, keepdims=True)
    e = jnp.exp2(logits - top)
    return (e if rate_ref is None else e * spread(rate_ref[...], q.shape[0])), top, logits


def column_sum(x):
    return jnp.sum(x, axis=0, keepdims=True)


def join(tops, sums):
    top = functools.reduce(jnp.maximum, tops)
    shrinks = [jnp.exp2(t - top) for t in tops]
    total = sum(x * s for x, s in zip(sums, shrinks))
    inverse = 1.0 / total
    return top, total, [s * inverse for s in shrinks]


def diagonal(block):
    return lax.broadcasted_iota(jnp.int32, (block, block), 0) == lax.broadcasted_iota(
        jnp.int32, (block, block), 1
    )


def early_kernel(n, q_ref, *refs):
    item_refs, (e_ref, tops_ref) = refs[:n], refs[n:]
    q = q_ref[...]
    for b in range(n):
        e, tops_ref[b : b + 1], logits = powers_of(q, item_refs[b])
        e_ref[b] = e
        if b == 0:
            tops_ref[n : n + 1] = column_sum(jnp.where(diagonal(q.shape[0]), logits, 0.0))


def rate_kernel(n, early, e_ref, near_ref, mate_ref, rate_ref, out_ref, sums_ref):
    block = e_ref.shape[1]
    near = [near_ref[:, k * block : (k + 1) * block].astype(F32) for k in range(n // 2)]
    mate = [mate_ref[:, k * block : (k + 1) * block].astype(F32) for k in range(n // 2)]
    counts = [near[0], mate[0]] + near[1:] + mate[1:]
    for b in range(n):
        rate = jnp.transpose(jnp.broadcast_to(1.0 / counts[b], (LANES, block)))
        rate_ref[b] = rate
        if b < early:
            e = e_ref[b] * spread(rate, block)
            out_ref[b] = e
            sums_ref[b : b + 1] = column_sum(e)
    sums_ref[early : early + 1] = jnp.log(counts[0]) * LOG2E


def far_powers(n, q, item_refs, rate_ref, e_ref):
    tops, sums = [], []
    for b in range(n):
        e, top, _ = powers_of(q, item_refs[b], rate_ref.at[b])
        if b < 2:
            e_ref[b] = e
        tops.append(top)
        sums.append(column_sum(e))
    return join(tops, sums)[2]


def main_kernel(early, late, *refs):
    n = early + late
    q_ref, far_ref, item_refs, refs = refs[0], refs[1], refs[2 : 2 + n], refs[2 + n :]
    rate_ref, e_ref, tops_ref, sums_ref, mine_out, mate_out, *refs = refs
    late_ref, factor_ref, far_e_ref = refs
    q, far = q_ref[...], far_ref[...]
    tops = [tops_ref[b : b + 1] for b in range(early)]
    sums = [sums_ref[b : b + 1] for b in range(early)]
    for b in range(late):
        e, top, _ = powers_of(q, item_refs[early + b], rate_ref.at[early + b])
        late_ref[b] = e
        tops.append(top)
        sums.append(column_sum(e))
    top, total, factors = join(tops, sums)
    far_factors = far_powers(n, far, item_refs, rate_ref, far_e_ref)
    mate = dot((e_ref[1] * factors[1]).astype(BF16), q)
    mate += dot((far_e_ref[1] * far_factors[1]).astype(BF16), far)
    mate_out[...] = code(mate * SCALE).astype(BF16) if mate_out.dtype == BF16 else mate
    weights = e_ref[0] * factors[0]
    weights = jnp.where(diagonal(q.shape[0]), weights - 1.0, weights)
    mine = dot(weights.astype(BF16), q)
    mine_out[...] = mine + dot((far_e_ref[0] * far_factors[0]).astype(BF16), far)
    chosen = tops_ref[early : early + 1] - sums_ref[early : early + 1]
    factor_ref[n : n + 1] = (top + jnp.log2(total) - chosen) * (1.0 / LOG2E)
    for b in range(n):
        factor_ref[b : b + 1] = factors[b]


def more_kernel(n, q_ref, *refs):
    item_refs, refs = refs[:n], refs[n:]
    rate_ref, mine_ref, mate_ref, mine_out, mate_out, e_ref = refs
    q = q_ref[...]
    factors = far_powers(n, q, item_refs, rate_ref, e_ref)
    mate = mate_ref[...] + dot((e_ref[1] * factors[1]).astype(BF16), q)
    mate_out[...] = code(mate * SCALE).astype(BF16) if mate_out.dtype == BF16 else mate
    mine_out[...] = mine_ref[...] + dot((e_ref[0] * factors[0]).astype(BF16), q)


def query_kernel(early, late, e_ref, late_ref, factor_ref, *refs):
    item_refs, out_ref, loss_ref = refs[:-2], refs[-2], refs[-1]
    loss_ref[...] = factor_ref[early + late]
    total = None
    for b, item_ref in enumerate(item_refs):
        e = e_ref[b] if b < early else late_ref[b - early]
        weights = e * factor_ref[b : b + 1]
        if b == 0:
            weights = jnp.where(diagonal(weights.shape[0]), weights - 1.0, weights)
        part = dot(weights.astype(BF16), item_ref[...], TN)
        total = part if total is None else total + part
    out_ref[...] = total * SCALE


def split(x):
    high = x.astype(BF16)
    return jnp.concatenate([high, (x - high.astype(F32)).astype(BF16)], axis=1)


def give_kernel(slots, pick_ref, mate_pick_ref, mine_ref, mate_ref, out_ref):
    mate = code(mate_ref[...] * SCALE).astype(BF16)
    out_ref[: 6 * slots] = dot(mate_pick_ref[2 * slots :], mate).astype(BF16)
    mine = code(mine_ref[...] * SCALE).astype(BF16)
    out_ref[6 * slots :] = dot(pick_ref[2 * slots : 4 * slots], mine).astype(BF16)


def keep_kernel(slots, pick_ref, mate_pick_ref, mine_ref, mate_ref, out_ref):
    mine = split(mine_ref[...] * SCALE)
    both = dot(pick_ref[: 2 * slots], mine)
    out_ref[: 2 * slots] = both[:, :D] + both[:, D:]
    both = dot(pick_ref[4 * slots :], mine)
    out_ref[2 * slots : 6 * slots] = both[:, :D] + both[:, D:]
    both = dot(mate_pick_ref[: 2 * slots], split(mate_ref[...] * SCALE))
    out_ref[6 * slots :] = both[:, :D] + both[:, D:]


def pack_kernel(slots, keep_ref, given_ref, tail_ref, mate_tail_ref, *out_refs):
    def rows(k):
        here = slice(k * slots, (k + 1) * slots)
        return code(keep_ref[here] + decode(given_ref[here].astype(F32))).astype(BF16)

    for p in range(2):
        out_refs[p][0, :slots] = rows(p)
        out_refs[p][0, slots:] = tail_ref[p]
        out_refs[p][1, :slots] = rows(6 + p)
        out_refs[p][1, slots:] = mate_tail_ref[p]
    for p in range(4):
        out_refs[2 + p][:slots] = rows(2 + p)
        out_refs[2 + p][slots:] = tail_ref[4 + p]


def plain_pack_kernel(groups, slots, pick_ref, tail_ref, mine_ref, other_ref, out_ref):
    grad = mine_ref[...] * SCALE + decode(other_ref[...].astype(F32))
    picked = dot(pick_ref[...], code(grad).astype(BF16)).astype(BF16)
    for g in range(groups):
        out_ref[g, :slots] = picked[g * slots : (g + 1) * slots]
        out_ref[g, slots:] = tail_ref[g]


def unpack(slots, paired, got_refs, values_ref, ids_ref):
    packets = []
    for ref in got_refs:
        if len(ref.shape) == 2:
            packets.append(ref)
        else:
            packets += [ref.at[g] for g in range(1 if paired else ref.shape[0])]
    half = len(packets) * slots
    for g, got in enumerate(packets):
        tail = got[slots : slots + TAIL].astype(F32)
        ids = tail[:, :slots] * LANES + tail[:, LANES : LANES + slots]
        ids_ref[:, g * slots : (g + 1) * slots] = ids
        values = decode(got[:slots].astype(F32))
        high = values.astype(BF16)
        values_ref[g * slots : (g + 1) * slots] = high
        low = (values - high.astype(F32)).astype(BF16)
        values_ref[half + g * slots : half + (g + 1) * slots] = low


def scatter(values_ref, ids_ref, first, rows):
    index = lax.broadcasted_iota(jnp.int32, (rows, ids_ref.shape[1]), 0) + first
    put = (index.astype(F32) == ids_ref[:1]).astype(F32).astype(BF16)
    return dot(jnp.concatenate([put, put], axis=1), values_ref[...])


def first_kernel(slots, partial, *refs):
    inputs, (out_ref, values_ref, ids_ref) = refs[:-3], refs[-3:]
    unpack(slots, True, inputs[partial:], values_ref, ids_ref)
    sums = scatter(values_ref, ids_ref, 0, out_ref.shape[0])
    out_ref[...] = sums + inputs[0][...] if partial else sums


def update_kernel(slots, partial, *refs):
    inputs, refs = refs[:-8], refs[-8:]
    table_ref, accum_ref, table_out, accum_out, values_ref, ids_ref, new_ref, sems = refs
    unpack(slots, partial, inputs[1:] if partial else inputs, values_ref, ids_ref)
    chunks = sems.shape[1]
    rows = table_ref.shape[0] // chunks
    copies = []
    for c in range(chunks):
        here = slice(c * rows, (c + 1) * rows)
        grad = scatter(values_ref, ids_ref, c * rows, rows)
        if partial:
            grad += inputs[0][here]
        accum_new = accum_ref[here] + grad * grad
        new_ref[1, here] = accum_new
        copies.append(pltpu.make_async_copy(new_ref.at[1, here], accum_out.at[here], sems.at[1, c]))
        copies[-1].start()
        new_ref[0, here] = table_ref[here] - 0.1 * grad / (jnp.sqrt(accum_new) + 1e-08)
        copies.append(pltpu.make_async_copy(new_ref.at[0, here], table_out.at[here], sems.at[0, c]))
        copies[-1].start()
    for copy in copies:
        copy.wait()


def call(kernel, outs, *args, scratch=(), limit=16, flops=0):
    return pl.pallas_call(
        kernel,
        out_shape=[jax.ShapeDtypeStruct(s, t) for s, t in outs],
        scratch_shapes=list(scratch),
        compiler_params=pltpu.CompilerParams(vmem_limit_bytes=limit * MIB),
        cost_estimate=pl.CostEstimate(flops=flops, bytes_accessed=1024, transcendentals=0),
    )(*args)


def shards(queries, items, item_owner, item_offset, sample_counts, table, accum):
    block = queries.shape[0]
    n, groups = lax.axis_size("wide"), lax.axis_size("group")
    capacity = 2 * block // groups
    slots = -(-capacity // TAIL) * TAIL
    paired = groups == 8 and n == 4

    def swap(x, k, axis="wide"):
        return lax.ppermute(x, axis, [(i, i ^ k) for i in range(lax.axis_size(axis))])

    far_counts = [swap(sample_counts, k) for k in range(2, n, 2)]
    far_items = [swap(items, k) for k in range(2, n, 2)]
    far_queries = [swap(queries, k) for k in range(2, n, 2)]

    owner = item_owner.reshape(1, block)
    if paired:
        partner = owner ^ lax.axis_index("group")
        flip = lax.axis_index("wide") % 2 * 2
        owner = jnp.zeros_like(partner)
        for core in range(2):
            for k in range(2):
                place = (2 * core + k) ^ flip
                owner = jnp.where(partner == FAR[k][core], place, owner)
        for k in range(4):
            owner = jnp.where(partner == NEAR[k], 4 + k, owner)
    codes = owner * ROW_CODES + item_offset.reshape(1, block)

    def route(codes, flip, flops):
        return call(
            functools.partial(local_kernel, groups, slots, flip),
            [((groups * slots, block), BF16), ((groups, TAIL, D), BF16)],
            codes,
            flops=flops,
        )

    pick, tail = route(codes, 0, 0)
    tails, own_items = [tail], items
    if paired:
        mate_codes, own_items = lax.optimization_barrier((swap(codes, 1), items))
        mate_pick, mate_tail = route(mate_codes, 2, 1 << 30)
        tails.append(mate_tail)
    far_items, far_counts, tails = lax.optimization_barrier((far_items, far_counts, tails))
    item_blocks = [items, swap(own_items, 1)] + far_items
    early = len(item_blocks)
    item_blocks += [swap(x, 1) for x in far_items]
    late = n - early
    near_counts = jnp.concatenate([sample_counts, *far_counts])
    mate_counts = swap(near_counts, 1)
    part = ((block, D), F32)
    square = (block, block)
    rows_of = ((-(-(n + 1) // TAIL) * TAIL, block), F32)
    sent = ((block, D), BF16)
    powers, stats = call(
        functools.partial(early_kernel, early),
        [((early, *square), F32), rows_of],
        queries,
        *item_blocks[:early],
        limit=8 + 2 * n,
        flops=1 << 29,
    )
    rates, powers, totals = call(
        functools.partial(rate_kernel, n, early),
        [((n, block, LANES), F32), ((early, *square), F32), rows_of],
        powers,
        near_counts.reshape(1, -1),
        mate_counts.reshape(1, -1),
        limit=8 + 4 * n,
    )
    mine, mate, late_powers, factors = call(
        functools.partial(main_kernel, early, late),
        [
            part,
            part if paired or far_queries[1:] else sent,
            ((late, *square), F32),
            rows_of,
        ],
        queries,
        far_queries[0],
        *item_blocks,
        rates,
        powers,
        stats,
        totals,
        scratch=[pltpu.VMEM((2, *square), F32)],
        limit=8 + 4 * n,
    )
    for k, far in enumerate(far_queries[1:], 2):
        mine, mate = call(
            functools.partial(more_kernel, n),
            [part, part if k < len(far_queries) else sent],
            far,
            *item_blocks,
            rates,
            mine,
            mate,
            scratch=[pltpu.VMEM((2, *square), F32)],
            limit=8 + 4 * n,
        )
    if paired:
        sums = ((groups * slots, D), BF16)
        partials = (pick, mate_pick, mine, mate)
        (give,) = call(functools.partial(give_kernel, slots), [sums], *partials)
        given = swap(give, 1)
        (keep,) = call(
            functools.partial(keep_kernel, slots), [(sums[0], F32)], *partials, flops=1 << 29
        )
        query_grad, loss = call(
            functools.partial(query_kernel, early, late),
            [part, ((block,), F32)],
            powers,
            late_powers,
            factors,
            *item_blocks,
            limit=8 + 2 * n,
            flops=1 << 30,
        )
        given, query_grad = lax.optimization_barrier((given, query_grad))
        packet = (slots + TAIL, D)
        packed = call(
            functools.partial(pack_kernel, slots),
            [((2, *packet), BF16)] * 2 + [(packet, BF16)] * 4,
            keep,
            given,
            *tails,
        )
        far = []
        for p in range(2):
            pairs = [
                (w * groups + g, w * groups + (g ^ FAR[p][w % 2]))
                for w in range(n)
                for g in range(groups)
            ]
            far.append(lax.ppermute(packed[p], ("wide", "group"), pairs))
        near = [swap(packed[2 + k], NEAR[k], "group") for k in range(1, 4)]
        forwarded = [swap(x[1], 1) for x in far]
        got = [packed[2], *far, *near, *forwarded]
    else:
        query_grad, loss = call(
            functools.partial(query_kernel, early, late),
            [part, ((block,), F32)],
            powers,
            late_powers,
            factors,
            *item_blocks,
            limit=8 + 2 * n,
            flops=1 << 30,
        )
        (packed,) = call(
            functools.partial(plain_pack_kernel, groups, slots),
            [((groups, slots + TAIL, D), BF16)],
            pick,
            *tails,
            mine,
            swap(mate, 1),
        )
        got = [lax.all_to_all(packed, "group", split_axis=0, concat_axis=0, tiled=True)]

    rows = table.shape[0]

    def scratch(packets):
        return [
            pltpu.VMEM((2 * packets * slots, D), BF16),
            pltpu.VMEM((TAIL, packets * slots), F32),
        ]

    before = []
    if paired:
        for part_of in (got[:3], got[3:5]):
            before = call(
                functools.partial(first_kernel, slots, len(before)),
                [((rows, D), F32)],
                *before,
                *part_of,
                scratch=scratch(len(part_of)),
                flops=1 << 28,
            )
        got = got[5:]
    table_new, accum_new = pl.pallas_call(
        functools.partial(update_kernel, slots, paired),
        out_shape=[jax.ShapeDtypeStruct(table.shape, F32)] * 2,
        out_specs=[pl.BlockSpec(memory_space=pl.ANY)] * 2,
        scratch_shapes=[
            *scratch(len(got) if paired else groups),
            pltpu.VMEM((2, rows, D), F32),
            pltpu.SemaphoreType.DMA((2, 4)),
        ],
        compiler_params=pltpu.CompilerParams(vmem_limit_bytes=32 * MIB),
    )(*before, *got, table, accum)
    return (loss, query_grad, table_new, accum_new)


def solution(mesh):
    placed = (
        P(("wide", "group"), None),
        P(("wide", "group"), None),
        P(("wide", "group"), None),
        P(("wide", "group")),
        P(("wide", "group")),
        P(("wide", "group"), None),
        P(("wide", "group"), None),
    )
    return jax.shard_map(
        shards,
        mesh=mesh,
        in_specs=placed,
        out_specs=(
            P(("wide", "group")),
            P(("wide", "group"), None),
            P(("wide", "group"), None),
            P(("wide", "group"), None),
        ),
        check_vma=False,
    )
```

```python
import functools
import math

import jax
import jax.numpy as jnp
from jax import lax
from jax.experimental import pallas as pl
from jax.experimental.pallas import tpu as pltpu
from jax.sharding import PartitionSpec as P

D = 256
SCALE = 3.0 / math.sqrt(D)
LOG2E = math.log2(math.e)
LANES = 128
TAIL = 8
ROW_CODES = 1 << 16
FAR = ((4, 5), (6, 7))
NEAR = (0, 3, 1, 2)
MIB = 1 << 20
NT = (((1,), (1,)), ((), ()))
TN = (((0,), (0,)), ((), ()))
F32 = jnp.float32
BF16 = jnp.bfloat16


def dot(a, b, dims=(((1,), (0,)), ((), ()))):
    return lax.dot_general(a, b, dims, preferred_element_type=F32)


def spread(column, width):
    pieces = [column] * (width // LANES)
    if width % LANES:
        pieces.append(column[:, : width % LANES])
    return jnp.concatenate(pieces, axis=1)


def code(x):
    y = x * x
    return jnp.where(x < 0, -y, y) * y


def decode(u):
    root = lax.rsqrt(lax.rsqrt(jnp.abs(u)))
    return jnp.where(u < 0, -root, root)


def diagonal(block):
    return lax.broadcasted_iota(jnp.int32, (block, block), 0) == lax.broadcasted_iota(
        jnp.int32, (block, block), 1
    )


def local_kernel(groups, slots, flip, code_ref, pick_ref, tail_ref):
    block = code_ref.shape[1]
    owner = code_ref[...] // ROW_CODES
    owner = jnp.where(owner < groups // 2, owner ^ flip, owner)
    offset = code_ref[...] % ROW_CODES
    member = lax.broadcasted_iota(jnp.int32, (groups, block), 0) == owner
    before = lax.broadcasted_iota(jnp.int32, (block, block), 0) < lax.broadcasted_iota(
        jnp.int32, (block, block), 1
    )
    ranks = dot(member.astype(BF16), before.astype(BF16))
    rank = jnp.sum(jnp.where(member, ranks, 0.0), axis=0, keepdims=True).astype(jnp.int32)
    high = jnp.broadcast_to((offset // LANES).astype(F32), (TAIL, block)).astype(BF16)
    low = jnp.broadcast_to((offset % LANES).astype(F32), (TAIL, block)).astype(BF16)
    here = lax.broadcasted_iota(jnp.int32, (LANES, block), 0) == rank
    for g in range(groups):
        pick = (here & (owner == g)).astype(F32).astype(BF16)
        pick_ref[g * slots : (g + 1) * slots] = pick[:slots]
        tail_ref[g] = jnp.concatenate([dot(high, pick, NT), dot(low, pick, NT)], axis=1).astype(BF16)


def powers_of(q, item_ref, rate_ref=None):
    logits = dot(item_ref[...], q, NT) * (SCALE * LOG2E)
    top = jnp.max(logits, axis=0, keepdims=True)
    e = jnp.exp2(logits - top)
    return (e if rate_ref is None else e * spread(rate_ref[...], q.shape[0])), top, logits


def column_sum(x):
    return jnp.sum(x, axis=0, keepdims=True)


def join(tops, sums):
    top = functools.reduce(jnp.maximum, tops)
    shrinks = [jnp.exp2(t - top) for t in tops]
    total = sum(x * s for x, s in zip(sums, shrinks))
    inverse = 1.0 / total
    return top, total, [s * inverse for s in shrinks]


def diagonal(block):
    return lax.broadcasted_iota(jnp.int32, (block, block), 0) == lax.broadcasted_iota(
        jnp.int32, (block, block), 1
    )


def early_kernel(n, q_ref, *refs):
    item_refs, (e_ref, tops_ref) = refs[:n], refs[n:]
    q = q_ref[...]
    for b in range(n):
        e, tops_ref[b : b + 1], logits = powers_of(q, item_refs[b])
        e_ref[b] = e
        if b == 0:
            tops_ref[n : n + 1] = column_sum(jnp.where(diagonal(q.shape[0]), logits, 0.0))


def rate_kernel(n, early, e_ref, near_ref, mate_ref, rate_ref, out_ref, sums_ref):
    block = e_ref.shape[1]
    near = [near_ref[:, k * block : (k + 1) * block].astype(F32) for k in range(n // 2)]
    mate = [mate_ref[:, k * block : (k + 1) * block].astype(F32) for k in range(n // 2)]
    counts = [near[0], mate[0]] + near[1:] + mate[1:]
    for b in range(n):
        rate = jnp.transpose(jnp.broadcast_to(1.0 / counts[b], (LANES, block)))
        rate_ref[b] = rate
        if b < early:
            e = e_ref[b] * spread(rate, block)
            out_ref[b] = e
            sums_ref[b : b + 1] = column_sum(e)
    sums_ref[early : early + 1] = jnp.log(counts[0]) * LOG2E


def far_powers(n, q, item_refs, rate_ref, e_ref):
    tops, sums = [], []
    for b in range(n):
        e, top, _ = powers_of(q, item_refs[b], rate_ref.at[b])
        if b < 2:
            e_ref[b] = e
        tops.append(top)
        sums.append(column_sum(e))
    return join(tops, sums)[2]


def main_kernel(early, late, *refs):
    n = early + late
    q_ref, far_ref, item_refs, refs = refs[0], refs[1], refs[2 : 2 + n], refs[2 + n :]
    rate_ref, e_ref, tops_ref, sums_ref, mine_out, mate_out, *refs = refs
    late_ref, factor_ref, far_e_ref = refs
    q, far = q_ref[...], far_ref[...]
    tops = [tops_ref[b : b + 1] for b in range(early)]
    sums = [sums_ref[b : b + 1] for b in range(early)]
    for b in range(late):
        e, top, _ = powers_of(q, item_refs[early + b], rate_ref.at[early + b])
        late_ref[b] = e
        tops.append(top)
        sums.append(column_sum(e))
    top, total, factors = join(tops, sums)
    far_factors = far_powers(n, far, item_refs, rate_ref, far_e_ref)
    mate = dot((e_ref[1] * factors[1]).astype(BF16), q)
    mate += dot((far_e_ref[1] * far_factors[1]).astype(BF16), far)
    mate_out[...] = code(mate * SCALE).astype(BF16) if mate_out.dtype == BF16 else mate
    weights = e_ref[0] * factors[0]
    weights = jnp.where(diagonal(q.shape[0]), weights - 1.0, weights)
    mine = dot(weights.astype(BF16), q)
    mine_out[...] = mine + dot((far_e_ref[0] * far_factors[0]).astype(BF16), far)
    chosen = tops_ref[early : early + 1] - sums_ref[early : early + 1]
    factor_ref[n : n + 1] = (top + jnp.log2(total) - chosen) * (1.0 / LOG2E)
    for b in range(n):
        factor_ref[b : b + 1] = factors[b]


def more_kernel(n, q_ref, *refs):
    item_refs, refs = refs[:n], refs[n:]
    rate_ref, mine_ref, mate_ref, mine_out, mate_out, e_ref = refs
    q = q_ref[...]
    factors = far_powers(n, q, item_refs, rate_ref, e_ref)
    mate = mate_ref[...] + dot((e_ref[1] * factors[1]).astype(BF16), q)
    mate_out[...] = code(mate * SCALE).astype(BF16) if mate_out.dtype == BF16 else mate
    mine_out[...] = mine_ref[...] + dot((e_ref[0] * factors[0]).astype(BF16), q)


def query_kernel(early, late, e_ref, late_ref, factor_ref, *refs):
    item_refs, out_ref, loss_ref = refs[:-2], refs[-2], refs[-1]
    loss_ref[...] = factor_ref[early + late]
    total = None
    for b, item_ref in enumerate(item_refs):
        e = e_ref[b] if b < early else late_ref[b - early]
        weights = e * factor_ref[b : b + 1]
        if b == 0:
            weights = jnp.where(diagonal(weights.shape[0]), weights - 1.0, weights)
        part = dot(weights.astype(BF16), item_ref[...], TN)
        total = part if total is None else total + part
    out_ref[...] = total * SCALE


def split(x):
    high = x.astype(BF16)
    return jnp.concatenate([high, (x - high.astype(F32)).astype(BF16)], axis=1)


def give_kernel(slots, pick_ref, mate_pick_ref, mine_ref, mate_ref, out_ref):
    mate = code(mate_ref[...] * SCALE).astype(BF16)
    out_ref[: 6 * slots] = dot(mate_pick_ref[2 * slots :], mate).astype(BF16)
    mine = code(mine_ref[...] * SCALE).astype(BF16)
    out_ref[6 * slots :] = dot(pick_ref[2 * slots : 4 * slots], mine).astype(BF16)


def keep_kernel(slots, pick_ref, mate_pick_ref, mine_ref, mate_ref, out_ref):
    mine = split(mine_ref[...] * SCALE)
    both = dot(pick_ref[: 2 * slots], mine)
    out_ref[: 2 * slots] = both[:, :D] + both[:, D:]
    both = dot(pick_ref[4 * slots :], mine)
    out_ref[2 * slots : 6 * slots] = both[:, :D] + both[:, D:]
    both = dot(mate_pick_ref[: 2 * slots], split(mate_ref[...] * SCALE))
    out_ref[6 * slots :] = both[:, :D] + both[:, D:]


def pack_kernel(slots, keep_ref, given_ref, tail_ref, mate_tail_ref, *out_refs):
    def rows(k):
        here = slice(k * slots, (k + 1) * slots)
        return code(keep_ref[here] + decode(given_ref[here].astype(F32))).astype(BF16)

    for p in range(2):
        out_refs[p][0, :slots] = rows(p)
        out_refs[p][0, slots:] = tail_ref[p]
        out_refs[p][1, :slots] = rows(6 + p)
        out_refs[p][1, slots:] = mate_tail_ref[p]
    for p in range(4):
        out_refs[2 + p][:slots] = rows(2 + p)
        out_refs[2 + p][slots:] = tail_ref[4 + p]


def plain_pack_kernel(groups, slots, pick_ref, tail_ref, mine_ref, other_ref, out_ref):
    grad = mine_ref[...] * SCALE + decode(other_ref[...].astype(F32))
    picked = dot(pick_ref[...], code(grad).astype(BF16)).astype(BF16)
    for g in range(groups):
        out_ref[g, :slots] = picked[g * slots : (g + 1) * slots]
        out_ref[g, slots:] = tail_ref[g]


def unpack(slots, paired, got_refs, values_ref, ids_ref):
    packets = []
    for ref in got_refs:
        if len(ref.shape) == 2:
            packets.append(ref)
        else:
            packets += [ref.at[g] for g in range(1 if paired else ref.shape[0])]
    half = len(packets) * slots
    for g, got in enumerate(packets):
        tail = got[slots : slots + TAIL].astype(F32)
        ids = tail[:, :slots] * LANES + tail[:, LANES : LANES + slots]
        ids_ref[:, g * slots : (g + 1) * slots] = ids
        values = decode(got[:slots].astype(F32))
        high = values.astype(BF16)
        values_ref[g * slots : (g + 1) * slots] = high
        low = (values - high.astype(F32)).astype(BF16)
        values_ref[half + g * slots : half + (g + 1) * slots] = low


def scatter(values_ref, ids_ref, first, rows):
    index = lax.broadcasted_iota(jnp.int32, (rows, ids_ref.shape[1]), 0) + first
    put = (index.astype(F32) == ids_ref[:1]).astype(F32).astype(BF16)
    return dot(jnp.concatenate([put, put], axis=1), values_ref[...])


def first_kernel(slots, partial, *refs):
    inputs, (out_ref, values_ref, ids_ref) = refs[:-3], refs[-3:]
    unpack(slots, True, inputs[partial:], values_ref, ids_ref)
    sums = scatter(values_ref, ids_ref, 0, out_ref.shape[0])
    out_ref[...] = sums + inputs[0][...] if partial else sums


def update_kernel(slots, partial, *refs):
    inputs, refs = refs[:-8], refs[-8:]
    table_ref, accum_ref, table_out, accum_out, values_ref, ids_ref, new_ref, sems = refs
    unpack(slots, partial, inputs[1:] if partial else inputs, values_ref, ids_ref)
    chunks = sems.shape[1]
    rows = table_ref.shape[0] // chunks
    copies = []
    for c in range(chunks):
        here = slice(c * rows, (c + 1) * rows)
        grad = scatter(values_ref, ids_ref, c * rows, rows)
        if partial:
            grad += inputs[0][here]
        accum_new = accum_ref[here] + grad * grad
        new_ref[1, here] = accum_new
        copies.append(pltpu.make_async_copy(new_ref.at[1, here], accum_out.at[here], sems.at[1, c]))
        copies[-1].start()
        new_ref[0, here] = table_ref[here] - 0.1 * grad / (accum_new * lax.rsqrt(accum_new) + 1e-08)
        copies.append(pltpu.make_async_copy(new_ref.at[0, here], table_out.at[here], sems.at[0, c]))
        copies[-1].start()
    for copy in copies:
        copy.wait()


def call(kernel, outs, *args, scratch=(), limit=16, flops=0):
    return pl.pallas_call(
        kernel,
        out_shape=[jax.ShapeDtypeStruct(s, t) for s, t in outs],
        scratch_shapes=list(scratch),
        compiler_params=pltpu.CompilerParams(vmem_limit_bytes=limit * MIB),
        cost_estimate=pl.CostEstimate(flops=flops, bytes_accessed=1024, transcendentals=0),
    )(*args)


def shards(queries, items, item_owner, item_offset, sample_counts, table, accum):
    block = queries.shape[0]
    n, groups = lax.axis_size("wide"), lax.axis_size("group")
    capacity = 2 * block // groups
    slots = -(-capacity // TAIL) * TAIL
    paired = groups == 8 and n == 4

    def swap(x, k, axis="wide"):
        return lax.ppermute(x, axis, [(i, i ^ k) for i in range(lax.axis_size(axis))])

    far_counts = [swap(sample_counts, k) for k in range(2, n, 2)]
    far_items = [swap(items, k) for k in range(2, n, 2)]
    far_queries = [swap(queries, k) for k in range(2, n, 2)]

    owner = item_owner
    if paired:
        partner = owner ^ lax.axis_index("group")
        flip = lax.axis_index("wide") % 2 * 2
        owner = jnp.zeros_like(partner)
        for core in range(2):
            for k in range(2):
                place = (2 * core + k) ^ flip
                owner = jnp.where(partner == FAR[k][core], place, owner)
        for k in range(4):
            owner = jnp.where(partner == NEAR[k], 4 + k, owner)
    codes = (owner * ROW_CODES + item_offset.reshape(block, 1)).reshape(1, block)

    def route(codes, flip, flops):
        return call(
            functools.partial(local_kernel, groups, slots, flip),
            [((groups * slots, block), BF16), ((groups, TAIL, D), BF16)],
            codes,
            flops=flops,
        )

    pick, tail = route(codes, 0, 0)
    tails, own_items = [tail], items
    if paired:
        mate_codes, own_items = lax.optimization_barrier((swap(codes, 1), items))
        mate_pick, mate_tail = route(mate_codes, 2, 1 << 30)
        tails.append(mate_tail)
    far_items, far_counts, tails = lax.optimization_barrier((far_items, far_counts, tails))
    item_blocks = [items, swap(own_items, 1)] + far_items
    early = len(item_blocks)
    item_blocks += [swap(x, 1) for x in far_items]
    late = n - early
    near_counts = jnp.concatenate([sample_counts, *far_counts])
    mate_counts = swap(near_counts, 1)
    part = ((block, D), F32)
    square = (block, block)
    rows_of = ((-(-(n + 1) // TAIL) * TAIL, block), F32)
    sent = ((block, D), BF16)
    powers, stats = call(
        functools.partial(early_kernel, early),
        [((early, *square), F32), rows_of],
        queries,
        *item_blocks[:early],
        limit=8 + 2 * n,
        flops=1 << 29,
    )
    rates, powers, totals = call(
        functools.partial(rate_kernel, n, early),
        [((n, block, LANES), F32), ((early, *square), F32), rows_of],
        powers,
        near_counts.reshape(1, -1),
        mate_counts.reshape(1, -1),
        limit=8 + 4 * n,
    )
    mine, mate, late_powers, factors = call(
        functools.partial(main_kernel, early, late),
        [
            part,
            part if paired or far_queries[1:] else sent,
            ((late, *square), F32),
            rows_of,
        ],
        queries,
        far_queries[0],
        *item_blocks,
        rates,
        powers,
        stats,
        totals,
        scratch=[pltpu.VMEM((2, *square), F32)],
        limit=8 + 4 * n,
    )
    for k, far in enumerate(far_queries[1:], 2):
        mine, mate = call(
            functools.partial(more_kernel, n),
            [part, part if k < len(far_queries) else sent],
            far,
            *item_blocks,
            rates,
            mine,
            mate,
            scratch=[pltpu.VMEM((2, *square), F32)],
            limit=8 + 4 * n,
        )
    if paired:
        sums = ((groups * slots, D), BF16)
        partials = (pick, mate_pick, mine, mate)
        (give,) = call(functools.partial(give_kernel, slots), [sums], *partials)
        given = swap(give, 1)
        (keep,) = call(
            functools.partial(keep_kernel, slots), [(sums[0], F32)], *partials, flops=1 << 29
        )
        query_grad, loss = call(
            functools.partial(query_kernel, early, late),
            [part, ((block,), F32)],
            powers,
            late_powers,
            factors,
            *item_blocks,
            limit=8 + 2 * n,
            flops=1 << 30,
        )
        given, query_grad = lax.optimization_barrier((given, query_grad))
        packet = (slots + TAIL, D)
        packed = call(
            functools.partial(pack_kernel, slots),
            [((2, *packet), BF16)] * 2 + [(packet, BF16)] * 4,
            keep,
            given,
            *tails,
        )
        far = []
        for p in range(2):
            pairs = [
                (w * groups + g, w * groups + (g ^ FAR[p][w % 2]))
                for w in range(n)
                for g in range(groups)
            ]
            far.append(lax.ppermute(packed[p], ("wide", "group"), pairs))
        near = [swap(packed[2 + k], NEAR[k], "group") for k in range(1, 4)]
        forwarded = [swap(x[1], 1) for x in far]
        got = [packed[2], *far, *near, *forwarded]
    else:
        query_grad, loss = call(
            functools.partial(query_kernel, early, late),
            [part, ((block,), F32)],
            powers,
            late_powers,
            factors,
            *item_blocks,
            limit=8 + 2 * n,
            flops=1 << 30,
        )
        (packed,) = call(
            functools.partial(plain_pack_kernel, groups, slots),
            [((groups, slots + TAIL, D), BF16)],
            pick,
            *tails,
            mine,
            swap(mate, 1),
        )
        got = [lax.all_to_all(packed, "group", split_axis=0, concat_axis=0, tiled=True)]

    rows = table.shape[0]

    def scratch(packets):
        return [
            pltpu.VMEM((2 * packets * slots, D), BF16),
            pltpu.VMEM((TAIL, packets * slots), F32),
        ]

    before = []
    if paired:
        for part_of in (got[:3], got[3:5]):
            before = call(
                functools.partial(first_kernel, slots, len(before)),
                [((rows, D), F32)],
                *before,
                *part_of,
                scratch=scratch(len(part_of)),
                flops=1 << 28,
            )
        got = got[5:]
    table_new, accum_new = pl.pallas_call(
        functools.partial(update_kernel, slots, paired),
        out_shape=[jax.ShapeDtypeStruct(table.shape, F32)] * 2,
        out_specs=[pl.BlockSpec(memory_space=pl.ANY)] * 2,
        scratch_shapes=[
            *scratch(len(got) if paired else groups),
            pltpu.VMEM((2, rows, D), F32),
            pltpu.SemaphoreType.DMA((2, 4)),
        ],
        compiler_params=pltpu.CompilerParams(vmem_limit_bytes=32 * MIB),
    )(*before, *got, table, accum)
    return (loss, query_grad, table_new, accum_new)


def solution(mesh):
    placed = (
        P(("wide", "group"), None),
        P(("wide", "group"), None),
        P(("wide", "group"), None),
        P(("wide", "group")),
        P(("wide", "group")),
        P(("wide", "group"), None),
        P(("wide", "group"), None),
    )
    return jax.shard_map(
        shards,
        mesh=mesh,
        in_specs=placed,
        out_specs=(
            P(("wide", "group")),
            P(("wide", "group"), None),
            P(("wide", "group"), None),
            P(("wide", "group"), None),
        ),
        check_vma=False,
    )
```
